32 devices in a mesh: atm: 8 (over z, y), cpl: 4 (over x, core).
Axes of the slice: x: 2, y: 2, z: 4, core: 2. Of those that a mesh axis runs over, the one named last changes fastest.
Arguments:
- air_temp: float32 [192, 64, 512], P('atm', None, 'cpl'), may hold values from -6 to 6
- wind_field: bfloat16 [2, 192, 64, 512], P(None, 'atm', None, 'cpl'), may hold values from -0.3984375 to 0.3984375
- physics: float32 [64, 64], replicated, may hold values from -0.75 to 0.75
- sea_surface: float32 [192, 512], P('atm', 'cpl'), may hold values from -6 to 6
- shortwave: float32 [192, 512], P('atm', 'cpl'), may hold values from 0 to 1
- ocean_mask: int32 [192, 512], P('atm', 'cpl'), may hold values 0 or 1
- owner_route: int32 [4, 192, 1], P('cpl', 'atm'), may hold values from 0 to 3; in each aligned block of 24 rows (0 to 23, 24 to 47, ..., all dimensions but the last counted through in order) at most 12 rows name the same one
- ocean_tile: int32 [4, 192], P('cpl', 'atm'), may hold values from 0 to 23
- weight_tile: int32 [4, 192], P('cpl', 'atm'), may hold values from 0 to 15
- remap_tiles: float32 [16, 32, 128], replicated, may hold values from 0.002 to 0.03
- ocean_temp: float32 [80, 24576], P(None, ('atm', 'cpl')), may hold values from -6 to 6
- mixing: float32 [80, 80], replicated, may hold values from -0.625 to 0.625
Outputs:
- air_next: float32 [192, 64, 512], P('atm', None, 'cpl')
- ocean_next: float32 [80, 24576], P(None, ('atm', 'cpl'))
- surface_temp: float32 [192, 512], P('atm', 'cpl')
The draws below stay inside these ranges and needn't reach their ends.
Inputs may be any that keep to these rules, and one draw needn't show every extreme that they name: `owner_route`: among the 24 tiles of one device at most 12 name the same owner, and in every draw some device's tiles name one owner exactly 12 times. `ocean_tile`: ocean tile index within the owner. `weight_tile`: row of remap_tiles used by the tile.
All inputs are finite; a program needn't handle non-finite values. No bound on the sum of `ocean_mask` on one device may be relied on, other than what follows from the above.
Results may differ from the reference program's by a relative error of at most 0.0015.
Values may be sent and summed in bfloat16 or wider, within the bound.
No kernel may reach another device: no remote copies, remote signals or barrier semaphores. Data moves between devices by JAX's collectives and lax.ppermute only.
A program may use at most 64 MiB of HBM per device.

```python
import math
import jax
import jax.numpy as jnp
import numpy as np
from jax import lax

GX = 24
GY = 128
LEV = 64
OLEV = 80
WT = 16
OTILE = 32
CAP = 12
NX = 192
NY = 512
NOCN = 24576
N_ATM = 8
N_CPL = 4


def plant(array, rng, least, largest):
    place = [jax.random.randint(jax.random.fold_in(rng, axis), (), 0, length) for axis, length in enumerate(array.shape)]
    longest = array.shape.index(max(array.shape))
    neighbour = place[:longest] + [(place[longest] + 1) % array.shape[longest]] + place[longest + 1:]
    return array.at[tuple(place)].set(least).at[tuple(neighbour)].set(largest)


def level_of(own_key, shape, shards, least, largest):
    def one(axis_at, parts):
        steps = jax.random.uniform(jax.random.fold_in(jax.random.fold_in(own_key, 6), axis_at), (parts,), jnp.float32, least / len(shards), largest / len(shards))
        return jnp.repeat(jnp.exp(steps), shape[axis_at] // parts).reshape((-1,) + (1,) * (len(shape) - axis_at - 1))

    factor_of = one(*shards[0])
    for cut in shards[1:]:
        factor_of = factor_of * one(*cut)
    return factor_of


def assign_block(key, own, number, rows, count, top, limit, skew):
    sequence = jax.random.permutation(key, count)
    packed, ordinary = portions_of(count, rows * top, limit, skew, True), portions_of(count, rows * top, limit, skew, False)
    places = jnp.arange(count)

    def named(lengths, turn):
        used = int((lengths > 0).sum())
        fixed = max(1, used // 4)
        moved = fixed + (places - fixed + turn * (used - fixed)) % max(1, count - fixed)
        return jnp.zeros((count,), jnp.int32).at[sequence[jnp.where(places < fixed, places, moved)]].set(jnp.asarray(lengths, jnp.int32))

    lengths = jnp.where(number % 4 == 0, named(packed, number // 4), named(ordinary, number - number // 4 - 1))
    mixed = jax.random.permutation(jax.random.fold_in(own, 3), count)
    donor, taker = mixed[0:count // 2 * 2:2], mixed[1:count // 2 * 2:2]
    slack = jnp.minimum(lengths[donor] - 1, limit - lengths[taker]) // 2
    slack = jnp.where((donor == sequence[0]) | (taker == sequence[0]) | (lengths[taker] == 0), 0, jnp.maximum(slack, 0))
    moved = jax.random.randint(jax.random.fold_in(own, 4), (count // 2,), 0, 1 << 20) % (slack + 1)
    lengths = lengths.at[donor].add(-moved).at[taker].add(moved)
    items = jnp.searchsorted(jnp.cumsum(lengths), jnp.arange(rows * top), side="right").astype(jnp.int32)
    listing = items.reshape(top, rows).T
    listing = listing[jax.random.permutation(jax.random.fold_in(own, 1), rows)]
    turn = jax.random.randint(jax.random.fold_in(own, 2), (rows, 1), 0, top)
    return jnp.take_along_axis(listing, (jnp.arange(top)[None, :] + turn) % top, axis=1)


def portions_of(count, total, most, slope, full):
    loads = [(1 << 20) // math.isqrt(grade ** slope) + 1 for grade in range(1, count + 1)]
    largest = most if full else min(most, max(-(-total // count), total * loads[0] // sum(loads)))
    least = 1 if total - largest >= count - 1 else 0
    counts, surplus = [largest] + [least] * (count - 1), total - largest - least * (count - 1)
    while surplus > 0:
        candidates = [i for i in range(1, count) if counts[i] < largest] or [i for i in range(1, count) if counts[i] < most]
        mass, left = sum([loads[i] for i in candidates]), surplus
        for i in candidates:
            more = min(most - counts[i], max(1, left * loads[i] // mass), surplus)
            counts[i] = counts[i] + more
            surplus = surplus - more
    return np.array(counts)


def bell_draw(stream_key, extent, deviation, reach, pieces=(), kind=jnp.bfloat16):
    level = level_of(stream_key, extent, pieces, -0.22, 0.18) if pieces else 1.0
    result = jax.random.normal(stream_key, extent, jnp.float32) * deviation * level
    return jnp.minimum(jnp.maximum(result, -reach), reach).astype(kind)


def setup_inputs(seed: int = 0) -> dict:
    keys = jax.random.split(jax.random.key(seed), 13)
    air_temp = bell_draw(keys[0], (NX, LEV, NY), 1.0, 6.0, ((0, 8), (2, 4)), jnp.float32)
    wind_field = jnp.clip(jax.random.uniform(keys[1], (2, NX, LEV, NY), jnp.float32, -0.3984375, 0.3984375) * level_of(keys[1], (2, NX, LEV, NY), ((1, 8), (3, 4)), -0.4, 0.0), -0.3984375, 0.3984375).astype(jnp.bfloat16)
    physics = bell_draw(keys[2], (LEV, LEV), LEV ** -0.5, 0.75, (), jnp.float32)
    sea_surface = bell_draw(keys[3], (NX, NY), 1.0, 6.0, ((0, 8), (1, 4)), jnp.float32)
    shortwave = jnp.clip(1.0 * jax.random.uniform(keys[4], (NX, NY), jnp.float32) ** level_of(keys[4], (NX, NY), ((0, 8), (1, 4)), -0.2, 0.2), 0.0, 1.0)
    ocean_mask = plant((jax.random.randint(keys[5], (NX, NY), 0, 3) < 2).astype(jnp.int32), jax.random.fold_in(keys[5], 1), 0, 1)
    owner_route_keys = jax.random.split(jax.random.fold_in(keys[6], 1), N_CPL * NX // GX)
    owner_route_turns = jax.random.permutation(jax.random.fold_in(keys[6], 3), N_CPL * NX // GX)
    owner_route = jax.vmap(lambda own, number: assign_block(jax.random.fold_in(keys[6], 2), own, number, GX, N_CPL, 1, CAP, 2))(owner_route_keys, owner_route_turns).reshape((N_CPL, NX, 1))
    ocean_tile = plant(jax.random.randint(keys[7], (N_CPL, NX), 0, GX), jax.random.fold_in(keys[7], 1), 0, GX - 1).astype(jnp.int32)
    weight_tile = plant(jax.random.randint(keys[8], (N_CPL, NX), 0, WT), jax.random.fold_in(keys[8], 1), 0, WT - 1).astype(jnp.int32)
    remap_tiles = jnp.clip(jnp.exp(jax.random.uniform(keys[9], (WT, OTILE, GY), jnp.float32, math.log(0.002), math.log(0.03))), 0.002, 0.03)
    ocean_temp = bell_draw(keys[10], (OLEV, NOCN), 1.0, 6.0, ((1, 32),), jnp.float32)
    mixing = bell_draw(keys[11], (OLEV, OLEV), OLEV ** -0.5, 0.625, (), jnp.float32)
    return dict(air_temp=air_temp, wind_field=wind_field, physics=physics, sea_surface=sea_surface, shortwave=shortwave, ocean_mask=ocean_mask, owner_route=owner_route, ocean_tile=ocean_tile, weight_tile=weight_tile, remap_tiles=remap_tiles, ocean_temp=ocean_temp, mixing=mixing)


diffusion_rate = 0.05
physics_rate = 0.5
highest = lax.Precision.HIGHEST

def transport(center, west_cell, east_cell, south_cell, north_cell, speed_first, speed_second):
    upwind = jnp.maximum(speed_first, 0.0) * (center - west_cell) + jnp.minimum(speed_first, 0.0) * (east_cell - center)
    upwind = upwind + jnp.maximum(speed_second, 0.0) * (center - south_cell) + jnp.minimum(speed_second, 0.0) * (north_cell - center)
    spread = west_cell + east_cell + south_cell + north_cell - 4.0 * center
    return center - upwind + diffusion_rate * spread

def column_physics(air_field, physics):
    tendency = jnp.einsum('kl,xlz->xkz', physics, air_field, precision=highest)
    return air_field + physics_rate * jnp.tanh(tendency)

def tiles_of(surface_grid):
    return surface_grid.reshape(NX, N_CPL, GY).transpose(1, 0, 2)

def reference(air_temp, wind_field, physics, sea_surface, shortwave, ocean_mask, owner_route, ocean_tile, weight_tile, remap_tiles, ocean_temp, mixing):
    speed_first = wind_field[0].astype(jnp.float32)
    speed_second = wind_field[1].astype(jnp.float32)
    air_field = air_temp
    for step_index in range(2):
        air_field = transport(air_field, jnp.roll(air_field, 1, 0), jnp.roll(air_field, -1, 0), jnp.roll(air_field, 1, 2), jnp.roll(air_field, -1, 2), speed_first, speed_second)
        air_field = column_physics(air_field, physics)
    bottom = air_field[:, 0, :]
    bottom_speed = jnp.sqrt(speed_first[:, 0, :] ** 2 + speed_second[:, 0, :] ** 2 + 0.01)
    ocean_frac = ocean_mask.astype(jnp.float32)
    heat_flux = ocean_frac * (0.5 + 2.0 * bottom_speed) * (bottom - sea_surface)
    solar_flux = ocean_frac * shortwave
    flux_tiles = jnp.stack([tiles_of(heat_flux), tiles_of(solar_flux)], axis=2)
    chosen = jnp.take(remap_tiles, weight_tile, axis=0)
    shares = jnp.einsum('cxoa,cxfa->cxfo', chosen, flux_tiles, precision=highest)
    group_index = jnp.arange(NX, dtype=jnp.int32)[None, :] // GX
    target = ((group_index * N_CPL + owner_route[:, :, 0]) * GX + ocean_tile).astype(jnp.int32)
    per_tile = jax.ops.segment_sum(shares.reshape(N_CPL * NX, 2, OTILE), target.reshape(-1), num_segments=N_ATM * N_CPL * GX)
    forcing = per_tile.transpose(1, 0, 2).reshape(2, NOCN)
    depth_index = jnp.arange(OLEV, dtype=jnp.float32)
    profile = jnp.exp(-depth_index / 8.0)
    profile = profile / jnp.sum(profile)
    heated = ocean_temp + forcing[1][None, :] * profile[:, None]
    heated = heated.at[0].add(forcing[0])
    ocean_next = 0.5 * heated + jnp.dot(mixing, heated, precision=highest, preferred_element_type=jnp.float32)
    surface_tiles = ocean_next[0].reshape(N_ATM * N_CPL * GX, OTILE)[target]
    weighted = jnp.einsum('cxoa,cxo->cxa', chosen, surface_tiles, precision=highest)
    returned = weighted / lax.optimization_barrier(jnp.sum(chosen, axis=2))
    returned = returned.transpose(1, 0, 2).reshape(NX, NY)
    surface_temp = ocean_frac * returned + (1.0 - ocean_frac) * bottom
    return (air_field, ocean_next, surface_temp)
```

```python
import jax
import jax.numpy as jnp
from jax import lax
from jax.experimental import pallas as pl
from jax.experimental.pallas import tpu as pltpu
from jax.sharding import PartitionSpec as P

diffusion_rate = 0.05
physics_rate = 0.5
highest = lax.Precision.HIGHEST
f32 = jnp.float32
bf16 = jnp.bfloat16


def pair_even(count):
    return [(i, i ^ 1) for i in range(count)]


def pair_odd(count):
    up = [(i, (i + 1) % count) for i in range(1, count, 2)]
    return up + [(target, source) for source, target in up]


def exchange(block, axis):
    count = lax.axis_size(axis)
    first = lax.ppermute(block[0], axis, pair_odd(count))
    second = lax.ppermute(block[1], axis, pair_even(count))
    return second, first


def iota(shape, dim):
    return lax.broadcasted_iota(jnp.int32, shape, dim)


def roll(value, shift):
    return pltpu.roll(value, shift % value.shape[-1], value.ndim - 1)


def pick(flag, yes, no):
    return jnp.where(flag, yes, no)


def rates(first, second):
    return (
        jnp.maximum(first, 0.0) + diffusion_rate,
        diffusion_rate - jnp.minimum(first, 0.0),
        jnp.maximum(second, 0.0) + diffusion_rate,
        diffusion_rate - jnp.minimum(second, 0.0),
    )


def split(value):
    high = value.astype(bf16)
    return high, (value - high.astype(f32)).astype(bf16)


def physics_stack(physics):
    high, low = split(physics)
    return jnp.concatenate([high, high, low], axis=1)


def column(stack, field):
    high, low = split(field)
    tendency = jnp.dot(
        stack, jnp.concatenate([high, low, high], axis=0), preferred_element_type=f32
    )
    return field + physics_rate * jnp.tanh(tendency)


def pack_kernel(air, wind, packed):
    rows, levels, width = air.shape
    lane = iota((levels, width), 1)
    place = lane // 4
    kind = lane % 4
    cells = jnp.zeros((levels, width), f32)
    first = jnp.zeros((levels, width), f32)
    second = jnp.zeros((levels, width), f32)
    for x in range(rows):
        here = place == x
        cells = pick(here, roll(air[x], 4 * x + 2), cells)
        first = pick(here, roll(wind[0, x].astype(f32), 4 * x + 2), first)
        second = pick(here, roll(wind[1, x].astype(f32), 4 * x + 2), second)
    winds = pick((kind == 1) | (kind == 2), first, roll(second, 2))
    packed[0] = cells.astype(bf16)
    packed[1] = winds.astype(bf16)


def cpl_sides(even_side, odd_side):
    upper = lax.axis_index("cpl") % 2 == 0
    high = pick(upper, even_side[...].astype(f32), odd_side[...].astype(f32))
    low = pick(upper, odd_side[...].astype(f32), even_side[...].astype(f32))
    return low, high


def outer_cells(low, high):
    kind = iota(low.shape[1:], 1) % 4
    return pick(kind < 2, low[0], high[0])


def swap_cells(cells):
    kind = iota(cells.shape, 1) % 4
    return pick(kind == 2, roll(cells, 1), roll(cells, -1))


def sideways(field, swapped, x):
    width = field.shape[1]
    lane = iota(field.shape, 1)
    halo = roll(swapped, -(4 * x + 2))
    south = pick(lane == 0, halo, roll(field, 1))
    north = pick(lane == width - 1, halo, roll(field, -1))
    return south, north


def advance_row(center, west, east, south, north, speeds):
    cw, ce, cs, cn = speeds
    return (
        center
        + (cw * (west - center) + ce * (east - center))
        + (cs * (south - center) + cn * (north - center))
    )


def advance_outer(own, low, high, outer, west, east):
    kind = iota(outer.shape, 1) % 4
    south = roll(pick(kind == 0, outer, own), 1)
    north = roll(pick(kind == 3, outer, own), -1)
    first = pick(kind == 1, low[1], high[1])
    second = roll(pick(kind == 3, low[1], high[1]), -2)
    return advance_row(outer, west, east, south, north, rates(first, second))


def make_edge_kernel(rows):
    def edge_kernel(air_low, air_high, wind_low, wind_high, even_side, odd_side, messages, partial):
        low, high = cpl_sides(even_side, odd_side)
        outer = outer_cells(low, high)
        swapped = swap_cells(outer)
        sent = []
        for at, (center, inner, wind, x) in enumerate(
            ((air_low[0], air_low[1], wind_low, 0), (air_high[1], air_high[0], wind_high, rows - 1))
        ):
            cw, ce, cs, cn = rates(wind[0, 0].astype(f32), wind[1, 0].astype(f32))
            inside, outside = (ce, cw) if at == 0 else (cw, ce)
            south, north = sideways(center, swapped, x)
            known = (
                center
                + (inside * (inner - center) - outside * center)
                + (cs * (south - center) + cn * (north - center))
            )
            partial[2 * at] = known
            partial[2 * at + 1] = outside
            sent.append([center, known, outside, outer])
        upper = lax.axis_index("atm") % 2 == 0
        for at, (to_low, to_high) in enumerate(zip(*sent)):
            messages[0, at] = pick(upper, to_high, to_low).astype(bf16)
            messages[1, at] = pick(upper, to_low, to_high).astype(bf16)

    return edge_kernel


def inner_kernel(air, wind, physics, own, even_side, odd_side, air_next, near, bottom, field):
    rows, levels, width = air.shape
    low, high = cpl_sides(even_side, odd_side)
    outer = outer_cells(low, high)
    stack = physics_stack(physics[...])
    swapped = swap_cells(outer)
    after = advance_outer(
        own[0].astype(f32), low, high, outer, roll(outer, 4), roll(outer, -4)
    )
    swapped_after = swap_cells(column(stack, after))

    def speeds(x):
        return rates(wind[0, x].astype(f32), wind[1, x].astype(f32))

    def step(source, halo, x):
        center = source[x]
        south, north = sideways(center, halo, x)
        return advance_row(center, source[x - 1], source[x + 1], south, north, speeds(x))

    def pair(source, halo, x):
        return column(stack, jnp.concatenate([step(source, halo, x), step(source, halo, x + 1)], axis=1))

    for x in range(1, rows - 1, 2):
        both = pair(air, swapped, x)
        field[x] = both[:, :width]
        field[x + 1] = both[:, width:]
    near[0] = field[1]
    near[1] = field[2]
    near[2] = field[rows - 3]
    near[3] = field[rows - 2]
    bottom[...] = jnp.zeros_like(bottom)
    for x in range(2, rows - 2, 2):
        both = pair(field, swapped_after, x)
        air_next[x] = both[:, :width]
        air_next[x + 1] = both[:, width:]
        bottom[x : x + 1] = both[0:1, :width]
        bottom[x + 1 : x + 2] = both[0:1, width:]


def as_column(row):
    size = row.shape[1]
    square = jnp.broadcast_to(row, (size, size))
    return jnp.sum(
        jnp.where(iota((size, size), 0) == iota((size, size), 1), square, 0.0),
        axis=1,
        keepdims=True,
    )


def fold(value, size):
    span = value.shape[1] // 2
    while span >= size:
        value = value + roll(value, span)
        span //= 2
    return value


def chosen_shares(fluxes, weights, bank, ocean_width):
    rows, width = fluxes.shape
    every = lax.dot_general(
        fluxes, weights, (((1,), (1,)), ((), ())), precision=highest, preferred_element_type=f32
    )
    total = jnp.zeros((rows, width), f32)
    for at in range(0, weights.shape[0], width):
        block = (iota((rows, width), 1) + at) // ocean_width
        total = total + jnp.where(block == bank, every[:, at : at + width], 0.0)
    return fold(total, ocean_width)


def start_kernel(
    winds, shortwave, mask, route, tile, bank, weights, ocean, mixing,
    exchange_rate, total_weight, message, base, response,
):
    rows, width = shortwave.shape
    depth = ocean.shape[0]
    banks, ocean_width, _ = weights.shape
    flat = weights[...].reshape(banks * ocean_width, width)
    frac = mask[...].astype(f32)
    bank_at = as_column(bank[...].astype(f32)).astype(jnp.int32)
    for x in range(rows):
        first = winds[0, x].astype(f32)[0:1]
        second = winds[1, x].astype(f32)[0:1]
        exchange_rate[x : x + 1] = first * first + second * second
    exchange_rate[...] = frac * (0.5 + 2.0 * jnp.sqrt(exchange_rate[...] + 0.01))
    solar = chosen_shares(frac * shortwave[...], flat, bank_at, ocean_width)
    lane = iota((rows, width), 1)
    total = jnp.zeros((rows, width), f32)
    for at in range(0, banks * ocean_width, width):
        hot = ((lane + at) // ocean_width == bank_at).astype(f32)
        total = total + jnp.dot(hot, flat[at : at + width], precision=highest, preferred_element_type=f32)
    total_weight[...] = total

    held = ocean[...]
    mixed = mixing[...]
    settled = 0.5 * held + jnp.dot(mixed, held, precision=highest, preferred_element_type=f32)
    base[...] = settled
    level = iota((depth, width), 0)
    profile = jnp.exp(level.astype(f32) / -8.0)
    profile = profile / jnp.sum(profile, axis=0, keepdims=True)
    part = iota((depth, width), 1)
    unit = jnp.where(part == 0, (level == 0).astype(f32), jnp.where(part == 1, profile, 0.0))
    response[...] = 0.5 * unit + jnp.dot(mixed, unit, precision=highest, preferred_element_type=f32)

    group = lax.axis_index("cpl")
    surface = jnp.zeros((rows, width), f32)
    for at in range(0, rows * ocean_width, width):
        spread = jnp.broadcast_to(settled[0:1, at : at + width], (rows, width))
        surface = surface + jnp.where((lane + at) // ocean_width == iota((rows, width), 0), spread, 0.0)
    surface = fold(surface, ocean_width)
    target = route[...] * rows + tile[...]
    target_at = as_column(target.astype(f32))
    own_at = (group * rows + iota((rows, width), 0)).astype(f32)
    message[...] = jnp.full(message.shape, -1.0, f32)
    message[0:rows, :] = jnp.where(
        lane < 2 * ocean_width,
        solar,
        jnp.where(
            lane < 3 * ocean_width,
            surface,
            jnp.where(lane == 3 * ocean_width, target_at, own_at),
        ),
    )
    message[rows : rows + 1, 0:rows] = target.astype(f32)
    message[rows : rows + 1, ocean_width : ocean_width + rows] = (
        group * rows + iota((1, rows), 1)
    ).astype(f32)


def make_outer_kernel(rows):
    def outer_kernel(
        even_atm, odd_atm, partial, air_low, air_high, wind_low, wind_high, own, even_side, odd_side,
        near, physics, bottom, rate, sea, bank, weights, start,
        air_edges, bottom_next, message,
    ):
        width = sea.shape[1]
        banks, ocean_width, _ = weights.shape
        upper = lax.axis_index("atm") % 2 == 0
        above = pick(upper, even_atm[...].astype(f32), odd_atm[...].astype(f32))
        below = pick(upper, odd_atm[...].astype(f32), even_atm[...].astype(f32))
        low, high = cpl_sides(even_side, odd_side)
        outer = outer_cells(low, high)
        stack = physics_stack(physics[...])
        place = iota(outer.shape, 1) // 4
        after = advance_outer(
            own[0].astype(f32),
            low,
            high,
            outer,
            pick(place == 0, roll(below[3], -4 * (rows - 1)), roll(outer, 4)),
            pick(place == rows - 1, roll(above[3], 4 * (rows - 1)), roll(outer, -4)),
        )
        moved = jnp.concatenate(
            [
                below[1] + below[2] * air_low[0],
                partial[0] + partial[1] * below[0],
                partial[2] + partial[3] * above[0],
                above[1] + above[2] * air_high[1],
                after,
            ],
            axis=1,
        )
        stepped = column(stack, moved)
        parts = [stepped[:, at * width : (at + 1) * width] for at in range(5)]
        halo = swap_cells(parts[4])
        inner = [near[at] for at in range(4)]
        bottom_next[...] = bottom[...]
        cells = []
        for center, west, east, wind, at, x in (
            (parts[1], parts[0], inner[0], wind_low, 0, 0),
            (inner[0], parts[1], inner[1], wind_low, 1, 1),
            (inner[3], inner[2], parts[2], wind_high, 0, rows - 2),
            (parts[2], inner[3], parts[3], wind_high, 1, rows - 1),
        ):
            south, north = sideways(center, halo, x)
            speeds = rates(wind[0, at].astype(f32), wind[1, at].astype(f32))
            cells.append(advance_row(center, west, east, south, north, speeds))
        final = column(stack, jnp.concatenate(cells, axis=1))
        for at, x in enumerate((0, 1, rows - 2, rows - 1)):
            row = final[:, at * width : (at + 1) * width]
            air_edges[at] = row
            bottom_next[x : x + 1] = row[0:1]
        heat = rate[...] * (bottom_next[...] - sea[...])
        flat = weights[...].reshape(banks * ocean_width, width)
        bank_at = as_column(bank[...].astype(f32)).astype(jnp.int32)
        shares = chosen_shares(heat, flat, bank_at, ocean_width)
        message[...] = start[...]
        message[0:rows, :] = jnp.where(
            iota((rows, width), 1) < ocean_width, shares, start[0:rows, :]
        )

    return outer_kernel


def patch_kernel(edges, _, out, sems):
    rows = out.shape[0]
    copies = [
        pltpu.make_async_copy(edges.at[pl.ds(0, 2)], out.at[pl.ds(0, 2)], sems.at[0]),
        pltpu.make_async_copy(edges.at[pl.ds(2, 2)], out.at[pl.ds(rows - 2, 2)], sems.at[1]),
    ]
    for copy in copies:
        copy.start()
    for copy in copies:
        copy.wait()


def make_last_kernel(count):
    def last_kernel(*refs):
        messages, (base, response, total_weight, bottom, mask, bank, weights, ocean_next, surface) = (
            refs[:count],
            refs[count:],
        )
        own = messages[0][...]
        if len(messages) == 2 and len(messages[1].shape) == 3:
            blocks = [messages[1][at] for at in range(messages[1].shape[0])]
        else:
            blocks = [ref[...] for ref in messages]
        rows, width = bottom.shape
        banks, ocean_width, _ = weights.shape
        slots = own.shape[0]
        depth = base.shape[0]
        own_part = own[0:rows]
        wanted = jnp.concatenate(
            [
                own_part[:, 3 * ocean_width : 3 * ocean_width + 1],
                own_part[:, 3 * ocean_width + 1 : 3 * ocean_width + 2],
            ],
            axis=0,
        )
        top = response[0:1, 0:1]
        sun = response[0:1, 1:2]
        lane = iota((slots, width), 1)
        hot = []
        values = []
        for block in blocks:
            label = block[rows : rows + 1, 0 : 2 * ocean_width]
            hot.append((wanted == label).astype(f32))
            raised = top * roll(block, 2 * ocean_width) + sun * roll(block, ocean_width)
            values.append(
                jnp.where(
                    lane < 2 * ocean_width, block, jnp.where(lane < 3 * ocean_width, raised, 0.0)
                )
            )
            values.append(
                jnp.where((lane >= 2 * ocean_width) & (lane < 3 * ocean_width), block, 0.0)
            )
        got = jnp.dot(
            jnp.concatenate(hot, axis=1),
            jnp.concatenate(values, axis=0),
            precision=highest,
            preferred_element_type=f32,
        )
        near = iota((rows, width), 1)
        seen = fold(
            jnp.where(
                (near >= 2 * ocean_width) & (near < 3 * ocean_width), got[0:rows], 0.0
            ),
            ocean_width,
        )
        forcing = got[rows : 2 * rows]
        heat = fold(jnp.where(near < ocean_width, forcing, 0.0), ocean_width)
        solar = fold(
            jnp.where((near >= ocean_width) & (near < 2 * ocean_width), forcing, 0.0), ocean_width
        )
        first = response[:, 0:1]
        second = response[:, 1:2]
        for at in range(0, base.shape[1], width):
            mine = (near + at) // ocean_width == iota((rows, width), 0)
            heat_row = jnp.sum(jnp.where(mine, heat, 0.0), axis=0, keepdims=True)
            solar_row = jnp.sum(jnp.where(mine, solar, 0.0), axis=0, keepdims=True)
            ocean_next[:, at : at + width] = base[:, at : at + width] + (
                first * heat_row + second * solar_row
            )
        flat = weights[...].reshape(banks * ocean_width, width)
        bank_at = as_column(bank[...].astype(f32)).astype(jnp.int32)
        spread = jnp.concatenate(
            [
                jnp.where((near + at) // ocean_width == bank_at, seen, 0.0)
                for at in range(0, banks * ocean_width, width)
            ],
            axis=1,
        )
        weighted = jnp.dot(spread, flat, precision=highest, preferred_element_type=f32)
        frac = mask[...].astype(f32)
        surface[...] = frac * (weighted / total_weight[...]) + (1.0 - frac) * bottom[...]

    return last_kernel


def shape_of(shape, dtype=f32):
    return jax.ShapeDtypeStruct(shape, dtype)


def whole(count):
    return [pl.BlockSpec(memory_space=pltpu.VMEM) for _ in range(count)]


params = pltpu.CompilerParams(vmem_limit_bytes=48 * 1024 * 1024)


def local(
    air_temp,
    wind_field,
    physics,
    sea_surface,
    shortwave,
    ocean_mask,
    owner_route,
    ocean_tile,
    weight_tile,
    remap_tiles,
    ocean_temp,
    mixing,
):
    rows, levels, width = air_temp.shape
    groups = lax.axis_size("cpl")
    ocean_width = remap_tiles.shape[1]
    slots = ocean_width
    ocean_shape = ocean_temp.shape

    packed = pl.pallas_call(
        pack_kernel,
        out_shape=shape_of((2, levels, width), bf16),
        in_specs=whole(2),
        out_specs=pl.BlockSpec(memory_space=pltpu.VMEM),
        compiler_params=params,
        name="pack",
    )(air_temp, wind_field)
    even_side, odd_side = exchange((packed, packed), "cpl")

    exchange_rate, total_weight, start, base, response = pl.pallas_call(
        start_kernel,
        grid=(1,),
        out_shape=(
            shape_of((rows, width)),
            shape_of((rows, width)),
            shape_of((slots, width)),
            shape_of(ocean_shape),
            shape_of((ocean_shape[0], width)),
        ),
        in_specs=[pl.BlockSpec((2, rows, 16, width), lambda i: (0, 0, 0, 0))] + whole(8),
        out_specs=whole(5),
        compiler_params=params,
        name="start",
    )(
        wind_field,
        shortwave,
        ocean_mask,
        owner_route.reshape(1, rows),
        ocean_tile,
        weight_tile,
        remap_tiles,
        ocean_temp,
        mixing,
    )

    last_pair = rows // 2 - 1
    air_specs = [
        pl.BlockSpec((2, levels, width), lambda i: (0, 0, 0)),
        pl.BlockSpec((2, levels, width), lambda i: (last_pair, 0, 0)),
    ]
    messages, partial = pl.pallas_call(
        make_edge_kernel(rows),
        grid=(1,),
        out_shape=(shape_of((2, 4, levels, width), bf16), shape_of((4, levels, width))),
        in_specs=air_specs
        + [
            pl.BlockSpec((2, 1, levels, width), lambda i: (0, 0, 0, 0)),
            pl.BlockSpec((2, 1, levels, width), lambda i: (0, rows - 1, 0, 0)),
        ]
        + whole(2),
        out_specs=whole(2),
        compiler_params=params,
        name="edge",
    )(air_temp, air_temp, wind_field, wind_field, even_side, odd_side)
    even_atm, odd_atm = exchange((messages[1], messages[0]), "atm")

    air_inner, near, bottom = pl.pallas_call(
        inner_kernel,
        out_shape=(
            shape_of((rows, levels, width)),
            shape_of((4, levels, width)),
            shape_of((rows, width)),
        ),
        in_specs=whole(6),
        out_specs=tuple(whole(3)),
        scratch_shapes=[pltpu.VMEM((rows, levels, width), f32)],
        compiler_params=params,
        name="inner",
    )(air_temp, wind_field, physics, packed, even_side, odd_side)

    air_edges, bottom_next, message = pl.pallas_call(
        make_outer_kernel(rows),
        grid=(1,),
        out_shape=(
            shape_of((4, levels, width)),
            shape_of((rows, width)),
            shape_of((slots, width)),
        ),
        in_specs=whole(3)
        + air_specs
        + [
            pl.BlockSpec((2, 2, levels, width), lambda i: (0, 0, 0, 0)),
            pl.BlockSpec((2, 2, levels, width), lambda i: (0, last_pair, 0, 0)),
        ]
        + whole(11),
        out_specs=whole(3),
        compiler_params=params,
        name="outer",
    )(
        even_atm,
        odd_atm,
        partial,
        air_temp,
        air_temp,
        wind_field,
        wind_field,
        packed,
        even_side,
        odd_side,
        near,
        physics,
        bottom,
        exchange_rate,
        sea_surface,
        weight_tile,
        remap_tiles,
        start,
    )

    if groups <= 4:
        gathered = [message] + [
            lax.ppermute(message, "cpl", [(i, (i + turn) % groups) for i in range(groups)])
            for turn in range(1, groups)
        ]
    else:
        gathered = [message, lax.all_gather(message, "cpl")]

    air_next = pl.pallas_call(
        patch_kernel,
        out_shape=shape_of((rows, levels, width)),
        in_specs=[pl.BlockSpec(memory_space=pl.ANY)] * 2,
        out_specs=pl.BlockSpec(memory_space=pl.ANY),
        scratch_shapes=[pltpu.SemaphoreType.DMA((2,))],
        input_output_aliases={1: 0},
        compiler_params=params,
        name="patch",
    )(air_edges, air_inner)

    ocean_next, surface_temp = pl.pallas_call(
        make_last_kernel(len(gathered)),
        out_shape=(shape_of(ocean_shape), shape_of((rows, width))),
        in_specs=whole(len(gathered) + 7),
        out_specs=tuple(whole(2)),
        compiler_params=params,
        name="last",
    )(
        *gathered,
        base,
        response,
        total_weight,
        bottom_next,
        ocean_mask,
        weight_tile,
        remap_tiles,
    )
    return (air_next, ocean_next, surface_temp)


def solution(mesh):
    placed = (
        P("atm", None, "cpl"),
        P(None, "atm", None, "cpl"),
        P(),
        P("atm", "cpl"),
        P("atm", "cpl"),
        P("atm", "cpl"),
        P("cpl", "atm", None),
        P("cpl", "atm"),
        P("cpl", "atm"),
        P(),
        P(None, ("atm", "cpl")),
        P(),
    )
    return jax.shard_map(
        local,
        mesh=mesh,
        in_specs=placed,
        out_specs=(P("atm", None, "cpl"), P(None, ("atm", "cpl")), P("atm", "cpl")),
        check_vma=False,
    )
```

```python
import jax
import jax.numpy as jnp
from jax import lax
from jax.experimental import pallas as pl
from jax.experimental.pallas import tpu as pltpu
from jax.sharding import PartitionSpec as P

diffusion_rate = 0.05
physics_rate = 0.5
highest = lax.Precision.HIGHEST
f32 = jnp.float32
bf16 = jnp.bfloat16


def pair_even(count):
    return [(i, i ^ 1) for i in range(count)]


def pair_odd(count):
    up = [(i, (i + 1) % count) for i in range(1, count, 2)]
    return up + [(target, source) for source, target in up]


def exchange(block, axis):
    count = lax.axis_size(axis)
    odd_side = lax.ppermute(block, axis, pair_odd(count))
    even_side = lax.ppermute(block, axis, pair_even(count))
    return even_side, odd_side


def shift(block, axis, turn):
    count = lax.axis_size(axis)
    return lax.ppermute(block, axis, [(i, (i + turn) % count) for i in range(count)])


def iota(shape, dim):
    return lax.broadcasted_iota(jnp.int32, shape, dim)


def roll(value, shift):
    return pltpu.roll(value, shift % value.shape[-1], value.ndim - 1)


def pick(flag, yes, no):
    return jnp.where(flag, yes, no)


def rates(first, second):
    return (
        jnp.maximum(first, 0.0) + diffusion_rate,
        diffusion_rate - jnp.minimum(first, 0.0),
        jnp.maximum(second, 0.0) + diffusion_rate,
        diffusion_rate - jnp.minimum(second, 0.0),
    )


def split(value):
    high = value.astype(bf16)
    return high, (value - high.astype(f32)).astype(bf16)


def physics_stack(physics):
    high, low = split(physics)
    return jnp.concatenate([high, high, low], axis=1)


def column(stack, field):
    high, low = split(field)
    tendency = jnp.dot(
        stack, jnp.concatenate([high, low, high], axis=0), preferred_element_type=f32
    )
    return field + physics_rate * jnp.tanh(tendency)


def pack_kernel(air, wind, *refs):
    others = (len(refs) - 5) // 2
    packed, air_here, wind_here = refs[others : others + 3]
    sems, other_sems = refs[-2:]
    rows, levels, width = air.shape
    lane = iota((levels, width), 1)
    place = lane // 4
    kind = lane % 4
    parts = sems.shape[1]
    size = rows // parts
    copies = []
    for part in range(parts):
        span = pl.ds(part * size, size)
        copies.append(
            (
                pltpu.make_async_copy(air.at[span], air_here.at[span], sems.at[0, part]),
                pltpu.make_async_copy(wind.at[:, span], wind_here.at[:, span], sems.at[1, part]),
            )
        )
        for copy in copies[-1]:
            copy.start()
    later = [
        pltpu.make_async_copy(source, target, other_sems.at[at])
        for at, (source, target) in enumerate(zip(refs[:others], refs[others + 3 : -2]))
    ]
    for copy in later:
        copy.start()
    cells = jnp.zeros((levels, width), f32)
    first = jnp.zeros((levels, width), f32)
    second = jnp.zeros((levels, width), f32)
    for x in range(rows):
        if x % size == 0:
            for copy in copies[x // size]:
                copy.wait()
        here = place == x
        cells = pick(here, roll(air_here[x], 4 * x + 2), cells)
        first = pick(here, roll(wind_here[0, x].astype(f32), 4 * x + 2), first)
        second = pick(here, roll(wind_here[1, x].astype(f32), 4 * x + 2), second)
    winds = pick((kind == 1) | (kind == 2), first, roll(second, 2))
    packed[0] = cells.astype(bf16)
    packed[1] = winds.astype(bf16)
    for copy in later:
        copy.wait()


def cpl_sides(even_side, odd_side):
    upper = lax.axis_index("cpl") % 2 == 0
    high = pick(upper, even_side[...].astype(f32), odd_side[...].astype(f32))
    low = pick(upper, odd_side[...].astype(f32), even_side[...].astype(f32))
    return low, high


def outer_cells(low, high):
    kind = iota(low.shape[1:], 1) % 4
    return pick(kind < 2, low[0], high[0])


def swap_cells(cells):
    kind = iota(cells.shape, 1) % 4
    return pick(kind == 2, roll(cells, 1), roll(cells, -1))


def sideways(field, swapped, x):
    width = field.shape[1]
    lane = iota(field.shape, 1)
    halo = roll(swapped, -(4 * x + 2))
    south = pick(lane == 0, halo, roll(field, 1))
    north = pick(lane == width - 1, halo, roll(field, -1))
    return south, north


def advance_row(center, west, east, south, north, speeds):
    cw, ce, cs, cn = speeds
    return (
        center
        + (cw * (west - center) + ce * (east - center))
        + (cs * (south - center) + cn * (north - center))
    )


def advance_outer(own, low, high, outer, west, east):
    kind = iota(outer.shape, 1) % 4
    south = roll(pick(kind == 0, outer, own), 1)
    north = roll(pick(kind == 3, outer, own), -1)
    first = pick(kind == 1, low[1], high[1])
    second = roll(pick(kind == 3, low[1], high[1]), -2)
    return advance_row(outer, west, east, south, north, rates(first, second))


def make_edge_kernel(rows, upper):
    def edge_kernel(air, wind, even_side, odd_side, _, message, partial):
        low, high = cpl_sides(even_side, odd_side)
        outer = outer_cells(low, high)
        center, inner = (air[1], air[0]) if upper else (air[0], air[1])
        cw, ce, cs, cn = rates(wind[0, 0].astype(f32), wind[1, 0].astype(f32))
        inside, outside = (cw, ce) if upper else (ce, cw)
        south, north = sideways(center, swap_cells(outer), rows - 1 if upper else 0)
        known = (
            center
            + (inside * (inner - center) - outside * center)
            + (cs * (south - center) + cn * (north - center))
        )
        partial[0] = known
        partial[1] = outside
        for at, value in enumerate((center, known, outside, outer)):
            message[at] = value.astype(bf16)

    return edge_kernel


def inner_kernel(
    air, wind, physics, own, even_side, odd_side, air_next, near, bottom, field, ready, sems
):
    rows, levels, width = air.shape
    low, high = cpl_sides(even_side, odd_side)
    outer = outer_cells(low, high)
    stack = physics_stack(physics[...])
    swapped = swap_cells(outer)
    after = advance_outer(
        own[0].astype(f32), low, high, outer, roll(outer, 4), roll(outer, -4)
    )
    swapped_after = swap_cells(column(stack, after))

    def speeds(x):
        return rates(wind[0, x].astype(f32), wind[1, x].astype(f32))

    def step(source, halo, x):
        center = source[x]
        south, north = sideways(center, halo, x)
        return advance_row(center, source[x - 1], source[x + 1], south, north, speeds(x))

    def pair(source, halo, x):
        return column(stack, jnp.concatenate([step(source, halo, x), step(source, halo, x + 1)], axis=1))

    for x in range(1, rows - 1, 2):
        both = pair(air, swapped, x)
        field[x] = both[:, :width]
        field[x + 1] = both[:, width:]
    near[0] = field[1]
    near[1] = field[2]
    near[2] = field[rows - 3]
    near[3] = field[rows - 2]
    bottom[...] = jnp.zeros_like(bottom)
    copies = []
    for x in range(2, rows - 2, 2):
        both = pair(field, swapped_after, x)
        ready[x] = both[:, :width]
        ready[x + 1] = both[:, width:]
        bottom[x : x + 1] = both[0:1, :width]
        bottom[x + 1 : x + 2] = both[0:1, width:]
        span = pl.ds(x, 2)
        copies.append(pltpu.make_async_copy(ready.at[span], air_next.at[span], sems.at[x // 2 - 1]))
        copies[-1].start()
    for copy in copies:
        copy.wait()


def as_column(row):
    size = row.shape[1]
    square = jnp.broadcast_to(row, (size, size))
    return jnp.sum(
        jnp.where(iota((size, size), 0) == iota((size, size), 1), square, 0.0),
        axis=1,
        keepdims=True,
    )


def fold(value, size):
    span = value.shape[1] // 2
    while span >= size:
        value = value + roll(value, span)
        span //= 2
    return value


def chosen_shares(fluxes, weights, bank, ocean_width):
    rows, width = fluxes.shape
    every = lax.dot_general(
        fluxes, weights, (((1,), (1,)), ((), ())), precision=highest, preferred_element_type=f32
    )
    total = jnp.zeros((rows, width), f32)
    for at in range(0, weights.shape[0], width):
        block = (iota((rows, width), 1) + at) // ocean_width
        total = total + jnp.where(block == bank, every[:, at : at + width], 0.0)
    return fold(total, ocean_width)


def start_kernel(
    winds, shortwave, mask, route, tile, bank, weights, ocean, mixing, _,
    exchange_rate, total_weight, message, base, response,
):
    rows, width = shortwave.shape
    depth = ocean.shape[0]
    banks, ocean_width, _ = weights.shape
    flat = weights[...].reshape(banks * ocean_width, width)
    frac = mask[...].astype(f32)
    bank_at = as_column(bank[...].astype(f32)).astype(jnp.int32)
    for x in range(rows):
        first = winds[0, x].astype(f32)[0:1]
        second = winds[1, x].astype(f32)[0:1]
        exchange_rate[x : x + 1] = first * first + second * second
    exchange_rate[...] = frac * (0.5 + 2.0 * jnp.sqrt(exchange_rate[...] + 0.01))
    solar = chosen_shares(frac * shortwave[...], flat, bank_at, ocean_width)
    lane = iota((rows, width), 1)
    total = jnp.zeros((rows, width), f32)
    for at in range(0, banks * ocean_width, width):
        hot = ((lane + at) // ocean_width == bank_at).astype(f32)
        total = total + jnp.dot(hot, flat[at : at + width], precision=highest, preferred_element_type=f32)
    total_weight[...] = total

    held = ocean[...]
    mixed = mixing[...]
    settled = 0.5 * held + jnp.dot(mixed, held, precision=highest, preferred_element_type=f32)
    base[...] = settled
    level = iota((depth, width), 0)
    profile = jnp.exp(level.astype(f32) / -8.0)
    profile = profile / jnp.sum(profile, axis=0, keepdims=True)
    part = iota((depth, width), 1)
    unit = jnp.where(part == 0, (level == 0).astype(f32), jnp.where(part == 1, profile, 0.0))
    response[...] = 0.5 * unit + jnp.dot(mixed, unit, precision=highest, preferred_element_type=f32)

    group = lax.axis_index("cpl")
    surface = jnp.zeros((rows, width), f32)
    for at in range(0, rows * ocean_width, width):
        spread = jnp.broadcast_to(settled[0:1, at : at + width], (rows, width))
        surface = surface + jnp.where((lane + at) // ocean_width == iota((rows, width), 0), spread, 0.0)
    surface = fold(surface, ocean_width)
    target = route[...] * rows + tile[...]
    target_at = as_column(target.astype(f32))
    own_at = (group * rows + iota((rows, width), 0)).astype(f32)
    message[...] = jnp.full(message.shape, -1.0, f32)
    message[0:rows, :] = jnp.where(
        lane < 2 * ocean_width,
        solar,
        jnp.where(
            lane < 3 * ocean_width,
            surface,
            jnp.where(lane == 3 * ocean_width, target_at, own_at),
        ),
    )
    message[rows : rows + 1, 0:rows] = target.astype(f32)
    message[rows : rows + 1, ocean_width : ocean_width + rows] = (
        group * rows + iota((1, rows), 1)
    ).astype(f32)


def make_outer_kernel(rows):
    def outer_kernel(
        above_ref, below_ref, partial_low, partial_high, air_low, air_high, wind_low, wind_high, own, even_side, odd_side,
        near, physics, bottom, rate, sea, bank, weights, start,
        air_edges, bottom_next, message,
    ):
        width = sea.shape[1]
        banks, ocean_width, _ = weights.shape
        above = above_ref[...].astype(f32)
        below = below_ref[...].astype(f32)
        low, high = cpl_sides(even_side, odd_side)
        outer = outer_cells(low, high)
        stack = physics_stack(physics[...])
        place = iota(outer.shape, 1) // 4
        after = advance_outer(
            own[0].astype(f32),
            low,
            high,
            outer,
            pick(place == 0, roll(below[3], -4 * (rows - 1)), roll(outer, 4)),
            pick(place == rows - 1, roll(above[3], 4 * (rows - 1)), roll(outer, -4)),
        )
        moved = jnp.concatenate(
            [
                below[1] + below[2] * air_low[0],
                partial_low[0] + partial_low[1] * below[0],
                partial_high[0] + partial_high[1] * above[0],
                above[1] + above[2] * air_high[1],
                after,
            ],
            axis=1,
        )
        stepped = column(stack, moved)
        parts = [stepped[:, at * width : (at + 1) * width] for at in range(5)]
        halo = swap_cells(parts[4])
        inner = [near[at] for at in range(4)]
        bottom_next[...] = bottom[...]
        cells = []
        for center, west, east, wind, at, x in (
            (parts[1], parts[0], inner[0], wind_low, 0, 0),
            (inner[0], parts[1], inner[1], wind_low, 1, 1),
            (inner[3], inner[2], parts[2], wind_high, 0, rows - 2),
            (parts[2], inner[3], parts[3], wind_high, 1, rows - 1),
        ):
            south, north = sideways(center, halo, x)
            speeds = rates(wind[0, at].astype(f32), wind[1, at].astype(f32))
            cells.append(advance_row(center, west, east, south, north, speeds))
        final = column(stack, jnp.concatenate(cells, axis=1))
        for at, x in enumerate((0, 1, rows - 2, rows - 1)):
            row = final[:, at * width : (at + 1) * width]
            air_edges[at] = row
            bottom_next[x : x + 1] = row[0:1]
        heat = rate[...] * (bottom_next[...] - sea[...])
        flat = weights[...].reshape(banks * ocean_width, width)
        bank_at = as_column(bank[...].astype(f32)).astype(jnp.int32)
        shares = chosen_shares(heat, flat, bank_at, ocean_width)
        message[...] = start[...]
        message[0:rows, :] = jnp.where(
            iota((rows, width), 1) < ocean_width, shares, start[0:rows, :]
        )

    return outer_kernel


def patch_kernel(edges, _, out, sems):
    rows = out.shape[0]
    copies = [
        pltpu.make_async_copy(edges.at[pl.ds(0, 2)], out.at[pl.ds(0, 2)], sems.at[0]),
        pltpu.make_async_copy(edges.at[pl.ds(2, 2)], out.at[pl.ds(rows - 2, 2)], sems.at[1]),
    ]
    for copy in copies:
        copy.start()
    for copy in copies:
        copy.wait()


def make_last_kernel(count):
    def last_kernel(*refs):
        messages, (base, response, total_weight, bottom, mask, bank, weights, ocean_next, surface) = (
            refs[:count],
            refs[count:],
        )
        own = messages[0][...]
        if len(messages) == 2 and len(messages[1].shape) == 3:
            blocks = [messages[1][at] for at in range(messages[1].shape[0])]
        else:
            blocks = [ref[...] for ref in messages]
        rows, width = bottom.shape
        banks, ocean_width, _ = weights.shape
        slots = own.shape[0]
        depth = base.shape[0]
        own_part = own[0:rows]
        wanted = jnp.concatenate(
            [
                own_part[:, 3 * ocean_width : 3 * ocean_width + 1],
                own_part[:, 3 * ocean_width + 1 : 3 * ocean_width + 2],
            ],
            axis=0,
        )
        top = response[0:1, 0:1]
        sun = response[0:1, 1:2]
        lane = iota((slots, width), 1)
        hot = []
        values = []
        for block in blocks:
            label = block[rows : rows + 1, 0 : 2 * ocean_width]
            hot.append((wanted == label).astype(f32))
            raised = top * roll(block, 2 * ocean_width) + sun * roll(block, ocean_width)
            values.append(
                jnp.where(
                    lane < 2 * ocean_width, block, jnp.where(lane < 3 * ocean_width, raised, 0.0)
                )
            )
            values.append(
                jnp.where((lane >= 2 * ocean_width) & (lane < 3 * ocean_width), block, 0.0)
            )
        got = jnp.dot(
            jnp.concatenate(hot, axis=1),
            jnp.concatenate(values, axis=0),
            precision=highest,
            preferred_element_type=f32,
        )
        near = iota((rows, width), 1)
        seen = fold(
            jnp.where(
                (near >= 2 * ocean_width) & (near < 3 * ocean_width), got[0:rows], 0.0
            ),
            ocean_width,
        )
        forcing = got[rows : 2 * rows]
        heat = fold(jnp.where(near < ocean_width, forcing, 0.0), ocean_width)
        solar = fold(
            jnp.where((near >= ocean_width) & (near < 2 * ocean_width), forcing, 0.0), ocean_width
        )
        first = response[:, 0:1]
        second = response[:, 1:2]
        for at in range(0, base.shape[1], width):
            mine = (near + at) // ocean_width == iota((rows, width), 0)
            heat_row = jnp.sum(jnp.where(mine, heat, 0.0), axis=0, keepdims=True)
            solar_row = jnp.sum(jnp.where(mine, solar, 0.0), axis=0, keepdims=True)
            ocean_next[:, at : at + width] = base[:, at : at + width] + (
                first * heat_row + second * solar_row
            )
        flat = weights[...].reshape(banks * ocean_width, width)
        bank_at = as_column(bank[...].astype(f32)).astype(jnp.int32)
        spread = jnp.concatenate(
            [
                jnp.where((near + at) // ocean_width == bank_at, seen, 0.0)
                for at in range(0, banks * ocean_width, width)
            ],
            axis=1,
        )
        weighted = jnp.dot(spread, flat, precision=highest, preferred_element_type=f32)
        frac = mask[...].astype(f32)
        surface[...] = frac * (weighted / total_weight[...]) + (1.0 - frac) * bottom[...]

    return last_kernel


def shape_of(shape, dtype=f32):
    return jax.ShapeDtypeStruct(shape, dtype)


def whole(count):
    return [pl.BlockSpec(memory_space=pltpu.VMEM) for _ in range(count)]


def in_hbm(value):
    return pltpu.with_memory_space_constraint(value, pltpu.HBM)


params = pltpu.CompilerParams(vmem_limit_bytes=48 * 1024 * 1024)


def local(
    air_temp,
    wind_field,
    physics,
    sea_surface,
    shortwave,
    ocean_mask,
    owner_route,
    ocean_tile,
    weight_tile,
    remap_tiles,
    ocean_temp,
    mixing,
):
    rows, levels, width = air_temp.shape
    groups = lax.axis_size("cpl")
    ocean_width = remap_tiles.shape[1]
    slots = ocean_width
    ocean_shape = ocean_temp.shape

    others = (
        physics,
        sea_surface,
        shortwave,
        ocean_mask,
        owner_route.reshape(1, rows),
        ocean_tile,
        weight_tile,
        remap_tiles,
        ocean_temp,
        mixing,
    )
    (
        packed,
        air_here,
        wind_here,
        physics,
        sea_surface,
        shortwave,
        ocean_mask,
        owner_route,
        ocean_tile,
        weight_tile,
        remap_tiles,
        ocean_temp,
        mixing,
    ) = (
        pl.pallas_call(
            pack_kernel,
            out_shape=(pltpu.VMEM((2, levels, width), bf16),)
            + tuple(
                pltpu.VMEM(value.shape, value.dtype) for value in (air_temp, wind_field) + others
            ),
            in_specs=[pl.BlockSpec(memory_space=pltpu.HBM)] * (2 + len(others)),
            out_specs=tuple(whole(3 + len(others))),
            scratch_shapes=[
                pltpu.SemaphoreType.DMA((2, 2)),
                pltpu.SemaphoreType.DMA((len(others),)),
            ],
            compiler_params=params,
            name="pack",
        )(*(in_hbm(value) for value in (air_temp, wind_field) + others))
    )
    even_side, odd_side = exchange(packed, "cpl")

    exchange_rate, total_weight, start, base, response = pl.pallas_call(
        start_kernel,
        grid=(1,),
        out_shape=(
            shape_of((rows, width)),
            shape_of((rows, width)),
            shape_of((slots, width)),
            shape_of(ocean_shape),
            shape_of((ocean_shape[0], width)),
        ),
        in_specs=[pl.BlockSpec((2, rows, 16, width), lambda i: (0, 0, 0, 0))]
        + whole(8)
        + [pl.BlockSpec(memory_space=pl.ANY)],
        out_specs=whole(5),
        compiler_params=params,
        name="start",
    )(
        wind_here,
        shortwave,
        ocean_mask,
        owner_route,
        ocean_tile,
        weight_tile,
        remap_tiles,
        ocean_temp,
        mixing,
        packed,
    )

    last_pair = rows // 2 - 1
    air_specs = [
        pl.BlockSpec((2, levels, width), lambda i: (0, 0, 0)),
        pl.BlockSpec((2, levels, width), lambda i: (last_pair, 0, 0)),
    ]

    def edge(upper, after):
        return pl.pallas_call(
            make_edge_kernel(rows, upper),
            grid=(1,),
            out_shape=(shape_of((4, levels, width), bf16), shape_of((2, levels, width))),
            in_specs=[
                air_specs[upper],
                pl.BlockSpec((2, 1, levels, width), lambda i: (0, (rows - 1) * upper, 0, 0)),
            ]
            + whole(2)
            + [pl.BlockSpec(memory_space=pl.ANY)],
            out_specs=whole(2),
            compiler_params=params,
            name="edge",
        )(air_here, wind_here, even_side, odd_side, after)

    to_high, partial_high = edge(1, start)
    below = shift(to_high, "atm", 1)
    to_low, partial_low = edge(0, partial_high)
    above = shift(to_low, "atm", -1)

    air_inner, near, bottom = pl.pallas_call(
        inner_kernel,
        out_shape=(
            shape_of((rows, levels, width)),
            shape_of((4, levels, width)),
            shape_of((rows, width)),
        ),
        in_specs=whole(6),
        out_specs=tuple([pl.BlockSpec(memory_space=pltpu.HBM)] + whole(2)),
        scratch_shapes=[
            pltpu.VMEM((rows, levels, width), f32),
            pltpu.VMEM((rows, levels, width), f32),
            pltpu.SemaphoreType.DMA((rows // 2 - 2,)),
        ],
        compiler_params=params,
        name="inner",
    )(air_here, wind_here, physics, packed, even_side, odd_side)

    air_edges, bottom_next, message = pl.pallas_call(
        make_outer_kernel(rows),
        grid=(1,),
        out_shape=(
            shape_of((4, levels, width)),
            shape_of((rows, width)),
            shape_of((slots, width)),
        ),
        in_specs=whole(4)
        + air_specs
        + [
            pl.BlockSpec((2, 2, levels, width), lambda i: (0, 0, 0, 0)),
            pl.BlockSpec((2, 2, levels, width), lambda i: (0, last_pair, 0, 0)),
        ]
        + whole(11),
        out_specs=whole(3),
        compiler_params=params,
        name="outer",
    )(
        above,
        below,
        partial_low,
        partial_high,
        air_here,
        air_here,
        wind_here,
        wind_here,
        packed,
        even_side,
        odd_side,
        near,
        physics,
        bottom,
        exchange_rate,
        sea_surface,
        weight_tile,
        remap_tiles,
        start,
    )

    if groups <= 4:
        turns = sorted(range(1, groups), key=lambda turn: abs(2 * turn - groups))
        gathered = [message] + [shift(message, "cpl", turn) for turn in turns]
    else:
        gathered = [message, lax.all_gather(message, "cpl")]

    air_next = pl.pallas_call(
        patch_kernel,
        out_shape=shape_of((rows, levels, width)),
        in_specs=[pl.BlockSpec(memory_space=pl.ANY)] * 2,
        out_specs=pl.BlockSpec(memory_space=pl.ANY),
        scratch_shapes=[pltpu.SemaphoreType.DMA((2,))],
        input_output_aliases={1: 0},
        compiler_params=params,
        name="patch",
    )(air_edges, air_inner)

    ocean_next, surface_temp = pl.pallas_call(
        make_last_kernel(len(gathered)),
        out_shape=(shape_of(ocean_shape), shape_of((rows, width))),
        in_specs=whole(len(gathered) + 7),
        out_specs=tuple(whole(2)),
        compiler_params=params,
        name="last",
    )(
        *gathered,
        base,
        response,
        total_weight,
        bottom_next,
        ocean_mask,
        weight_tile,
        remap_tiles,
    )
    return (air_next, ocean_next, surface_temp)


def solution(mesh):
    placed = (
        P("atm", None, "cpl"),
        P(None, "atm", None, "cpl"),
        P(),
        P("atm", "cpl"),
        P("atm", "cpl"),
        P("atm", "cpl"),
        P("cpl", "atm", None),
        P("cpl", "atm"),
        P("cpl", "atm"),
        P(),
        P(None, ("atm", "cpl")),
        P(),
    )
    return jax.shard_map(
        local,
        mesh=mesh,
        in_specs=placed,
        out_specs=(P("atm", None, "cpl"), P(None, ("atm", "cpl")), P("atm", "cpl")),
        check_vma=False,
    )
```

```python
import jax
import jax.numpy as jnp
from jax import lax
from jax.experimental import pallas as pl
from jax.experimental.pallas import tpu as pltpu
from jax.sharding import PartitionSpec as P

diffusion_rate = 0.05
physics_rate = 0.5
highest = lax.Precision.HIGHEST
f32 = jnp.float32
bf16 = jnp.bfloat16


def pair_even(count):
    return [(i, i ^ 1) for i in range(count)]


def pair_odd(count):
    up = [(i, (i + 1) % count) for i in range(1, count, 2)]
    return up + [(target, source) for source, target in up]


def exchange(to_even, to_odd, axis):
    count = lax.axis_size(axis)
    odd_side = lax.ppermute(to_odd, axis, pair_odd(count))
    even_side = lax.ppermute(to_even, axis, pair_even(count))
    return even_side, odd_side


def shift(block, axis, turn):
    count = lax.axis_size(axis)
    return lax.ppermute(block, axis, [(i, (i + turn) % count) for i in range(count)])


def iota(shape, dim):
    return lax.broadcasted_iota(jnp.int32, shape, dim)


def roll(value, shift):
    return pltpu.roll(value, shift % value.shape[-1], value.ndim - 1)


def pick(flag, yes, no):
    return jnp.where(flag, yes, no)


def rates(first, second):
    return (
        jnp.maximum(first, 0.0) + diffusion_rate,
        diffusion_rate - jnp.minimum(first, 0.0),
        jnp.maximum(second, 0.0) + diffusion_rate,
        diffusion_rate - jnp.minimum(second, 0.0),
    )


def split(value):
    high = value.astype(bf16)
    return high, (value - high.astype(f32)).astype(bf16)


def physics_stack(physics):
    high, low = split(physics)
    return jnp.concatenate([high, high, low], axis=1)


def column(stack, field):
    high, low = split(field)
    tendency = jnp.dot(
        stack, jnp.concatenate([high, low, high], axis=0), preferred_element_type=f32
    )
    return field + physics_rate * jnp.tanh(tendency)


def pack_kernel(air, wind, *refs):
    others = (len(refs) - 7) // 2
    packed, to_even, to_odd, air_here, wind_here = refs[others : others + 5]
    sems, other_sems = refs[-2:]
    rows, levels, width = air.shape
    lane = iota((levels, width), 1)
    place = lane // 4
    kind = lane % 4
    parts = sems.shape[1]
    size = rows // parts
    copies = []
    for part in range(parts):
        span = pl.ds(part * size, size)
        copies.append(
            (
                pltpu.make_async_copy(air.at[span], air_here.at[span], sems.at[0, part]),
                pltpu.make_async_copy(wind.at[:, span], wind_here.at[:, span], sems.at[1, part]),
            )
        )
        for copy in copies[-1]:
            copy.start()
    later = [
        pltpu.make_async_copy(source, target, other_sems.at[at])
        for at, (source, target) in enumerate(zip(refs[:others], refs[others + 5 : -2]))
    ]
    for copy in later:
        copy.start()
    cells = jnp.zeros((levels, width), bf16)
    first = jnp.zeros((levels, width), bf16)
    second = jnp.zeros((levels, width), bf16)
    for x in range(rows):
        if x % size == 0:
            for copy in copies[x // size]:
                copy.wait()
        here = place == x
        cells = pick(here, roll(air_here[x].astype(bf16), 4 * x + 2), cells)
        first = pick(here, roll(wind_here[0, x], 4 * x + 2), first)
        second = pick(here, roll(wind_here[1, x], 4 * x + 2), second)
    cells, first, second = (value.astype(f32) for value in (cells, first, second))
    winds = pick((kind == 1) | (kind == 2), first, roll(second, 2))
    to_high = pick(kind < 2, cells, pick(kind == 2, roll(winds, 1), winds))
    to_low = pick(kind >= 2, cells, pick(kind == 0, roll(winds, -2), roll(winds, -3)))
    upper = lax.axis_index("cpl") % 2 == 0
    packed[...] = cells
    to_even[...] = pick(upper, to_high, to_low).astype(bf16)
    to_odd[...] = pick(upper, to_low, to_high).astype(bf16)
    for copy in later:
        copy.wait()


def cpl_sides(even_side, odd_side):
    upper = lax.axis_index("cpl") % 2 == 0
    high = pick(upper, even_side[...].astype(f32), odd_side[...].astype(f32))
    low = pick(upper, odd_side[...].astype(f32), even_side[...].astype(f32))
    return low, high


def outer_cells(low, high):
    kind = iota(low.shape, 1) % 4
    return pick(kind < 2, low, high)


def swap_cells(cells):
    kind = iota(cells.shape, 1) % 4
    return pick(kind == 2, roll(cells, 1), roll(cells, -1))


def sideways(field, swapped, x):
    width = field.shape[1]
    lane = iota(field.shape, 1)
    halo = roll(swapped, -(4 * x + 2))
    south = pick(lane == 0, halo, roll(field, 1))
    north = pick(lane == width - 1, halo, roll(field, -1))
    return south, north


def advance_row(center, west, east, south, north, speeds):
    cw, ce, cs, cn = speeds
    return (
        center
        + (cw * (west - center) + ce * (east - center))
        + (cs * (south - center) + cn * (north - center))
    )


def advance_outer(own, low, high, outer, west, east):
    kind = iota(outer.shape, 1) % 4
    south = roll(pick(kind == 0, outer, own), 1)
    north = roll(pick(kind == 3, outer, own), -1)
    first = pick(kind == 1, roll(low, -1), roll(high, 2))
    second = pick(kind == 1, roll(low, -2), roll(high, 1))
    return advance_row(outer, west, east, south, north, rates(first, second))


def pack_corners(outer, x):
    levels, width = outer.shape
    place = iota((8, width), 1) // 4
    held = jnp.zeros((8, width), f32)
    for at in range(levels // 8):
        held = pick(place == at, roll(outer[8 * at : 8 * at + 8], 4 * (at - x)), held)
    return jnp.concatenate([held, jnp.zeros_like(held)], axis=0)


def unpack_corners(held, levels, x):
    return jnp.concatenate([roll(held[0:8], 4 * (x - at)) for at in range(levels // 8)], axis=0)


def make_edge_kernel(rows, upper):
    def edge_kernel(air, wind, even_side, odd_side, _, message, partial):
        low, high = cpl_sides(even_side, odd_side)
        outer = outer_cells(low, high)
        center, inner = (air[1], air[0]) if upper else (air[0], air[1])
        levels = center.shape[0]
        cw, ce, cs, cn = rates(wind[0, 0].astype(f32), wind[1, 0].astype(f32))
        inside, outside = (cw, ce) if upper else (ce, cw)
        south, north = sideways(center, swap_cells(outer), rows - 1 if upper else 0)
        known = (
            center
            + (inside * (inner - center) - outside * center)
            + (cs * (south - center) + cn * (north - center))
        )
        partial[0] = known
        partial[1] = outside
        for at, value in enumerate((center, known, outside)):
            message[at * levels : (at + 1) * levels] = value.astype(bf16)
        message[3 * levels :] = pack_corners(outer, rows - 1 if upper else 0).astype(bf16)

    return edge_kernel


def inner_kernel(
    air, wind, stack_ref, own, even_side, odd_side, ready, near, bottom, field
):
    rows, levels, width = air.shape
    low, high = cpl_sides(even_side, odd_side)
    outer = outer_cells(low, high)
    stack = stack_ref[...]
    swapped = swap_cells(outer)
    after = advance_outer(
        own[...], low, high, outer, roll(outer, 4), roll(outer, -4)
    )
    swapped_after = swap_cells(column(stack, after))

    def speeds(x):
        return rates(wind[0, x].astype(f32), wind[1, x].astype(f32))

    def step(source, halo, x):
        center = source[x]
        south, north = sideways(center, halo, x)
        return advance_row(center, source[x - 1], source[x + 1], south, north, speeds(x))

    def pair(source, halo, x):
        return column(stack, jnp.concatenate([step(source, halo, x), step(source, halo, x + 1)], axis=1))

    for x in range(1, rows - 1, 2):
        both = pair(air, swapped, x)
        field[x] = both[:, :width]
        field[x + 1] = both[:, width:]
    near[0] = field[1]
    near[1] = field[2]
    near[2] = field[rows - 3]
    near[3] = field[rows - 2]
    bottom[...] = jnp.zeros_like(bottom)
    for x in range(2, rows - 2, 2):
        both = pair(field, swapped_after, x)
        ready[x] = both[:, :width]
        ready[x + 1] = both[:, width:]
        bottom[x : x + 1] = both[0:1, :width]
        bottom[x + 1 : x + 2] = both[0:1, width:]


def as_column(row):
    size = row.shape[1]
    square = jnp.broadcast_to(row, (size, size))
    return jnp.sum(
        jnp.where(iota((size, size), 0) == iota((size, size), 1), square, 0.0),
        axis=1,
        keepdims=True,
    )


def fold(value, size):
    span = value.shape[1] // 2
    while span >= size:
        value = value + roll(value, span)
        span //= 2
    return value


def chosen_shares(fluxes, halves, bank, ocean_width):
    rows, width = fluxes.shape
    high, low = split(fluxes)
    every = jnp.dot(
        jnp.concatenate([high, low, high], axis=1), halves, preferred_element_type=f32
    )
    total = jnp.zeros((rows, width), f32)
    for at in range(0, halves.shape[1], width):
        block = (iota((rows, width), 1) + at) // ocean_width
        total = total + jnp.where(block == bank, every[:, at : at + width], 0.0)
    return fold(total, ocean_width)


def start_kernel(
    winds, shortwave, mask, route, tile, bank, physics, weights_far, ocean_far, mixing_far, _,
    exchange_rate, message, forward, backward, stack, weights, ocean, mixing, sems,
):
    copies = [
        pltpu.make_async_copy(source, target, sems.at[at])
        for at, (source, target) in enumerate(
            ((weights_far, weights), (ocean_far, ocean), (mixing_far, mixing))
        )
    ]
    for copy in copies:
        copy.start()
    stack[...] = physics_stack(physics[...])
    for copy in copies:
        copy.wait()
    rows, width = shortwave.shape
    banks, ocean_width, _ = weights.shape
    flat = weights[...].reshape(banks * ocean_width, width)
    high, low = split(flat)
    backward[...] = jnp.concatenate([high, high, low], axis=0)
    turned = flat.T
    high, low = split(turned)
    forward[...] = jnp.concatenate([high, high, low], axis=0)
    frac = mask[...].astype(f32)
    bank_at = as_column(bank[...].astype(f32)).astype(jnp.int32)
    for x in range(rows):
        first = winds[0, x].astype(f32)[0:1]
        second = winds[1, x].astype(f32)[0:1]
        exchange_rate[x : x + 1] = first * first + second * second
    exchange_rate[...] = frac * (0.5 + 2.0 * jnp.sqrt(exchange_rate[...] + 0.01))
    solar = chosen_shares(frac * shortwave[...], forward[...], bank_at, ocean_width)
    lane = iota((rows, width), 1)
    settled = 0.5 * ocean[0:8] + jnp.dot(
        mixing[0:8], ocean[...], precision=highest, preferred_element_type=f32
    )
    group = lax.axis_index("cpl")
    surface = jnp.zeros((rows, width), f32)
    for at in range(0, rows * ocean_width, width):
        spread = jnp.broadcast_to(settled[0:1, at : at + width], (rows, width))
        surface = surface + jnp.where((lane + at) // ocean_width == iota((rows, width), 0), spread, 0.0)
    surface = fold(surface, ocean_width)
    target = route[...] * rows + tile[...]
    target_at = as_column(target.astype(f32))
    own_at = (group * rows + iota((rows, width), 0)).astype(f32)
    message[...] = jnp.full(message.shape, -1.0, f32)
    message[0:rows, :] = jnp.where(
        lane < 2 * ocean_width,
        solar,
        jnp.where(
            lane < 3 * ocean_width,
            surface,
            jnp.where(lane == 3 * ocean_width, target_at, own_at),
        ),
    )
    message[rows : rows + 1, 0:rows] = target.astype(f32)
    message[rows : rows + 1, ocean_width : ocean_width + rows] = (
        group * rows + iota((1, rows), 1)
    ).astype(f32)


def make_outer_kernel(rows):
    def outer_kernel(
        above_ref, below_ref, partial_low, partial_high, air_low, air_high, wind_low, wind_high, own, even_side, odd_side,
        near, stack_ref, bottom, rate, sea, bank, forward, start,
        air_edges, bottom_next, message,
    ):
        width = sea.shape[1]
        ocean_width = start.shape[0]
        levels = air_low.shape[1]
        above = [above_ref[at * levels : (at + 1) * levels].astype(f32) for at in range(3)]
        below = [below_ref[at * levels : (at + 1) * levels].astype(f32) for at in range(3)]
        above.append(unpack_corners(above_ref[3 * levels :].astype(f32), levels, rows - 1))
        below.append(unpack_corners(below_ref[3 * levels :].astype(f32), levels, 0))
        low, high = cpl_sides(even_side, odd_side)
        outer = outer_cells(low, high)
        stack = stack_ref[...]
        place = iota(outer.shape, 1) // 4
        after = advance_outer(
            own[...],
            low,
            high,
            outer,
            pick(place == 0, below[3], roll(outer, 4)),
            pick(place == rows - 1, above[3], roll(outer, -4)),
        )
        moved = jnp.concatenate(
            [
                below[1] + below[2] * air_low[0],
                partial_low[0] + partial_low[1] * below[0],
                partial_high[0] + partial_high[1] * above[0],
                above[1] + above[2] * air_high[1],
                after,
            ],
            axis=1,
        )
        stepped = column(stack, moved)
        parts = [stepped[:, at * width : (at + 1) * width] for at in range(5)]
        halo = swap_cells(parts[4])
        inner = [near[at] for at in range(4)]
        bottom_next[...] = bottom[...]
        cells = []
        for center, west, east, wind, at, x in (
            (parts[1], parts[0], inner[0], wind_low, 0, 0),
            (inner[0], parts[1], inner[1], wind_low, 1, 1),
            (inner[3], inner[2], parts[2], wind_high, 0, rows - 2),
            (parts[2], inner[3], parts[3], wind_high, 1, rows - 1),
        ):
            south, north = sideways(center, halo, x)
            speeds = rates(wind[0, at].astype(f32), wind[1, at].astype(f32))
            cells.append(advance_row(center, west, east, south, north, speeds))
        final = column(stack, jnp.concatenate(cells, axis=1))
        for at, x in enumerate((0, 1, rows - 2, rows - 1)):
            row = final[:, at * width : (at + 1) * width]
            air_edges[at] = row
            bottom_next[x : x + 1] = row[0:1]
        heat = rate[...] * (bottom_next[...] - sea[...])
        bank_at = as_column(bank[...].astype(f32)).astype(jnp.int32)
        shares = chosen_shares(heat, forward[...], bank_at, ocean_width)
        message[...] = start[...]
        message[0:rows, :] = jnp.where(
            iota((rows, width), 1) < ocean_width, shares, start[0:rows, :]
        )

    return outer_kernel


def settle_kernel(
    edges, inner, bank, weights, ocean, mixing, out, base, response, total_weight, sems
):
    rows = out.shape[0]
    middle = pl.ds(2, rows - 4)
    copies = [
        pltpu.make_async_copy(inner.at[middle], out.at[middle], sems.at[2]),
        pltpu.make_async_copy(edges.at[pl.ds(0, 2)], out.at[pl.ds(0, 2)], sems.at[0]),
        pltpu.make_async_copy(edges.at[pl.ds(2, 2)], out.at[pl.ds(rows - 2, 2)], sems.at[1]),
    ]
    for copy in copies:
        copy.start()
    width = total_weight.shape[1]
    depth = ocean.shape[0]
    banks, ocean_width, _ = weights.shape
    sums = jnp.concatenate(
        [jnp.sum(weights[at], axis=0, keepdims=True) for at in range(banks)], axis=0
    )
    bank_at = as_column(bank[...].astype(f32)).astype(jnp.int32)
    hot = (iota((rows, banks), 1) == bank_at).astype(f32)
    total_weight[...] = jnp.dot(hot, sums, precision=highest, preferred_element_type=f32)
    mixed = mixing[...]
    held = ocean[...]
    base[...] = 0.5 * held + jnp.dot(mixed, held, precision=highest, preferred_element_type=f32)
    level = iota((depth, width), 0)
    profile = jnp.exp(level.astype(f32) / -8.0)
    profile = profile / jnp.sum(profile, axis=0, keepdims=True)
    part = iota((depth, width), 1)
    unit = jnp.where(part == 0, (level == 0).astype(f32), jnp.where(part == 1, profile, 0.0))
    response[...] = 0.5 * unit + jnp.dot(mixed, unit, precision=highest, preferred_element_type=f32)
    for copy in copies:
        copy.wait()


def make_last_kernel(count):
    def last_kernel(*refs):
        messages, (base, response, total_weight, bottom, mask, bank, backward, ocean_next, surface, ocean_here, surface_here, sems) = (
            refs[:count],
            refs[count:],
        )
        own = messages[0][...]
        if len(messages) == 2 and len(messages[1].shape) == 3:
            blocks = [messages[1][at] for at in range(messages[1].shape[0])]
        else:
            blocks = [ref[...] for ref in messages]
        rows, width = bottom.shape
        slots = own.shape[0]
        ocean_width = slots
        cells = backward.shape[0] // 3
        own_part = own[0:rows]
        wanted = jnp.concatenate(
            [
                own_part[:, 3 * ocean_width : 3 * ocean_width + 1],
                own_part[:, 3 * ocean_width + 1 : 3 * ocean_width + 2],
            ],
            axis=0,
        )
        top = response[0:1, 0:1]
        sun = response[0:1, 1:2]
        lane = iota((slots, width), 1)
        hot = []
        values = []
        for block in blocks:
            label = block[rows : rows + 1, 0 : 2 * ocean_width]
            hot.append((wanted == label).astype(f32).astype(bf16))
            raised = top * roll(block, 2 * ocean_width) + sun * roll(block, ocean_width)
            values.append(
                jnp.where(
                    lane < 2 * ocean_width, block, jnp.where(lane < 3 * ocean_width, raised, 0.0)
                )
            )
            values.append(
                jnp.where((lane >= 2 * ocean_width) & (lane < 3 * ocean_width), block, 0.0)
            )
        high, low = split(jnp.concatenate(values, axis=0))
        got = jnp.dot(
            jnp.concatenate(hot + hot, axis=1),
            jnp.concatenate([high, low], axis=0),
            preferred_element_type=f32,
        )
        near = iota((rows, width), 1)
        seen = fold(
            jnp.where(
                (near >= 2 * ocean_width) & (near < 3 * ocean_width), got[0:rows], 0.0
            ),
            ocean_width,
        )
        bank_at = as_column(bank[...].astype(f32)).astype(jnp.int32)
        high, low = split(
            jnp.concatenate(
                [
                    jnp.where((near + at) // ocean_width == bank_at, seen, 0.0)
                    for at in range(0, cells, width)
                ],
                axis=1,
            )
        )
        weighted = jnp.dot(
            jnp.concatenate([high, low, high], axis=1), backward[...], preferred_element_type=f32
        )
        forcing = got[rows : 2 * rows]
        heat = fold(jnp.where(near < ocean_width, forcing, 0.0), ocean_width)
        solar = fold(
            jnp.where((near >= ocean_width) & (near < 2 * ocean_width), forcing, 0.0), ocean_width
        )
        first = response[:, 0:1]
        second = response[:, 1:2]
        for at in range(0, base.shape[1], width):
            mine = (near + at) // ocean_width == iota((rows, width), 0)
            heat_row = jnp.sum(jnp.where(mine, heat, 0.0), axis=0, keepdims=True)
            solar_row = jnp.sum(jnp.where(mine, solar, 0.0), axis=0, keepdims=True)
            ocean_here[:, at : at + width] = base[:, at : at + width] + (
                first * heat_row + second * solar_row
            )
        ocean_out = pltpu.make_async_copy(ocean_here, ocean_next, sems.at[0])
        ocean_out.start()
        frac = mask[...].astype(f32)
        surface_here[...] = frac * (weighted / total_weight[...]) + (1.0 - frac) * bottom[...]
        surface_out = pltpu.make_async_copy(surface_here, surface, sems.at[1])
        surface_out.start()
        ocean_out.wait()
        surface_out.wait()

    return last_kernel


def shape_of(shape, dtype=f32):
    return jax.ShapeDtypeStruct(shape, dtype)


def whole(count):
    return [pl.BlockSpec(memory_space=pltpu.VMEM) for _ in range(count)]


def in_hbm(value):
    return pltpu.with_memory_space_constraint(value, pltpu.HBM)


params = pltpu.CompilerParams(vmem_limit_bytes=48 * 1024 * 1024)


def local(
    air_temp,
    wind_field,
    physics,
    sea_surface,
    shortwave,
    ocean_mask,
    owner_route,
    ocean_tile,
    weight_tile,
    remap_tiles,
    ocean_temp,
    mixing,
):
    rows, levels, width = air_temp.shape
    groups = lax.axis_size("cpl")
    ocean_width = remap_tiles.shape[1]
    slots = ocean_width
    ocean_shape = ocean_temp.shape

    others = (
        physics,
        sea_surface,
        shortwave,
        ocean_mask,
        owner_route.reshape(1, rows),
        ocean_tile,
        weight_tile,
    )
    (
        packed,
        to_even,
        to_odd,
        air_here,
        wind_here,
        physics,
        sea_surface,
        shortwave,
        ocean_mask,
        owner_route,
        ocean_tile,
        weight_tile,
    ) = (
        pl.pallas_call(
            pack_kernel,
            out_shape=(
                pltpu.VMEM((levels, width), f32),
                pltpu.VMEM((levels, width), bf16),
                pltpu.VMEM((levels, width), bf16),
            )
            + tuple(
                pltpu.VMEM(value.shape, value.dtype) for value in (air_temp, wind_field) + others
            ),
            in_specs=[pl.BlockSpec(memory_space=pltpu.HBM)] * (2 + len(others)),
            out_specs=tuple(whole(5 + len(others))),
            scratch_shapes=[
                pltpu.SemaphoreType.DMA((2, 2)),
                pltpu.SemaphoreType.DMA((len(others),)),
            ],
            compiler_params=params,
            name="pack",
        )(*(in_hbm(value) for value in (air_temp, wind_field) + others))
    )
    even_side, odd_side = exchange(to_even, to_odd, "cpl")

    exchange_rate, start, forward, backward, stack, remap_tiles, ocean_temp, mixing = pl.pallas_call(
        start_kernel,
        grid=(1,),
        out_shape=(
            shape_of((rows, width)),
            shape_of((slots, width)),
            shape_of((3 * width, remap_tiles.shape[0] * ocean_width), bf16),
            shape_of((3 * remap_tiles.shape[0] * ocean_width, width), bf16),
            shape_of((levels, 3 * levels), bf16),
            pltpu.VMEM(remap_tiles.shape, f32),
            pltpu.VMEM(ocean_shape, f32),
            pltpu.VMEM(mixing.shape, f32),
        ),
        in_specs=[pl.BlockSpec((2, rows, 16, width), lambda i: (0, 0, 0, 0))]
        + whole(6)
        + [pl.BlockSpec(memory_space=pltpu.HBM)] * 3
        + [pl.BlockSpec(memory_space=pl.ANY)],
        out_specs=whole(8),
        scratch_shapes=[pltpu.SemaphoreType.DMA((3,))],
        compiler_params=params,
        name="start",
    )(
        wind_here,
        shortwave,
        ocean_mask,
        owner_route,
        ocean_tile,
        weight_tile,
        physics,
        in_hbm(remap_tiles),
        in_hbm(ocean_temp),
        in_hbm(mixing),
        packed,
    )

    last_pair = rows // 2 - 1
    air_specs = [
        pl.BlockSpec((2, levels, width), lambda i: (0, 0, 0)),
        pl.BlockSpec((2, levels, width), lambda i: (last_pair, 0, 0)),
    ]

    def edge(upper, after):
        return pl.pallas_call(
            make_edge_kernel(rows, upper),
            grid=(1,),
            out_shape=(shape_of((3 * levels + 16, width), bf16), shape_of((2, levels, width))),
            in_specs=[
                air_specs[upper],
                pl.BlockSpec((2, 1, levels, width), lambda i: (0, (rows - 1) * upper, 0, 0)),
            ]
            + whole(2)
            + [pl.BlockSpec(memory_space=pl.ANY)],
            out_specs=whole(2),
            compiler_params=params,
            name="edge",
        )(air_here, wind_here, even_side, odd_side, after)

    to_high, partial_high = edge(1, start)
    below = shift(to_high, "atm", 1)
    to_low, partial_low = edge(0, partial_high)
    above = shift(to_low, "atm", -1)

    air_inner, near, bottom = pl.pallas_call(
        inner_kernel,
        out_shape=(
            pltpu.VMEM((rows, levels, width), f32),
            shape_of((4, levels, width)),
            shape_of((rows, width)),
        ),
        in_specs=whole(6),
        out_specs=tuple(whole(3)),
        scratch_shapes=[pltpu.VMEM((rows, levels, width), f32)],
        compiler_params=params,
        name="inner",
    )(air_here, wind_here, stack, packed, even_side, odd_side)

    air_edges, bottom_next, message = pl.pallas_call(
        make_outer_kernel(rows),
        grid=(1,),
        out_shape=(
            shape_of((4, levels, width)),
            shape_of((rows, width)),
            shape_of((slots, width)),
        ),
        in_specs=whole(4)
        + air_specs
        + [
            pl.BlockSpec((2, 2, levels, width), lambda i: (0, 0, 0, 0)),
            pl.BlockSpec((2, 2, levels, width), lambda i: (0, last_pair, 0, 0)),
        ]
        + whole(11),
        out_specs=whole(3),
        compiler_params=params,
        name="outer",
    )(
        above,
        below,
        partial_low,
        partial_high,
        air_here,
        air_here,
        wind_here,
        wind_here,
        packed,
        even_side,
        odd_side,
        near,
        stack,
        bottom,
        exchange_rate,
        sea_surface,
        weight_tile,
        forward,
        start,
    )

    if groups <= 4:
        turns = sorted(range(1, groups), key=lambda turn: abs(2 * turn - groups))
        gathered = [message] + [shift(message, "cpl", turn) for turn in turns]
    else:
        gathered = [message, lax.all_gather(message, "cpl")]

    air_next, base, response, total_weight = pl.pallas_call(
        settle_kernel,
        out_shape=(
            shape_of((rows, levels, width)),
            shape_of(ocean_shape),
            shape_of((ocean_shape[0], width)),
            shape_of((rows, width)),
        ),
        in_specs=whole(6),
        out_specs=tuple([pl.BlockSpec(memory_space=pltpu.HBM)] + whole(3)),
        scratch_shapes=[pltpu.SemaphoreType.DMA((3,))],
        compiler_params=params,
        name="settle",
    )(air_edges, air_inner, weight_tile, remap_tiles, ocean_temp, mixing)

    ocean_next, surface_temp = pl.pallas_call(
        make_last_kernel(len(gathered)),
        out_shape=(shape_of(ocean_shape), shape_of((rows, width))),
        in_specs=whole(len(gathered) + 7),
        out_specs=(pl.BlockSpec(memory_space=pltpu.HBM),) * 2,
        scratch_shapes=[
            pltpu.VMEM(ocean_shape, f32),
            pltpu.VMEM((rows, width), f32),
            pltpu.SemaphoreType.DMA((2,)),
        ],
        compiler_params=params,
        name="last",
    )(
        *gathered,
        base,
        response,
        total_weight,
        bottom_next,
        ocean_mask,
        weight_tile,
        backward,
    )
    return (air_next, ocean_next, surface_temp)


def solution(mesh):
    placed = (
        P("atm", None, "cpl"),
        P(None, "atm", None, "cpl"),
        P(),
        P("atm", "cpl"),
        P("atm", "cpl"),
        P("atm", "cpl"),
        P("cpl", "atm", None),
        P("cpl", "atm"),
        P("cpl", "atm"),
        P(),
        P(None, ("atm", "cpl")),
        P(),
    )
    return jax.shard_map(
        local,
        mesh=mesh,
        in_specs=placed,
        out_specs=(P("atm", None, "cpl"), P(None, ("atm", "cpl")), P("atm", "cpl")),
        check_vma=False,
    )
```

```python
import jax
import jax.numpy as jnp
from jax import lax
from jax.experimental import pallas as pl
from jax.experimental.pallas import tpu as pltpu
from jax.sharding import PartitionSpec as P

diffusion_rate = 0.05
physics_rate = 0.5
highest = lax.Precision.HIGHEST
f32 = jnp.float32
bf16 = jnp.bfloat16


def pair_even(count):
    return [(i, i ^ 1) for i in range(count)]


def pair_odd(count):
    up = [(i, (i + 1) % count) for i in range(1, count, 2)]
    return up + [(target, source) for source, target in up]


def exchange(to_even, to_odd, axis):
    count = lax.axis_size(axis)
    odd_side = lax.ppermute(to_odd, axis, pair_odd(count))
    even_side = lax.ppermute(to_even, axis, pair_even(count))
    return even_side, odd_side


def shift(block, axis, turn):
    count = lax.axis_size(axis)
    return lax.ppermute(block, axis, [(i, (i + turn) % count) for i in range(count)])


def iota(shape, dim):
    return lax.broadcasted_iota(jnp.int32, shape, dim)


def roll(value, shift):
    return pltpu.roll(value, shift % value.shape[-1], value.ndim - 1)


def pick(flag, yes, no):
    return jnp.where(flag, yes, no)


def rates(first, second):
    return (
        jnp.maximum(first, 0.0) + diffusion_rate,
        diffusion_rate - jnp.minimum(first, 0.0),
        jnp.maximum(second, 0.0) + diffusion_rate,
        diffusion_rate - jnp.minimum(second, 0.0),
    )


def split(value):
    high = value.astype(bf16)
    return high, (value - high.astype(f32)).astype(bf16)


def physics_stack(physics):
    high, low = split(physics)
    return jnp.concatenate([high, high, low], axis=1)


def column(stack, field):
    high, low = split(field)
    tendency = jnp.dot(
        stack, jnp.concatenate([high, low, high], axis=0), preferred_element_type=f32
    )
    return field + physics_rate * jnp.tanh(tendency)


def pack_kernel(
    air, wind, physics, mixing,
    packed, to_even, to_odd, air_here, wind_here, physics_here, mixing_here, sems, square_sems,
):
    rows, levels, width = air.shape
    lane = iota((levels, width), 1)
    place = lane // 4
    kind = lane % 4
    squares = [
        pltpu.make_async_copy(physics, physics_here, square_sems.at[0]),
        pltpu.make_async_copy(mixing, mixing_here, square_sems.at[1]),
    ]
    for copy in squares:
        copy.start()
    parts = sems.shape[1]
    size = rows // parts
    copies = []
    for part in range(parts):
        span = pl.ds(part * size, size)
        copies.append(
            (
                pltpu.make_async_copy(air.at[span], air_here.at[span], sems.at[0, part]),
                pltpu.make_async_copy(wind.at[:, span], wind_here.at[:, span], sems.at[1, part]),
            )
        )
        for copy in copies[-1]:
            copy.start()
    cells = jnp.zeros((levels, width), bf16)
    first = jnp.zeros((levels, width), bf16)
    second = jnp.zeros((levels, width), bf16)
    for x in range(rows):
        if x % size == 0:
            for copy in copies[x // size]:
                copy.wait()
        here = place == x
        cells = pick(here, roll(air_here[x].astype(bf16), 4 * x + 2), cells)
        first = pick(here, roll(wind_here[0, x], 4 * x + 2), first)
        second = pick(here, roll(wind_here[1, x], 4 * x + 2), second)
    cells, first, second = (value.astype(f32) for value in (cells, first, second))
    winds = pick((kind == 1) | (kind == 2), first, roll(second, 2))
    to_high = pick(kind < 2, cells, pick(kind == 2, roll(winds, 1), winds))
    to_low = pick(kind >= 2, cells, pick(kind == 0, roll(winds, -2), roll(winds, -3)))
    upper = lax.axis_index("cpl") % 2 == 0
    packed[...] = cells
    to_even[...] = pick(upper, to_high, to_low).astype(bf16)
    to_odd[...] = pick(upper, to_low, to_high).astype(bf16)
    for copy in squares:
        copy.wait()


def cpl_sides(even_side, odd_side):
    upper = lax.axis_index("cpl") % 2 == 0
    high = pick(upper, even_side[...].astype(f32), odd_side[...].astype(f32))
    low = pick(upper, odd_side[...].astype(f32), even_side[...].astype(f32))
    return low, high


def outer_cells(low, high):
    kind = iota(low.shape, 1) % 4
    return pick(kind < 2, low, high)


def swap_cells(cells):
    kind = iota(cells.shape, 1) % 4
    return pick(kind == 2, roll(cells, 1), roll(cells, -1))


def sideways(field, swapped, x):
    width = field.shape[1]
    lane = iota(field.shape, 1)
    halo = roll(swapped, -(4 * x + 2))
    south = pick(lane == 0, halo, roll(field, 1))
    north = pick(lane == width - 1, halo, roll(field, -1))
    return south, north


def advance_row(center, west, east, south, north, speeds):
    cw, ce, cs, cn = speeds
    return (
        center
        + (cw * (west - center) + ce * (east - center))
        + (cs * (south - center) + cn * (north - center))
    )


def advance_outer(own, low, high, outer, west, east):
    kind = iota(outer.shape, 1) % 4
    south = roll(pick(kind == 0, outer, own), 1)
    north = roll(pick(kind == 3, outer, own), -1)
    first = pick(kind == 1, roll(low, -1), roll(high, 2))
    second = pick(kind == 1, roll(low, -2), roll(high, 1))
    return advance_row(outer, west, east, south, north, rates(first, second))


def pack_corners(outer, x):
    levels, width = outer.shape
    place = iota((8, width), 1) // 4
    held = jnp.zeros((8, width), f32)
    for at in range(levels // 8):
        held = pick(place == at, roll(outer[8 * at : 8 * at + 8], 4 * (at - x)), held)
    return jnp.concatenate([held, jnp.zeros_like(held)], axis=0)


def unpack_corners(held, levels, x):
    return jnp.concatenate([roll(held[0:8], 4 * (x - at)) for at in range(levels // 8)], axis=0)


def make_edge_kernel(rows, upper):
    def edge_kernel(air, wind, even_side, odd_side, _, message, partial):
        low, high = cpl_sides(even_side, odd_side)
        outer = outer_cells(low, high)
        center, inner = (air[1], air[0]) if upper else (air[0], air[1])
        levels = center.shape[0]
        cw, ce, cs, cn = rates(wind[0, 0].astype(f32), wind[1, 0].astype(f32))
        inside, outside = (cw, ce) if upper else (ce, cw)
        south, north = sideways(center, swap_cells(outer), rows - 1 if upper else 0)
        known = (
            center
            + (inside * (inner - center) - outside * center)
            + (cs * (south - center) + cn * (north - center))
        )
        partial[0] = known
        partial[1] = outside
        for at, value in enumerate((center, known, outside)):
            message[at * levels : (at + 1) * levels] = value.astype(bf16)
        message[3 * levels :] = pack_corners(outer, rows - 1 if upper else 0).astype(bf16)

    return edge_kernel


def inner_kernel(
    air, wind, stack_ref, own, even_side, odd_side, ready, near, bottom, field
):
    rows, levels, width = air.shape
    low, high = cpl_sides(even_side, odd_side)
    outer = outer_cells(low, high)
    stack = stack_ref[...]
    swapped = swap_cells(outer)
    after = advance_outer(
        own[...], low, high, outer, roll(outer, 4), roll(outer, -4)
    )
    swapped_after = swap_cells(column(stack, after))

    def speeds(x):
        return rates(wind[0, x].astype(f32), wind[1, x].astype(f32))

    def step(source, halo, x):
        center = source[x]
        south, north = sideways(center, halo, x)
        return advance_row(center, source[x - 1], source[x + 1], south, north, speeds(x))

    def pair(source, halo, x):
        return column(stack, jnp.concatenate([step(source, halo, x), step(source, halo, x + 1)], axis=1))

    for x in range(1, rows - 1, 2):
        both = pair(air, swapped, x)
        field[x] = both[:, :width]
        field[x + 1] = both[:, width:]
    near[0] = field[1]
    near[1] = field[2]
    near[2] = field[rows - 3]
    near[3] = field[rows - 2]
    bottom[...] = jnp.zeros_like(bottom)
    for x in range(2, rows - 2, 2):
        both = pair(field, swapped_after, x)
        ready[x] = both[:, :width]
        ready[x + 1] = both[:, width:]
        bottom[x : x + 1] = both[0:1, :width]
        bottom[x + 1 : x + 2] = both[0:1, width:]


def as_column(row):
    size = row.shape[1]
    square = jnp.broadcast_to(row, (size, size))
    return jnp.sum(
        jnp.where(iota((size, size), 0) == iota((size, size), 1), square, 0.0),
        axis=1,
        keepdims=True,
    )


def fold(value, size):
    span = value.shape[1] // 2
    while span >= size:
        value = value + roll(value, span)
        span //= 2
    return value


def chosen_shares(fluxes, halves, bank, ocean_width):
    rows, width = fluxes.shape
    high, low = split(fluxes)
    every = jnp.dot(
        jnp.concatenate([high, low, high], axis=1), halves, preferred_element_type=f32
    )
    total = jnp.zeros((rows, width), f32)
    for at in range(0, halves.shape[1], width):
        block = (iota((rows, width), 1) + at) // ocean_width
        total = total + jnp.where(block == bank, every[:, at : at + width], 0.0)
    return fold(total, ocean_width)


def start_kernel(winds, physics, mixing, _, *refs):
    count = 8
    far, here = refs[:count], refs[count : 2 * count]
    exchange_rate, message, wanted, forward, stack, sems = refs[2 * count :]
    route, tile, mask, shortwave, bank, sea, weights, ocean = here
    copies = [
        pltpu.make_async_copy(source, target, sems.at[at])
        for at, (source, target) in enumerate(zip(far, here))
    ]
    for copy in copies:
        copy.start()
    rows, width = shortwave.shape
    banks, ocean_width, _ = weights.shape
    depth = ocean.shape[0]
    lane = iota((rows, width), 1)
    group = lax.axis_index("cpl")
    for x in range(rows):
        first = winds[0, x].astype(f32)[0:1]
        second = winds[1, x].astype(f32)[0:1]
        exchange_rate[x : x + 1] = first * first + second * second
    level = iota((depth, width), 0)
    profile = jnp.exp(level.astype(f32) / -8.0)
    profile = profile / jnp.sum(profile, axis=0, keepdims=True)
    unit = jnp.where(iota((depth, width), 1) == 0, (level == 0).astype(f32), profile)
    message[...] = jnp.full(message.shape, -1.0, f32)
    for copy in copies:
        copy.wait()
    stack[...] = physics_stack(physics[...])
    frac = mask[...].astype(f32)
    exchange_rate[...] = frac * (0.5 + 2.0 * jnp.sqrt(exchange_rate[...] + 0.01))
    target = route[...] * rows + tile[...]
    target_at = as_column(target.astype(f32))
    own_at = (group * rows + iota((rows, 1), 0)).astype(f32)
    wanted[0:rows] = jnp.broadcast_to(target_at, (rows, width))
    wanted[rows : 2 * rows] = jnp.broadcast_to(own_at, (rows, width))
    for at in (0, 2 * ocean_width):
        message[rows : rows + 1, at : at + rows] = target.astype(f32)
        message[rows : rows + 1, at + ocean_width : at + ocean_width + rows] = (
            group * rows + iota((1, rows), 1)
        ).astype(f32)
    bank_at = as_column(bank[...].astype(f32)).astype(jnp.int32)
    high, low = split(weights[...].reshape(banks * ocean_width, width).T)
    forward[...] = jnp.concatenate([high, high, low], axis=0)
    solar = chosen_shares(frac * shortwave[...], forward[...], bank_at, ocean_width)
    top = mixing[0:8]
    settled = 0.5 * ocean[0:8] + jnp.dot(
        top, ocean[...], precision=highest, preferred_element_type=f32
    )
    answer = 0.5 * unit[0:8] + jnp.dot(top, unit, precision=highest, preferred_element_type=f32)
    surface = jnp.zeros((rows, width), f32)
    for at in range(0, rows * ocean_width, width):
        spread = jnp.broadcast_to(settled[0:1, at : at + width], (rows, width))
        surface = surface + jnp.where((lane + at) // ocean_width == iota((rows, width), 0), spread, 0.0)
    surface = fold(surface, ocean_width)
    message[0:rows, :] = jnp.where(
        lane < 2 * ocean_width,
        solar,
        jnp.where(lane < 3 * ocean_width, answer[0:1, 1:2] * solar, surface),
    )
    message[rows + 1 : rows + 2, :] = jnp.broadcast_to(answer[0:1, 0:1], (1, width))


def make_outer_kernel(rows):
    def outer_kernel(
        above_ref, below_ref, partial_low, partial_high, air_low, air_high, wind_low, wind_high, own, even_side, odd_side,
        near, stack_ref, bottom, rate, sea, bank, forward, start,
        air_edges, bottom_next, message,
    ):
        width = sea.shape[1]
        ocean_width = start.shape[0]
        levels = air_low.shape[1]
        above = [above_ref[at * levels : (at + 1) * levels].astype(f32) for at in range(3)]
        below = [below_ref[at * levels : (at + 1) * levels].astype(f32) for at in range(3)]
        above.append(unpack_corners(above_ref[3 * levels :].astype(f32), levels, rows - 1))
        below.append(unpack_corners(below_ref[3 * levels :].astype(f32), levels, 0))
        low, high = cpl_sides(even_side, odd_side)
        outer = outer_cells(low, high)
        stack = stack_ref[...]
        place = iota(outer.shape, 1) // 4
        after = advance_outer(
            own[...],
            low,
            high,
            outer,
            pick(place == 0, below[3], roll(outer, 4)),
            pick(place == rows - 1, above[3], roll(outer, -4)),
        )
        moved = jnp.concatenate(
            [
                below[1] + below[2] * air_low[0],
                partial_low[0] + partial_low[1] * below[0],
                partial_high[0] + partial_high[1] * above[0],
                above[1] + above[2] * air_high[1],
                after,
            ],
            axis=1,
        )
        stepped = column(stack, moved)
        parts = [stepped[:, at * width : (at + 1) * width] for at in range(5)]
        halo = swap_cells(parts[4])
        inner = [near[at] for at in range(4)]
        bottom_next[...] = bottom[...]
        cells = []
        for center, west, east, wind, at, x in (
            (parts[1], parts[0], inner[0], wind_low, 0, 0),
            (inner[0], parts[1], inner[1], wind_low, 1, 1),
            (inner[3], inner[2], parts[2], wind_high, 0, rows - 2),
            (parts[2], inner[3], parts[3], wind_high, 1, rows - 1),
        ):
            south, north = sideways(center, halo, x)
            speeds = rates(wind[0, at].astype(f32), wind[1, at].astype(f32))
            cells.append(advance_row(center, west, east, south, north, speeds))
        final = column(stack, jnp.concatenate(cells, axis=1))
        for at, x in enumerate((0, 1, rows - 2, rows - 1)):
            row = final[:, at * width : (at + 1) * width]
            air_edges[at] = row
            bottom_next[x : x + 1] = row[0:1]
        heat = rate[...] * (bottom_next[...] - sea[...])
        bank_at = as_column(bank[...].astype(f32)).astype(jnp.int32)
        shares = chosen_shares(heat, forward[...], bank_at, ocean_width)
        message[...] = start[...]
        lane = iota((rows, width), 1)
        held = start[0:rows, :]
        message[0:rows, :] = jnp.where(
            lane < ocean_width,
            shares,
            jnp.where(
                (lane >= 2 * ocean_width) & (lane < 3 * ocean_width),
                held + start[rows + 1 : rows + 2, :] * shares,
                held,
            ),
        )

    return outer_kernel


def settle_kernel(
    edges, inner, bank, weights, ocean, mixing, out, base, response, total_weight, backward, sems
):
    rows = out.shape[0]
    middle = pl.ds(2, rows - 4)
    copies = [
        pltpu.make_async_copy(inner.at[middle], out.at[middle], sems.at[2]),
        pltpu.make_async_copy(edges.at[pl.ds(0, 2)], out.at[pl.ds(0, 2)], sems.at[0]),
        pltpu.make_async_copy(edges.at[pl.ds(2, 2)], out.at[pl.ds(rows - 2, 2)], sems.at[1]),
    ]
    for copy in copies:
        copy.start()
    width = total_weight.shape[1]
    depth = ocean.shape[0]
    banks, ocean_width, _ = weights.shape
    high, low = split(weights[...].reshape(banks * ocean_width, width))
    backward[...] = jnp.concatenate([high, high, low], axis=0)
    sums = jnp.concatenate(
        [jnp.sum(weights[at], axis=0, keepdims=True) for at in range(banks)], axis=0
    )
    bank_at = as_column(bank[...].astype(f32)).astype(jnp.int32)
    hot = (iota((rows, banks), 1) == bank_at).astype(f32)
    total_weight[...] = jnp.dot(hot, sums, precision=highest, preferred_element_type=f32)
    mixed = mixing[...]
    held = ocean[...]
    base[...] = 0.5 * held + jnp.dot(mixed, held, precision=highest, preferred_element_type=f32)
    level = iota((depth, width), 0)
    profile = jnp.exp(level.astype(f32) / -8.0)
    profile = profile / jnp.sum(profile, axis=0, keepdims=True)
    part = iota((depth, width), 1)
    unit = jnp.where(part == 0, (level == 0).astype(f32), jnp.where(part == 1, profile, 0.0))
    response[...] = 0.5 * unit + jnp.dot(mixed, unit, precision=highest, preferred_element_type=f32)
    for copy in copies:
        copy.wait()


def make_last_kernel(count):
    def last_kernel(*refs):
        messages, (wanted, base, response, total_weight, bottom, mask, bank, backward, ocean_next, surface, ocean_here, surface_here, sems) = (
            refs[:count],
            refs[count:],
        )
        own = messages[0][...]
        if len(messages) == 2 and len(messages[1].shape) == 3:
            blocks = [messages[1][at] for at in range(messages[1].shape[0])]
        else:
            blocks = [ref[...] for ref in messages]
        rows, width = bottom.shape
        slots = own.shape[0]
        ocean_width = slots
        cells = backward.shape[0] // 3
        lane = iota((slots, width), 1)
        labels = []
        values = []
        for block in blocks:
            labels.append(block[rows : rows + 1, :])
            values.append(jnp.where(lane < 3 * ocean_width, block, 0.0))
            values.append(jnp.where(lane < 3 * ocean_width, 0.0, block))
        left = iota((1, width), 1) < 2 * ocean_width
        hot = [
            (wanted[...] == jnp.where(left, labels[at], labels[at + 1])).astype(f32).astype(bf16)
            for at in range(0, len(labels), 2)
        ]
        high, low = split(jnp.concatenate(values, axis=0))
        got = jnp.dot(
            jnp.concatenate(hot + hot, axis=1),
            jnp.concatenate([high, low], axis=0),
            preferred_element_type=f32,
        )
        near = iota((rows, width), 1)
        seen = fold(jnp.where(near >= 2 * ocean_width, got[0:rows], 0.0), ocean_width)
        bank_at = as_column(bank[...].astype(f32)).astype(jnp.int32)
        high, low = split(
            jnp.concatenate(
                [
                    jnp.where((near + at) // ocean_width == bank_at, seen, 0.0)
                    for at in range(0, cells, width)
                ],
                axis=1,
            )
        )
        weighted = jnp.dot(
            jnp.concatenate([high, low, high], axis=1), backward[...], preferred_element_type=f32
        )
        forcing = got[rows : 2 * rows]
        heat = fold(jnp.where(near < ocean_width, forcing, 0.0), ocean_width)
        solar = fold(
            jnp.where((near >= ocean_width) & (near < 2 * ocean_width), forcing, 0.0), ocean_width
        )
        first = response[:, 0:1]
        second = response[:, 1:2]
        for at in range(0, base.shape[1], width):
            mine = (near + at) // ocean_width == iota((rows, width), 0)
            heat_row = jnp.sum(jnp.where(mine, heat, 0.0), axis=0, keepdims=True)
            solar_row = jnp.sum(jnp.where(mine, solar, 0.0), axis=0, keepdims=True)
            ocean_here[:, at : at + width] = base[:, at : at + width] + (
                first * heat_row + second * solar_row
            )
        ocean_out = pltpu.make_async_copy(ocean_here, ocean_next, sems.at[0])
        ocean_out.start()
        frac = mask[...].astype(f32)
        surface_here[...] = frac * (weighted / total_weight[...]) + (1.0 - frac) * bottom[...]
        surface_out = pltpu.make_async_copy(surface_here, surface, sems.at[1])
        surface_out.start()
        ocean_out.wait()
        surface_out.wait()

    return last_kernel


def shape_of(shape, dtype=f32):
    return jax.ShapeDtypeStruct(shape, dtype)


def whole(count):
    return [pl.BlockSpec(memory_space=pltpu.VMEM) for _ in range(count)]


def in_hbm(value):
    return pltpu.with_memory_space_constraint(value, pltpu.HBM)


params = pltpu.CompilerParams(vmem_limit_bytes=48 * 1024 * 1024)


def local(
    air_temp,
    wind_field,
    physics,
    sea_surface,
    shortwave,
    ocean_mask,
    owner_route,
    ocean_tile,
    weight_tile,
    remap_tiles,
    ocean_temp,
    mixing,
):
    rows, levels, width = air_temp.shape
    groups = lax.axis_size("cpl")
    ocean_width = remap_tiles.shape[1]
    slots = ocean_width
    ocean_shape = ocean_temp.shape

    packed, to_even, to_odd, air_here, wind_here, physics, mixing = pl.pallas_call(
        pack_kernel,
        out_shape=(
            pltpu.VMEM((levels, width), f32),
            pltpu.VMEM((levels, width), bf16),
            pltpu.VMEM((levels, width), bf16),
            pltpu.VMEM(air_temp.shape, f32),
            pltpu.VMEM(wind_field.shape, bf16),
            pltpu.VMEM(physics.shape, f32),
            pltpu.VMEM(mixing.shape, f32),
        ),
        in_specs=[pl.BlockSpec(memory_space=pltpu.HBM)] * 4,
        out_specs=tuple(whole(7)),
        scratch_shapes=[pltpu.SemaphoreType.DMA((2, 2)), pltpu.SemaphoreType.DMA((2,))],
        compiler_params=params,
        name="pack",
    )(*(in_hbm(value) for value in (air_temp, wind_field, physics, mixing)))
    even_side, odd_side = exchange(to_even, to_odd, "cpl")

    far = (
        owner_route.reshape(1, rows),
        ocean_tile,
        ocean_mask,
        shortwave,
        weight_tile,
        sea_surface,
        remap_tiles,
        ocean_temp,
    )
    (
        _,
        _,
        ocean_mask,
        shortwave,
        weight_tile,
        sea_surface,
        remap_tiles,
        ocean_temp,
        exchange_rate,
        start,
        wanted,
        forward,
        stack,
    ) = pl.pallas_call(
        start_kernel,
        grid=(1,),
        out_shape=tuple(pltpu.VMEM(value.shape, value.dtype) for value in far)
        + (
            shape_of((rows, width)),
            shape_of((slots, width)),
            shape_of((2 * rows, width)),
            shape_of((3 * width, remap_tiles.shape[0] * ocean_width), bf16),
            shape_of((levels, 3 * levels), bf16),
        ),
        in_specs=[
            pl.BlockSpec((2, rows, 16, width), lambda i: (0, 0, 0, 0)),
            *whole(2),
            pl.BlockSpec(memory_space=pl.ANY),
        ]
        + [pl.BlockSpec(memory_space=pltpu.HBM)] * len(far),
        out_specs=whole(len(far) + 5),
        scratch_shapes=[pltpu.SemaphoreType.DMA((len(far),))],
        compiler_params=params,
        name="start",
    )(wind_here, physics, mixing, packed, *(in_hbm(value) for value in far))

    last_pair = rows // 2 - 1
    air_specs = [
        pl.BlockSpec((2, levels, width), lambda i: (0, 0, 0)),
        pl.BlockSpec((2, levels, width), lambda i: (last_pair, 0, 0)),
    ]

    def edge(upper, after):
        return pl.pallas_call(
            make_edge_kernel(rows, upper),
            grid=(1,),
            out_shape=(shape_of((3 * levels + 16, width), bf16), shape_of((2, levels, width))),
            in_specs=[
                air_specs[upper],
                pl.BlockSpec((2, 1, levels, width), lambda i: (0, (rows - 1) * upper, 0, 0)),
            ]
            + whole(2)
            + [pl.BlockSpec(memory_space=pl.ANY)],
            out_specs=whole(2),
            compiler_params=params,
            name="edge",
        )(air_here, wind_here, even_side, odd_side, after)

    to_high, partial_high = edge(1, start)
    below = shift(to_high, "atm", 1)
    to_low, partial_low = edge(0, partial_high)
    above = shift(to_low, "atm", -1)

    air_inner, near, bottom = pl.pallas_call(
        inner_kernel,
        out_shape=(
            pltpu.VMEM((rows, levels, width), f32),
            shape_of((4, levels, width)),
            shape_of((rows, width)),
        ),
        in_specs=whole(6),
        out_specs=tuple(whole(3)),
        scratch_shapes=[pltpu.VMEM((rows, levels, width), f32)],
        compiler_params=params,
        name="inner",
    )(air_here, wind_here, stack, packed, even_side, odd_side)

    air_edges, bottom_next, message = pl.pallas_call(
        make_outer_kernel(rows),
        grid=(1,),
        out_shape=(
            shape_of((4, levels, width)),
            shape_of((rows, width)),
            shape_of((slots, width)),
        ),
        in_specs=whole(4)
        + air_specs
        + [
            pl.BlockSpec((2, 2, levels, width), lambda i: (0, 0, 0, 0)),
            pl.BlockSpec((2, 2, levels, width), lambda i: (0, last_pair, 0, 0)),
        ]
        + whole(11),
        out_specs=whole(3),
        compiler_params=params,
        name="outer",
    )(
        above,
        below,
        partial_low,
        partial_high,
        air_here,
        air_here,
        wind_here,
        wind_here,
        packed,
        even_side,
        odd_side,
        near,
        stack,
        bottom,
        exchange_rate,
        sea_surface,
        weight_tile,
        forward,
        start,
    )

    if groups <= 4:
        turns = sorted(range(1, groups), key=lambda turn: abs(2 * turn - groups))
        gathered = [message] + [shift(message, "cpl", turn) for turn in turns]
    else:
        gathered = [message, lax.all_gather(message, "cpl")]

    air_next, base, response, total_weight, backward = pl.pallas_call(
        settle_kernel,
        out_shape=(
            shape_of((rows, levels, width)),
            shape_of(ocean_shape),
            shape_of((ocean_shape[0], width)),
            shape_of((rows, width)),
            shape_of((3 * remap_tiles.shape[0] * ocean_width, width), bf16),
        ),
        in_specs=whole(6),
        out_specs=tuple([pl.BlockSpec(memory_space=pltpu.HBM)] + whole(4)),
        scratch_shapes=[pltpu.SemaphoreType.DMA((3,))],
        compiler_params=params,
        name="settle",
    )(air_edges, air_inner, weight_tile, remap_tiles, ocean_temp, mixing)

    ocean_next, surface_temp = pl.pallas_call(
        make_last_kernel(len(gathered)),
        out_shape=(shape_of(ocean_shape), shape_of((rows, width))),
        in_specs=whole(len(gathered) + 8),
        out_specs=(pl.BlockSpec(memory_space=pltpu.HBM),) * 2,
        scratch_shapes=[
            pltpu.VMEM(ocean_shape, f32),
            pltpu.VMEM((rows, width), f32),
            pltpu.SemaphoreType.DMA((2,)),
        ],
        compiler_params=params,
        name="last",
    )(
        *gathered,
        wanted,
        base,
        response,
        total_weight,
        bottom_next,
        ocean_mask,
        weight_tile,
        backward,
    )
    return (air_next, ocean_next, surface_temp)


def solution(mesh):
    placed = (
        P("atm", None, "cpl"),
        P(None, "atm", None, "cpl"),
        P(),
        P("atm", "cpl"),
        P("atm", "cpl"),
        P("atm", "cpl"),
        P("cpl", "atm", None),
        P("cpl", "atm"),
        P("cpl", "atm"),
        P(),
        P(None, ("atm", "cpl")),
        P(),
    )
    return jax.shard_map(
        local,
        mesh=mesh,
        in_specs=placed,
        out_specs=(P("atm", None, "cpl"), P(None, ("atm", "cpl")), P("atm", "cpl")),
        check_vma=False,
    )
```

```python
import jax
import jax.numpy as jnp
from jax import lax
from jax.experimental import pallas as pl
from jax.experimental.pallas import tpu as pltpu
from jax.sharding import PartitionSpec as P

diffusion_rate = 0.05
physics_rate = 0.5
highest = lax.Precision.HIGHEST
f32 = jnp.float32
bf16 = jnp.bfloat16


def pair_even(count):
    return [(i, i ^ 1) for i in range(count)]


def pair_odd(count):
    up = [(i, (i + 1) % count) for i in range(1, count, 2)]
    return up + [(target, source) for source, target in up]


def exchange(to_even, to_odd, axis):
    count = lax.axis_size(axis)
    odd_side = lax.ppermute(to_odd, axis, pair_odd(count))
    even_side = lax.ppermute(to_even, axis, pair_even(count))
    return even_side, odd_side


def shift(block, axis, turn):
    count = lax.axis_size(axis)
    return lax.ppermute(block, axis, [(i, (i + turn) % count) for i in range(count)])


def iota(shape, dim):
    return lax.broadcasted_iota(jnp.int32, shape, dim)


def roll(value, shift):
    return pltpu.roll(value, shift % value.shape[-1], value.ndim - 1)


def pick(flag, yes, no):
    return jnp.where(flag, yes, no)


def rates(first, second):
    return (
        jnp.maximum(first, 0.0) + diffusion_rate,
        diffusion_rate - jnp.minimum(first, 0.0),
        jnp.maximum(second, 0.0) + diffusion_rate,
        diffusion_rate - jnp.minimum(second, 0.0),
    )


def split(value):
    high = value.astype(bf16)
    return high, (value - high.astype(f32)).astype(bf16)


def physics_stack(physics):
    high, low = split(physics)
    return jnp.concatenate([high, high, low], axis=1)


def column(stack, field):
    high, low = split(field)
    tendency = jnp.dot(
        stack, jnp.concatenate([high, low, high], axis=0), preferred_element_type=f32
    )
    return field + physics_rate * jnp.tanh(tendency)


def pack_kernel(
    air, wind, physics, mixing,
    packed, to_even, to_odd, air_here, wind_here, physics_here, mixing_here, sems, square_sems,
):
    rows, levels, width = air.shape
    lane = iota((levels, width), 1)
    place = lane // 4
    kind = lane % 4
    squares = [
        pltpu.make_async_copy(physics, physics_here, square_sems.at[0]),
        pltpu.make_async_copy(mixing, mixing_here, square_sems.at[1]),
    ]
    for copy in squares:
        copy.start()
    parts = sems.shape[1]
    size = rows // parts
    copies = []
    for part in range(parts):
        span = pl.ds(part * size, size)
        copies.append(
            (
                pltpu.make_async_copy(air.at[span], air_here.at[span], sems.at[0, part]),
                pltpu.make_async_copy(wind.at[:, span], wind_here.at[:, span], sems.at[1, part]),
            )
        )
        for copy in copies[-1]:
            copy.start()
    cells = jnp.zeros((levels, width), bf16)
    first = jnp.zeros((levels, width), bf16)
    second = jnp.zeros((levels, width), bf16)
    for x in range(rows):
        if x % size == 0:
            for copy in copies[x // size]:
                copy.wait()
        here = place == x
        cells = pick(here, roll(air_here[x].astype(bf16), 4 * x + 2), cells)
        first = pick(here, roll(wind_here[0, x], 4 * x + 2), first)
        second = pick(here, roll(wind_here[1, x], 4 * x + 2), second)
    to_high = pick(kind < 2, cells, pick(kind == 2, roll(first, 1), roll(second, 2)))
    to_low = pick(kind >= 2, cells, pick(kind == 0, roll(first, -2), roll(second, -1)))
    upper = lax.axis_index("cpl") % 2 == 0
    packed[...] = cells.astype(f32)
    to_even[...] = pick(upper, to_high, to_low)
    to_odd[...] = pick(upper, to_low, to_high)
    for copy in squares:
        copy.wait()


def cpl_sides(even_side, odd_side):
    upper = lax.axis_index("cpl") % 2 == 0
    high = pick(upper, even_side[...].astype(f32), odd_side[...].astype(f32))
    low = pick(upper, odd_side[...].astype(f32), even_side[...].astype(f32))
    return low, high


def outer_cells(low, high):
    kind = iota(low.shape, 1) % 4
    return pick(kind < 2, low, high)


def swap_cells(cells):
    kind = iota(cells.shape, 1) % 4
    return pick(kind == 2, roll(cells, 1), roll(cells, -1))


def sideways(field, swapped, x):
    width = field.shape[1]
    lane = iota(field.shape, 1)
    halo = roll(swapped, -(4 * x + 2))
    south = pick(lane == 0, halo, roll(field, 1))
    north = pick(lane == width - 1, halo, roll(field, -1))
    return south, north


def sideways_of(field, cells, x):
    width = field.shape[1]
    lane = iota(field.shape, 1)
    south = pick(lane == 0, roll(cells, -(4 * x + 1)), roll(field, 1))
    north = pick(lane == width - 1, roll(cells, -(4 * x + 3)), roll(field, -1))
    return south, north


def advance_row(center, west, east, south, north, speeds):
    cw, ce, cs, cn = speeds
    return (
        center
        + (cw * (west - center) + ce * (east - center))
        + (cs * (south - center) + cn * (north - center))
    )


def advance_outer(own, low, high, outer, west, east):
    kind = iota(outer.shape, 1) % 4
    south = roll(pick(kind == 0, outer, own), 1)
    north = roll(pick(kind == 3, outer, own), -1)
    first = pick(kind == 1, roll(low, -1), roll(high, 2))
    second = pick(kind == 1, roll(low, -2), roll(high, 1))
    return advance_row(outer, west, east, south, north, rates(first, second))


def pack_corners(outer, x):
    levels, width = outer.shape
    place = iota((8, width), 1) // 4
    held = jnp.zeros((8, width), f32)
    for at in range(levels // 8):
        held = pick(place == at, roll(outer[8 * at : 8 * at + 8], 4 * (at - x)), held)
    return jnp.concatenate([held, jnp.zeros_like(held)], axis=0)


def unpack_corners(held, levels, x):
    return jnp.concatenate([roll(held[0:8], 4 * (x - at)) for at in range(levels // 8)], axis=0)


def make_edge_kernel(rows, upper):
    def edge_kernel(air, wind, even_side, odd_side, _, message, partial):
        low, high = cpl_sides(even_side, odd_side)
        outer = outer_cells(low, high)
        at, beside = (rows - 1, rows - 2) if upper else (0, 1)
        center, inner = air[at], air[beside]
        levels = center.shape[0]
        cw, ce, cs, cn = rates(wind[0, at].astype(f32), wind[1, at].astype(f32))
        inside, outside = (cw, ce) if upper else (ce, cw)
        south, north = sideways_of(center, outer, rows - 1 if upper else 0)
        known = (
            center
            + (inside * (inner - center) - outside * center)
            + (cs * (south - center) + cn * (north - center))
        )
        partial[0] = known
        partial[1] = outside
        for part, value in enumerate((center, known, outside)):
            message[part * levels : (part + 1) * levels] = value.astype(bf16)
        message[3 * levels :] = pack_corners(outer, rows - 1 if upper else 0).astype(bf16)

    return edge_kernel


def inner_kernel(
    air, wind, stack_ref, own, even_side, odd_side, ready, near, bottom, field
):
    rows, levels, width = air.shape
    low, high = cpl_sides(even_side, odd_side)
    outer = outer_cells(low, high)
    stack = stack_ref[...]
    swapped = swap_cells(outer)
    after = advance_outer(
        own[...], low, high, outer, roll(outer, 4), roll(outer, -4)
    )
    swapped_after = swap_cells(column(stack, after))

    def speeds(x):
        return rates(wind[0, x].astype(f32), wind[1, x].astype(f32))

    def step(source, halo, x):
        center = source[x]
        south, north = sideways(center, halo, x)
        return advance_row(center, source[x - 1], source[x + 1], south, north, speeds(x))

    def pair(source, halo, x):
        return column(stack, jnp.concatenate([step(source, halo, x), step(source, halo, x + 1)], axis=1))

    for x in range(1, rows - 1, 2):
        both = pair(air, swapped, x)
        field[x] = both[:, :width]
        field[x + 1] = both[:, width:]
    near[0] = field[1]
    near[1] = field[2]
    near[2] = field[rows - 3]
    near[3] = field[rows - 2]
    bottom[...] = jnp.zeros_like(bottom)
    for x in range(2, rows - 2, 2):
        both = pair(field, swapped_after, x)
        ready[x] = both[:, :width]
        ready[x + 1] = both[:, width:]
        bottom[x : x + 1] = both[0:1, :width]
        bottom[x + 1 : x + 2] = both[0:1, width:]


def as_column(row):
    size = row.shape[1]
    square = jnp.broadcast_to(row, (size, size))
    return jnp.sum(
        jnp.where(iota((size, size), 0) == iota((size, size), 1), square, 0.0),
        axis=1,
        keepdims=True,
    )


def fold(value, size):
    span = value.shape[1] // 2
    while span >= size:
        value = value + roll(value, span)
        span //= 2
    return value


def chosen_shares(fluxes, halves, bank, ocean_width):
    rows, width = fluxes[0].shape
    high, low = split(jnp.concatenate(fluxes, axis=0))
    every = jnp.dot(
        jnp.concatenate([high, low, high], axis=1), halves, preferred_element_type=f32
    )
    shares = []
    for part in range(len(fluxes)):
        total = jnp.zeros((rows, width), f32)
        for at in range(0, halves.shape[1], width):
            block = (iota((rows, width), 1) + at) // ocean_width
            mine = every[part * rows : (part + 1) * rows, at : at + width]
            total = total + jnp.where(block == bank, mine, 0.0)
        shares.append(fold(total, ocean_width))
    return shares


def start_kernel(winds, physics, mixing, _, *refs):
    count = 8
    far = refs[:count]
    mask, sea, weights, ocean, exchange_rate, sun, bank_near, message, wanted, forward, stack = refs[
        count : count + 11
    ]
    route, tile, shortwave, bank, sems = refs[count + 11 :]
    here = (route, tile, shortwave, bank, mask, sea, weights, ocean)
    copies = [
        pltpu.make_async_copy(source, target, sems.at[at])
        for at, (source, target) in enumerate(zip(far, here))
    ]
    for copy in copies:
        copy.start()
    rows, width = shortwave.shape
    banks, ocean_width, _ = weights.shape
    depth = ocean.shape[0]
    lane = iota((rows, width), 1)
    group = lax.axis_index("cpl")
    for x in range(rows):
        first = winds[0, x, 0:16].astype(f32)[0:1]
        second = winds[1, x, 0:16].astype(f32)[0:1]
        exchange_rate[x : x + 1] = first * first + second * second
    level = iota((depth, width), 0)
    profile = jnp.exp(level.astype(f32) / -8.0)
    profile = profile / jnp.sum(profile, axis=0, keepdims=True)
    unit = jnp.where(iota((depth, width), 1) == 0, (level == 0).astype(f32), profile)
    message[...] = jnp.full(message.shape, -1.0, f32)
    for copy in copies:
        copy.wait()
    stack[...] = physics_stack(physics[...])
    frac = mask[...].astype(f32)
    exchange_rate[...] = frac * (0.5 + 2.0 * jnp.sqrt(exchange_rate[...] + 0.01))
    target = route[...] * rows + tile[...]
    target_at = as_column(target.astype(f32))
    own_at = (group * rows + iota((rows, 1), 0)).astype(f32)
    wanted[0:rows] = jnp.broadcast_to(target_at, (rows, width))
    wanted[rows : 2 * rows] = jnp.broadcast_to(own_at, (rows, width))
    for at in (0, 2 * ocean_width):
        message[rows : rows + 1, at : at + rows] = target.astype(f32)
        message[rows : rows + 1, at + ocean_width : at + ocean_width + rows] = (
            group * rows + iota((1, rows), 1)
        ).astype(f32)
    bank_at = as_column(bank[...].astype(f32)).astype(jnp.int32)
    high, low = split(weights[...].reshape(banks * ocean_width, width).T)
    forward[...] = jnp.concatenate([high, high, low], axis=0)
    sun[...] = frac * shortwave[...]
    bank_near[...] = jnp.broadcast_to(bank_at, (rows, width))
    top = mixing[0:8]
    settled = 0.5 * ocean[0:8] + jnp.dot(
        top, ocean[...], precision=highest, preferred_element_type=f32
    )
    answer = 0.5 * unit[0:8] + jnp.dot(top, unit, precision=highest, preferred_element_type=f32)
    surface = jnp.zeros((rows, width), f32)
    for at in range(0, rows * ocean_width, width):
        spread = jnp.broadcast_to(settled[0:1, at : at + width], (rows, width))
        surface = surface + jnp.where((lane + at) // ocean_width == iota((rows, width), 0), spread, 0.0)
    surface = fold(surface, ocean_width)
    message[0:rows, :] = surface
    message[rows + 1 : rows + 2, :] = jnp.broadcast_to(answer[0:1, 0:1], (1, width))
    message[rows + 2 : rows + 3, :] = jnp.broadcast_to(answer[0:1, 1:2], (1, width))


def make_outer_kernel(rows):
    def outer_kernel(
        above_ref, below_ref, partial_low, partial_high, air, wind, own, even_side, odd_side,
        near, stack_ref, bottom, rate, sun, sea, bank, forward, start,
        air_edges, bottom_next, message,
    ):
        width = sea.shape[1]
        ocean_width = start.shape[0]
        levels = air.shape[1]
        above = [above_ref[at * levels : (at + 1) * levels].astype(f32) for at in range(3)]
        below = [below_ref[at * levels : (at + 1) * levels].astype(f32) for at in range(3)]
        above.append(unpack_corners(above_ref[3 * levels :].astype(f32), levels, rows - 1))
        below.append(unpack_corners(below_ref[3 * levels :].astype(f32), levels, 0))
        low, high = cpl_sides(even_side, odd_side)
        outer = outer_cells(low, high)
        stack = stack_ref[...]
        place = iota(outer.shape, 1) // 4
        after = advance_outer(
            own[...],
            low,
            high,
            outer,
            pick(place == 0, below[3], roll(outer, 4)),
            pick(place == rows - 1, above[3], roll(outer, -4)),
        )
        moved = jnp.concatenate(
            [
                below[1] + below[2] * air[0],
                partial_low[0] + partial_low[1] * below[0],
                partial_high[0] + partial_high[1] * above[0],
                above[1] + above[2] * air[rows - 1],
                after,
            ],
            axis=1,
        )
        stepped = column(stack, moved)
        parts = [stepped[:, at * width : (at + 1) * width] for at in range(5)]
        inner = [near[at] for at in range(4)]
        bottom_next[...] = bottom[...]
        cells = []
        for center, west, east, x in (
            (parts[1], parts[0], inner[0], 0),
            (inner[0], parts[1], inner[1], 1),
            (inner[3], inner[2], parts[2], rows - 2),
            (parts[2], inner[3], parts[3], rows - 1),
        ):
            south, north = sideways_of(center, parts[4], x)
            speeds = rates(wind[0, x].astype(f32), wind[1, x].astype(f32))
            cells.append(advance_row(center, west, east, south, north, speeds))
        final = column(stack, jnp.concatenate(cells, axis=1))
        for at, x in enumerate((0, 1, rows - 2, rows - 1)):
            row = final[:, at * width : (at + 1) * width]
            air_edges[at] = row
            bottom_next[x : x + 1] = row[0:1]
        heat = rate[...] * (bottom_next[...] - sea[...])
        shares, solar = chosen_shares(
            [heat, sun[...]], forward[...], bank[...], ocean_width
        )
        message[...] = start[...]
        block = iota((rows, width), 1) // ocean_width
        raised = start[rows + 1 : rows + 2, :] * shares + start[rows + 2 : rows + 3, :] * solar
        message[0:rows, :] = jnp.where(
            block == 0,
            shares,
            jnp.where(block == 1, solar, jnp.where(block == 2, raised, start[0:rows, :])),
        )

    return outer_kernel


def settle_kernel(
    edges, inner, bank, weights, ocean, mixing, out, base, response, total_weight, backward, sems
):
    rows = out.shape[0]
    middle = pl.ds(2, rows - 4)
    copies = [
        pltpu.make_async_copy(inner.at[middle], out.at[middle], sems.at[2]),
        pltpu.make_async_copy(edges.at[pl.ds(0, 2)], out.at[pl.ds(0, 2)], sems.at[0]),
        pltpu.make_async_copy(edges.at[pl.ds(2, 2)], out.at[pl.ds(rows - 2, 2)], sems.at[1]),
    ]
    for copy in copies:
        copy.start()
    width = total_weight.shape[1]
    depth = ocean.shape[0]
    banks, ocean_width, _ = weights.shape
    high, low = split(weights[...].reshape(banks * ocean_width, width))
    backward[...] = jnp.concatenate([high, high, low], axis=0)
    sums = jnp.concatenate(
        [jnp.sum(weights[at], axis=0, keepdims=True) for at in range(banks)], axis=0
    )
    hot = (iota((rows, banks), 1) == bank[:, 0:banks]).astype(f32)
    total_weight[...] = jnp.dot(hot, sums, precision=highest, preferred_element_type=f32)
    mixed = mixing[...]
    held = ocean[...]
    base[...] = 0.5 * held + jnp.dot(mixed, held, precision=highest, preferred_element_type=f32)
    level = iota((depth, width), 0)
    profile = jnp.exp(level.astype(f32) / -8.0)
    profile = profile / jnp.sum(profile, axis=0, keepdims=True)
    part = iota((depth, width), 1)
    unit = jnp.where(part == 0, (level == 0).astype(f32), jnp.where(part == 1, profile, 0.0))
    response[...] = 0.5 * unit + jnp.dot(mixed, unit, precision=highest, preferred_element_type=f32)
    for copy in copies:
        copy.wait()


def make_last_kernel(count):
    def last_kernel(*refs):
        messages, (wanted, base, response, total_weight, bottom, mask, bank, backward, ocean_next, surface, ocean_here, surface_here, sems) = (
            refs[:count],
            refs[count:],
        )
        own = messages[0][...]
        if len(messages) == 2 and len(messages[1].shape) == 3:
            blocks = [messages[1][at] for at in range(messages[1].shape[0])]
        else:
            blocks = [ref[...] for ref in messages]
        rows, width = bottom.shape
        slots = own.shape[0]
        ocean_width = slots
        cells = backward.shape[0] // 3
        lane = iota((slots, width), 1)
        labels = []
        values = []
        for block in blocks:
            labels.append(block[rows : rows + 1, :])
            values.append(jnp.where(lane < 3 * ocean_width, block, 0.0))
            values.append(jnp.where(lane < 3 * ocean_width, 0.0, block))
        left = iota((1, width), 1) < 2 * ocean_width
        hot = [
            (wanted[...] == jnp.where(left, labels[at], labels[at + 1])).astype(f32).astype(bf16)
            for at in range(0, len(labels), 2)
        ]
        high, low = split(jnp.concatenate(values, axis=0))
        got = jnp.dot(
            jnp.concatenate(hot + hot, axis=1),
            jnp.concatenate([high, low], axis=0),
            preferred_element_type=f32,
        )
        near = iota((rows, width), 1)
        seen = fold(jnp.where(near >= 2 * ocean_width, got[0:rows], 0.0), ocean_width)
        bank_at = bank[...]
        high, low = split(
            jnp.concatenate(
                [
                    jnp.where((near + at) // ocean_width == bank_at, seen, 0.0)
                    for at in range(0, cells, width)
                ],
                axis=1,
            )
        )
        weighted = jnp.dot(
            jnp.concatenate([high, low, high], axis=1), backward[...], preferred_element_type=f32
        )
        forcing = got[rows : 2 * rows]
        heat = fold(jnp.where(near < ocean_width, forcing, 0.0), ocean_width)
        solar = fold(
            jnp.where((near >= ocean_width) & (near < 2 * ocean_width), forcing, 0.0), ocean_width
        )
        first = response[:, 0:1]
        second = response[:, 1:2]
        for at in range(0, base.shape[1], width):
            mine = (near + at) // ocean_width == iota((rows, width), 0)
            heat_row = jnp.sum(jnp.where(mine, heat, 0.0), axis=0, keepdims=True)
            solar_row = jnp.sum(jnp.where(mine, solar, 0.0), axis=0, keepdims=True)
            ocean_here[:, at : at + width] = base[:, at : at + width] + (
                first * heat_row + second * solar_row
            )
        ocean_out = pltpu.make_async_copy(ocean_here, ocean_next, sems.at[0])
        ocean_out.start()
        frac = mask[...].astype(f32)
        surface_here[...] = frac * (weighted / total_weight[...]) + (1.0 - frac) * bottom[...]
        surface_out = pltpu.make_async_copy(surface_here, surface, sems.at[1])
        surface_out.start()
        ocean_out.wait()
        surface_out.wait()

    return last_kernel


def shape_of(shape, dtype=f32):
    return jax.ShapeDtypeStruct(shape, dtype)


def whole(count):
    return [pl.BlockSpec(memory_space=pltpu.VMEM) for _ in range(count)]


def in_hbm(value):
    return pltpu.with_memory_space_constraint(value, pltpu.HBM)


params = pltpu.CompilerParams(vmem_limit_bytes=48 * 1024 * 1024)


def local(
    air_temp,
    wind_field,
    physics,
    sea_surface,
    shortwave,
    ocean_mask,
    owner_route,
    ocean_tile,
    weight_tile,
    remap_tiles,
    ocean_temp,
    mixing,
):
    rows, levels, width = air_temp.shape
    groups = lax.axis_size("cpl")
    ocean_width = remap_tiles.shape[1]
    slots = ocean_width
    ocean_shape = ocean_temp.shape

    packed, to_even, to_odd, air_here, wind_here, physics, mixing = pl.pallas_call(
        pack_kernel,
        out_shape=(
            pltpu.VMEM((levels, width), f32),
            pltpu.VMEM((levels, width), bf16),
            pltpu.VMEM((levels, width), bf16),
            pltpu.VMEM(air_temp.shape, f32),
            pltpu.VMEM(wind_field.shape, bf16),
            pltpu.VMEM(physics.shape, f32),
            pltpu.VMEM(mixing.shape, f32),
        ),
        in_specs=[pl.BlockSpec(memory_space=pltpu.HBM)] * 4,
        out_specs=tuple(whole(7)),
        scratch_shapes=[pltpu.SemaphoreType.DMA((2, 3)), pltpu.SemaphoreType.DMA((2,))],
        compiler_params=params,
        name="pack",
    )(*(in_hbm(value) for value in (air_temp, wind_field, physics, mixing)))
    even_side, odd_side = exchange(to_even, to_odd, "cpl")

    kept = (ocean_mask, sea_surface, remap_tiles, ocean_temp)
    passing = (owner_route.reshape(1, rows), ocean_tile, shortwave, weight_tile)
    (
        ocean_mask,
        sea_surface,
        remap_tiles,
        ocean_temp,
        exchange_rate,
        sun,
        bank_near,
        start,
        wanted,
        forward,
        stack,
    ) = pl.pallas_call(
        start_kernel,
        out_shape=tuple(pltpu.VMEM(value.shape, value.dtype) for value in kept)
        + (
            shape_of((rows, width)),
            shape_of((rows, width)),
            shape_of((rows, width), jnp.int32),
            shape_of((slots, width)),
            shape_of((2 * rows, width)),
            shape_of((3 * width, remap_tiles.shape[0] * ocean_width), bf16),
            shape_of((levels, 3 * levels), bf16),
        ),
        in_specs=whole(3)
        + [pl.BlockSpec(memory_space=pl.ANY)]
        + [pl.BlockSpec(memory_space=pltpu.HBM)] * len(passing + kept),
        out_specs=tuple(whole(len(kept) + 7)),
        scratch_shapes=[pltpu.VMEM(value.shape, value.dtype) for value in passing]
        + [pltpu.SemaphoreType.DMA((len(passing + kept),))],
        compiler_params=params,
        name="start",
    )(wind_here, physics, mixing, packed, *(in_hbm(value) for value in passing + kept))

    def edge(upper, after):
        return pl.pallas_call(
            make_edge_kernel(rows, upper),
            out_shape=(shape_of((3 * levels + 16, width), bf16), shape_of((2, levels, width))),
            in_specs=whole(4) + [pl.BlockSpec(memory_space=pl.ANY)],
            out_specs=tuple(whole(2)),
            compiler_params=params,
            name="edge",
        )(air_here, wind_here, even_side, odd_side, after)

    to_high, partial_high = edge(1, start)
    below = shift(to_high, "atm", 1)
    to_low, partial_low = edge(0, partial_high)
    above = shift(to_low, "atm", -1)

    air_inner, near, bottom = pl.pallas_call(
        inner_kernel,
        out_shape=(
            pltpu.VMEM((rows, levels, width), f32),
            shape_of((4, levels, width)),
            shape_of((rows, width)),
        ),
        in_specs=whole(6),
        out_specs=tuple(whole(3)),
        scratch_shapes=[pltpu.VMEM((rows, levels, width), f32)],
        compiler_params=params,
        name="inner",
    )(air_here, wind_here, stack, packed, even_side, odd_side)

    air_edges, bottom_next, message = pl.pallas_call(
        make_outer_kernel(rows),
        out_shape=(
            shape_of((4, levels, width)),
            shape_of((rows, width)),
            shape_of((slots, width)),
        ),
        in_specs=whole(18),
        out_specs=tuple(whole(3)),
        compiler_params=params,
        name="outer",
    )(
        above,
        below,
        partial_low,
        partial_high,
        air_here,
        wind_here,
        packed,
        even_side,
        odd_side,
        near,
        stack,
        bottom,
        exchange_rate,
        sun,
        sea_surface,
        bank_near,
        forward,
        start,
    )

    if groups <= 4:
        turns = sorted(range(1, groups), key=lambda turn: abs(2 * turn - groups))
        gathered = [message] + [shift(message, "cpl", turn) for turn in turns]
    else:
        gathered = [message, lax.all_gather(message, "cpl")]

    air_next, base, response, total_weight, backward = pl.pallas_call(
        settle_kernel,
        out_shape=(
            shape_of((rows, levels, width)),
            shape_of(ocean_shape),
            shape_of((ocean_shape[0], width)),
            shape_of((rows, width)),
            shape_of((3 * remap_tiles.shape[0] * ocean_width, width), bf16),
        ),
        in_specs=whole(6),
        out_specs=tuple([pl.BlockSpec(memory_space=pltpu.HBM)] + whole(4)),
        scratch_shapes=[pltpu.SemaphoreType.DMA((3,))],
        compiler_params=params,
        name="settle",
    )(air_edges, air_inner, bank_near, remap_tiles, ocean_temp, mixing)

    ocean_next, surface_temp = pl.pallas_call(
        make_last_kernel(len(gathered)),
        out_shape=(shape_of(ocean_shape), shape_of((rows, width))),
        in_specs=whole(len(gathered) + 8),
        out_specs=(pl.BlockSpec(memory_space=pltpu.HBM),) * 2,
        scratch_shapes=[
            pltpu.VMEM(ocean_shape, f32),
            pltpu.VMEM((rows, width), f32),
            pltpu.SemaphoreType.DMA((2,)),
        ],
        compiler_params=params,
        name="last",
    )(
        *gathered,
        wanted,
        base,
        response,
        total_weight,
        bottom_next,
        ocean_mask,
        bank_near,
        backward,
    )
    return (air_next, ocean_next, surface_temp)


def solution(mesh):
    placed = (
        P("atm", None, "cpl"),
        P(None, "atm", None, "cpl"),
        P(),
        P("atm", "cpl"),
        P("atm", "cpl"),
        P("atm", "cpl"),
        P("cpl", "atm", None),
        P("cpl", "atm"),
        P("cpl", "atm"),
        P(),
        P(None, ("atm", "cpl")),
        P(),
    )
    return jax.shard_map(
        local,
        mesh=mesh,
        in_specs=placed,
        out_specs=(P("atm", None, "cpl"), P(None, ("atm", "cpl")), P("atm", "cpl")),
        check_vma=False,
    )
```

```python
import jax
import jax.numpy as jnp
from jax import lax
from jax.experimental import pallas as pl
from jax.experimental.pallas import tpu as pltpu
from jax.sharding import PartitionSpec as P

diffusion_rate = 0.05
physics_rate = 0.5
highest = lax.Precision.HIGHEST
f32 = jnp.float32
bf16 = jnp.bfloat16


def pair_even(count):
    return [(i, i ^ 1) for i in range(count)]


def pair_odd(count):
    up = [(i, (i + 1) % count) for i in range(1, count, 2)]
    return up + [(target, source) for source, target in up]


def exchange(to_even, to_odd, axis):
    count = lax.axis_size(axis)
    odd_side = lax.ppermute(to_odd, axis, pair_odd(count))
    even_side = lax.ppermute(to_even, axis, pair_even(count))
    return even_side, odd_side


def shift(block, axis, turn):
    count = lax.axis_size(axis)
    return lax.ppermute(block, axis, [(i, (i + turn) % count) for i in range(count)])


def iota(shape, dim):
    return lax.broadcasted_iota(jnp.int32, shape, dim)


def roll(value, shift):
    return pltpu.roll(value, shift % value.shape[-1], value.ndim - 1)


def pick(flag, yes, no):
    return jnp.where(flag, yes, no)


def rates(first, second):
    return (
        jnp.maximum(first, 0.0) + diffusion_rate,
        diffusion_rate - jnp.minimum(first, 0.0),
        jnp.maximum(second, 0.0) + diffusion_rate,
        diffusion_rate - jnp.minimum(second, 0.0),
    )


def split(value):
    high = value.astype(bf16)
    return high, (value - high.astype(f32)).astype(bf16)


def physics_stack(physics):
    high, low = split(physics)
    return jnp.concatenate([high, high, low], axis=1)


def column(stack, field):
    high, low = split(field)
    tendency = jnp.dot(
        stack, jnp.concatenate([high, low, high], axis=0), preferred_element_type=f32
    )
    return field + physics_rate * jnp.tanh(tendency)


def pack_kernel(
    air, wind, physics, mixing,
    packed, to_even, to_odd, air_here, wind_here, physics_here, mixing_here, sems, square_sems,
):
    rows, levels, width = air.shape
    lane = iota((levels, width), 1)
    place = lane // 4
    kind = lane % 4
    squares = [
        pltpu.make_async_copy(physics, physics_here, square_sems.at[0]),
        pltpu.make_async_copy(mixing, mixing_here, square_sems.at[1]),
    ]
    for copy in squares:
        copy.start()
    parts = sems.shape[1]
    size = rows // parts
    copies = []
    for part in range(parts):
        span = pl.ds(part * size, size)
        copies.append(
            (
                pltpu.make_async_copy(air.at[span], air_here.at[span], sems.at[0, part]),
                pltpu.make_async_copy(wind.at[:, span], wind_here.at[:, span], sems.at[1, part]),
            )
        )
        for copy in copies[-1]:
            copy.start()
    cells = jnp.zeros((levels, width), bf16)
    first = jnp.zeros((levels, width), bf16)
    second = jnp.zeros((levels, width), bf16)
    for x in range(rows):
        if x % size == 0:
            for copy in copies[x // size]:
                copy.wait()
        here = place == x
        cells = pick(here, roll(air_here[x].astype(bf16), 4 * x + 2), cells)
        first = pick(here, roll(wind_here[0, x], 4 * x + 2), first)
        second = pick(here, roll(wind_here[1, x], 4 * x + 2), second)
    to_high = pick(kind < 2, cells, pick(kind == 2, roll(first, 1), roll(second, 2)))
    to_low = pick(kind >= 2, cells, pick(kind == 0, roll(first, -2), roll(second, -1)))
    upper = lax.axis_index("cpl") % 2 == 0
    packed[...] = cells.astype(f32)
    to_even[...] = pick(upper, to_high, to_low)
    to_odd[...] = pick(upper, to_low, to_high)
    for copy in squares:
        copy.wait()


def cpl_sides(even_side, odd_side):
    upper = lax.axis_index("cpl") % 2 == 0
    high = pick(upper, even_side[...].astype(f32), odd_side[...].astype(f32))
    low = pick(upper, odd_side[...].astype(f32), even_side[...].astype(f32))
    return low, high


def outer_cells(low, high):
    kind = iota(low.shape, 1) % 4
    return pick(kind < 2, low, high)


def swap_cells(cells):
    kind = iota(cells.shape, 1) % 4
    return pick(kind == 2, roll(cells, 1), roll(cells, -1))


def sideways(field, swapped, x):
    width = field.shape[1]
    lane = iota(field.shape, 1)
    halo = roll(swapped, -(4 * x + 2))
    south = pick(lane == 0, halo, roll(field, 1))
    north = pick(lane == width - 1, halo, roll(field, -1))
    return south, north


def sideways_of(field, cells, x):
    width = field.shape[1]
    lane = iota(field.shape, 1)
    south = pick(lane == 0, roll(cells, -(4 * x + 1)), roll(field, 1))
    north = pick(lane == width - 1, roll(cells, -(4 * x + 3)), roll(field, -1))
    return south, north


def advance_row(center, west, east, south, north, first, second):
    around = (west + east) + (south + north)
    upwind_first = jnp.where(first > 0.0, west, east) - center
    upwind_second = jnp.where(second > 0.0, south, north) - center
    return ((1.0 - 4.0 * diffusion_rate) * center + diffusion_rate * around) + (
        jnp.abs(first) * upwind_first + jnp.abs(second) * upwind_second
    )


def advance_outer(own, low, high, outer, west, east):
    kind = iota(outer.shape, 1) % 4
    south = roll(pick(kind == 0, outer, own), 1)
    north = roll(pick(kind == 3, outer, own), -1)
    first = pick(kind == 1, roll(low, -1), roll(high, 2))
    second = pick(kind == 1, roll(low, -2), roll(high, 1))
    return advance_row(outer, west, east, south, north, first, second)


def pack_corners(outer, x):
    levels, width = outer.shape
    place = iota((8, width), 1) // 4
    held = jnp.zeros((8, width), f32)
    for at in range(levels // 8):
        held = pick(place == at, roll(outer[8 * at : 8 * at + 8], 4 * (at - x)), held)
    return jnp.concatenate([held, jnp.zeros_like(held)], axis=0)


def unpack_corners(held, levels, x):
    return jnp.concatenate([roll(held[0:8], 4 * (x - at)) for at in range(levels // 8)], axis=0)


def make_edge_kernel(rows, upper):
    def edge_kernel(air, wind, even_side, odd_side, _, message, partial):
        low, high = cpl_sides(even_side, odd_side)
        outer = outer_cells(low, high)
        at, beside = (rows - 1, rows - 2) if upper else (0, 1)
        center, inner = air[at], air[beside]
        levels = center.shape[0]
        cw, ce, cs, cn = rates(wind[0, at].astype(f32), wind[1, at].astype(f32))
        inside, outside = (cw, ce) if upper else (ce, cw)
        south, north = sideways_of(center, outer, rows - 1 if upper else 0)
        known = (
            center
            + (inside * (inner - center) - outside * center)
            + (cs * (south - center) + cn * (north - center))
        )
        partial[0] = known
        partial[1] = outside
        for part, value in enumerate((center, known, outside)):
            message[part * levels : (part + 1) * levels] = value.astype(bf16)
        message[3 * levels :] = pack_corners(outer, rows - 1 if upper else 0).astype(bf16)

    return edge_kernel


def inner_kernel(
    air, wind, stack_ref, own, even_side, odd_side, ready, near, bottom, field
):
    rows, levels, width = air.shape
    low, high = cpl_sides(even_side, odd_side)
    outer = outer_cells(low, high)
    stack = stack_ref[...]
    swapped = swap_cells(outer)
    after = advance_outer(
        own[...], low, high, outer, roll(outer, 4), roll(outer, -4)
    )
    swapped_after = swap_cells(column(stack, after))

    def step(source, halo, x):
        center = source[x]
        south, north = sideways(center, halo, x)
        first, second = wind[0, x].astype(f32), wind[1, x].astype(f32)
        return advance_row(center, source[x - 1], source[x + 1], south, north, first, second)

    def pair(source, halo, x):
        return column(stack, jnp.concatenate([step(source, halo, x), step(source, halo, x + 1)], axis=1))

    for x in range(1, rows - 1, 2):
        both = pair(air, swapped, x)
        field[x] = both[:, :width]
        field[x + 1] = both[:, width:]
    near[0] = field[1]
    near[1] = field[2]
    near[2] = field[rows - 3]
    near[3] = field[rows - 2]
    bottom[...] = jnp.zeros_like(bottom)
    for x in range(2, rows - 2, 2):
        both = pair(field, swapped_after, x)
        ready[x] = both[:, :width]
        ready[x + 1] = both[:, width:]
        bottom[x : x + 1] = both[0:1, :width]
        bottom[x + 1 : x + 2] = both[0:1, width:]


def as_column(row):
    size = row.shape[1]
    square = jnp.broadcast_to(row, (size, size))
    return jnp.sum(
        jnp.where(iota((size, size), 0) == iota((size, size), 1), square, 0.0),
        axis=1,
        keepdims=True,
    )


def fold(value, size):
    span = value.shape[1] // 2
    while span >= size:
        value = value + roll(value, span)
        span //= 2
    return value


def chosen_shares(fluxes, halves, bank, ocean_width):
    rows, width = fluxes[0].shape
    high, low = split(jnp.concatenate(fluxes, axis=0))
    every = jnp.dot(
        jnp.concatenate([high, low, high], axis=1), halves, preferred_element_type=f32
    )
    shares = []
    for part in range(len(fluxes)):
        total = jnp.zeros((rows, width), f32)
        for at in range(0, halves.shape[1], width):
            block = (iota((rows, width), 1) + at) // ocean_width
            mine = every[part * rows : (part + 1) * rows, at : at + width]
            total = total + jnp.where(block == bank, mine, 0.0)
        shares.append(fold(total, ocean_width))
    return shares


def start_kernel(winds, physics, mixing, _, *refs):
    count = 8
    far = refs[:count]
    mask, sea, weights, ocean, exchange_rate, sun, bank_near, message, wanted, forward, stack = refs[
        count : count + 11
    ]
    route, tile, shortwave, bank, sems = refs[count + 11 :]
    here = (route, tile, shortwave, bank, mask, sea, weights, ocean)
    copies = [
        pltpu.make_async_copy(source, target, sems.at[at])
        for at, (source, target) in enumerate(zip(far, here))
    ]
    for copy in copies:
        copy.start()
    rows, width = shortwave.shape
    banks, ocean_width, _ = weights.shape
    depth = ocean.shape[0]
    lane = iota((rows, width), 1)
    group = lax.axis_index("cpl")
    for x in range(rows):
        first = winds[0, x, 0:16].astype(f32)[0:1]
        second = winds[1, x, 0:16].astype(f32)[0:1]
        exchange_rate[x : x + 1] = first * first + second * second
    level = iota((depth, width), 0)
    profile = jnp.exp(level.astype(f32) / -8.0)
    profile = profile / jnp.sum(profile, axis=0, keepdims=True)
    unit = jnp.where(iota((depth, width), 1) == 0, (level == 0).astype(f32), profile)
    message[...] = jnp.full(message.shape, -1.0, f32)
    for copy in copies:
        copy.wait()
    stack[...] = physics_stack(physics[...])
    frac = mask[...].astype(f32)
    exchange_rate[...] = frac * (0.5 + 2.0 * jnp.sqrt(exchange_rate[...] + 0.01))
    target = route[...] * rows + tile[...]
    target_at = as_column(target.astype(f32))
    own_at = (group * rows + iota((rows, 1), 0)).astype(f32)
    wanted[0:rows] = jnp.broadcast_to(target_at, (rows, width))
    wanted[rows : 2 * rows] = jnp.broadcast_to(own_at, (rows, width))
    for at in (0, 2 * ocean_width):
        message[rows : rows + 1, at : at + rows] = target.astype(f32)
        message[rows : rows + 1, at + ocean_width : at + ocean_width + rows] = (
            group * rows + iota((1, rows), 1)
        ).astype(f32)
    bank_at = as_column(bank[...].astype(f32)).astype(jnp.int32)
    high, low = split(weights[...].reshape(banks * ocean_width, width).T)
    forward[...] = jnp.concatenate([high, high, low], axis=0)
    sun[...] = frac * shortwave[...]
    bank_near[...] = jnp.broadcast_to(bank_at, (rows, width))
    top = mixing[0:8]
    settled = 0.5 * ocean[0:8] + jnp.dot(
        top, ocean[...], precision=highest, preferred_element_type=f32
    )
    answer = 0.5 * unit[0:8] + jnp.dot(top, unit, precision=highest, preferred_element_type=f32)
    surface = jnp.zeros((rows, width), f32)
    for at in range(0, rows * ocean_width, width):
        spread = jnp.broadcast_to(settled[0:1, at : at + width], (rows, width))
        surface = surface + jnp.where((lane + at) // ocean_width == iota((rows, width), 0), spread, 0.0)
    surface = fold(surface, ocean_width)
    message[0:rows, :] = surface
    message[rows + 1 : rows + 2, :] = jnp.broadcast_to(answer[0:1, 0:1], (1, width))
    message[rows + 2 : rows + 3, :] = jnp.broadcast_to(answer[0:1, 1:2], (1, width))


def make_outer_kernel(rows):
    def outer_kernel(
        above_ref, below_ref, partial_low, partial_high, air, wind, own, even_side, odd_side,
        near, stack_ref, bottom, rate, sun, sea, bank, forward, start,
        air_edges, bottom_next, message,
    ):
        width = sea.shape[1]
        ocean_width = start.shape[0]
        levels = air.shape[1]
        above = [above_ref[at * levels : (at + 1) * levels].astype(f32) for at in range(3)]
        below = [below_ref[at * levels : (at + 1) * levels].astype(f32) for at in range(3)]
        above.append(unpack_corners(above_ref[3 * levels :].astype(f32), levels, rows - 1))
        below.append(unpack_corners(below_ref[3 * levels :].astype(f32), levels, 0))
        low, high = cpl_sides(even_side, odd_side)
        outer = outer_cells(low, high)
        stack = stack_ref[...]
        place = iota(outer.shape, 1) // 4
        after = advance_outer(
            own[...],
            low,
            high,
            outer,
            pick(place == 0, below[3], roll(outer, 4)),
            pick(place == rows - 1, above[3], roll(outer, -4)),
        )
        moved = jnp.concatenate(
            [
                below[1] + below[2] * air[0],
                partial_low[0] + partial_low[1] * below[0],
                partial_high[0] + partial_high[1] * above[0],
                above[1] + above[2] * air[rows - 1],
                after,
            ],
            axis=1,
        )
        stepped = column(stack, moved)
        parts = [stepped[:, at * width : (at + 1) * width] for at in range(5)]
        inner = [near[at] for at in range(4)]
        bottom_next[...] = bottom[...]
        cells = []
        for center, west, east, x in (
            (parts[1], parts[0], inner[0], 0),
            (inner[0], parts[1], inner[1], 1),
            (inner[3], inner[2], parts[2], rows - 2),
            (parts[2], inner[3], parts[3], rows - 1),
        ):
            south, north = sideways_of(center, parts[4], x)
            first, second = wind[0, x].astype(f32), wind[1, x].astype(f32)
            cells.append(advance_row(center, west, east, south, north, first, second))
        final = column(stack, jnp.concatenate(cells, axis=1))
        for at, x in enumerate((0, 1, rows - 2, rows - 1)):
            row = final[:, at * width : (at + 1) * width]
            air_edges[at] = row
            bottom_next[x : x + 1] = row[0:1]
        heat = rate[...] * (bottom_next[...] - sea[...])
        shares, solar = chosen_shares(
            [heat, sun[...]], forward[...], bank[...], ocean_width
        )
        message[...] = start[...]
        block = iota((rows, width), 1) // ocean_width
        raised = start[rows + 1 : rows + 2, :] * shares + start[rows + 2 : rows + 3, :] * solar
        message[0:rows, :] = jnp.where(
            block == 0,
            shares,
            jnp.where(block == 1, solar, jnp.where(block == 2, raised, start[0:rows, :])),
        )

    return outer_kernel


def settle_kernel(
    edges, inner, bank, weights, ocean, mixing, out, base, response, total_weight, backward, sems
):
    rows = out.shape[0]
    middle = pl.ds(2, rows - 4)
    copies = [
        pltpu.make_async_copy(inner.at[middle], out.at[middle], sems.at[2]),
        pltpu.make_async_copy(edges.at[pl.ds(0, 2)], out.at[pl.ds(0, 2)], sems.at[0]),
        pltpu.make_async_copy(edges.at[pl.ds(2, 2)], out.at[pl.ds(rows - 2, 2)], sems.at[1]),
    ]
    for copy in copies:
        copy.start()
    width = total_weight.shape[1]
    depth = ocean.shape[0]
    banks, ocean_width, _ = weights.shape
    high, low = split(weights[...].reshape(banks * ocean_width, width))
    backward[...] = jnp.concatenate([high, high, low], axis=0)
    sums = jnp.concatenate(
        [jnp.sum(weights[at], axis=0, keepdims=True) for at in range(banks)], axis=0
    )
    hot = (iota((rows, banks), 1) == bank[:, 0:banks]).astype(f32)
    total_weight[...] = jnp.dot(hot, sums, precision=highest, preferred_element_type=f32)
    mixed = mixing[...]
    held = ocean[...]
    base[...] = 0.5 * held + jnp.dot(mixed, held, precision=highest, preferred_element_type=f32)
    level = iota((depth, width), 0)
    profile = jnp.exp(level.astype(f32) / -8.0)
    profile = profile / jnp.sum(profile, axis=0, keepdims=True)
    part = iota((depth, width), 1)
    unit = jnp.where(part == 0, (level == 0).astype(f32), jnp.where(part == 1, profile, 0.0))
    response[...] = 0.5 * unit + jnp.dot(mixed, unit, precision=highest, preferred_element_type=f32)
    for copy in copies:
        copy.wait()


def make_last_kernel(count):
    def last_kernel(*refs):
        messages, (wanted, base, response, total_weight, bottom, mask, bank, backward, ocean_next, surface, ocean_here, surface_here, sems) = (
            refs[:count],
            refs[count:],
        )
        own = messages[0][...]
        if len(messages) == 2 and len(messages[1].shape) == 3:
            blocks = [messages[1][at] for at in range(messages[1].shape[0])]
        else:
            blocks = [ref[...] for ref in messages]
        rows, width = bottom.shape
        slots = own.shape[0]
        ocean_width = slots
        cells = backward.shape[0] // 3
        lane = iota((slots, width), 1)
        labels = []
        values = []
        for block in blocks:
            labels.append(block[rows : rows + 1, :])
            values.append(jnp.where(lane < 3 * ocean_width, block, 0.0))
            values.append(jnp.where(lane < 3 * ocean_width, 0.0, block))
        left = iota((1, width), 1) < 2 * ocean_width
        hot = [
            (wanted[...] == jnp.where(left, labels[at], labels[at + 1])).astype(f32).astype(bf16)
            for at in range(0, len(labels), 2)
        ]
        high, low = split(jnp.concatenate(values, axis=0))
        got = jnp.dot(
            jnp.concatenate(hot + hot, axis=1),
            jnp.concatenate([high, low], axis=0),
            preferred_element_type=f32,
        )
        near = iota((rows, width), 1)
        seen = fold(jnp.where(near >= 2 * ocean_width, got[0:rows], 0.0), ocean_width)
        bank_at = bank[...]
        high, low = split(
            jnp.concatenate(
                [
                    jnp.where((near + at) // ocean_width == bank_at, seen, 0.0)
                    for at in range(0, cells, width)
                ],
                axis=1,
            )
        )
        weighted = jnp.dot(
            jnp.concatenate([high, low, high], axis=1), backward[...], preferred_element_type=f32
        )
        forcing = got[rows : 2 * rows]
        heat = fold(jnp.where(near < ocean_width, forcing, 0.0), ocean_width)
        solar = fold(
            jnp.where((near >= ocean_width) & (near < 2 * ocean_width), forcing, 0.0), ocean_width
        )
        first = response[:, 0:1]
        second = response[:, 1:2]
        for at in range(0, base.shape[1], width):
            mine = (near + at) // ocean_width == iota((rows, width), 0)
            heat_row = jnp.sum(jnp.where(mine, heat, 0.0), axis=0, keepdims=True)
            solar_row = jnp.sum(jnp.where(mine, solar, 0.0), axis=0, keepdims=True)
            ocean_here[:, at : at + width] = base[:, at : at + width] + (
                first * heat_row + second * solar_row
            )
        ocean_out = pltpu.make_async_copy(ocean_here, ocean_next, sems.at[0])
        ocean_out.start()
        frac = mask[...].astype(f32)
        surface_here[...] = frac * (weighted / total_weight[...]) + (1.0 - frac) * bottom[...]
        surface_out = pltpu.make_async_copy(surface_here, surface, sems.at[1])
        surface_out.start()
        ocean_out.wait()
        surface_out.wait()

    return last_kernel


def shape_of(shape, dtype=f32):
    return jax.ShapeDtypeStruct(shape, dtype)


def whole(count):
    return [pl.BlockSpec(memory_space=pltpu.VMEM) for _ in range(count)]


def in_hbm(value):
    return pltpu.with_memory_space_constraint(value, pltpu.HBM)


params = pltpu.CompilerParams(vmem_limit_bytes=48 * 1024 * 1024)


def local(
    air_temp,
    wind_field,
    physics,
    sea_surface,
    shortwave,
    ocean_mask,
    owner_route,
    ocean_tile,
    weight_tile,
    remap_tiles,
    ocean_temp,
    mixing,
):
    rows, levels, width = air_temp.shape
    groups = lax.axis_size("cpl")
    ocean_width = remap_tiles.shape[1]
    slots = ocean_width
    ocean_shape = ocean_temp.shape

    packed, to_even, to_odd, air_here, wind_here, physics, mixing = pl.pallas_call(
        pack_kernel,
        out_shape=(
            pltpu.VMEM((levels, width), f32),
            pltpu.VMEM((levels, width), bf16),
            pltpu.VMEM((levels, width), bf16),
            pltpu.VMEM(air_temp.shape, f32),
            pltpu.VMEM(wind_field.shape, bf16),
            pltpu.VMEM(physics.shape, f32),
            pltpu.VMEM(mixing.shape, f32),
        ),
        in_specs=[pl.BlockSpec(memory_space=pltpu.HBM)] * 4,
        out_specs=tuple(whole(7)),
        scratch_shapes=[pltpu.SemaphoreType.DMA((2, 3)), pltpu.SemaphoreType.DMA((2,))],
        compiler_params=params,
        name="pack",
    )(*(in_hbm(value) for value in (air_temp, wind_field, physics, mixing)))
    even_side, odd_side = exchange(to_even, to_odd, "cpl")

    kept = (ocean_mask, sea_surface, remap_tiles, ocean_temp)
    passing = (owner_route.reshape(1, rows), ocean_tile, shortwave, weight_tile)
    (
        ocean_mask,
        sea_surface,
        remap_tiles,
        ocean_temp,
        exchange_rate,
        sun,
        bank_near,
        start,
        wanted,
        forward,
        stack,
    ) = pl.pallas_call(
        start_kernel,
        out_shape=tuple(pltpu.VMEM(value.shape, value.dtype) for value in kept)
        + (
            shape_of((rows, width)),
            shape_of((rows, width)),
            shape_of((rows, width), jnp.int32),
            shape_of((slots, width)),
            shape_of((2 * rows, width)),
            shape_of((3 * width, remap_tiles.shape[0] * ocean_width), bf16),
            shape_of((levels, 3 * levels), bf16),
        ),
        in_specs=whole(3)
        + [pl.BlockSpec(memory_space=pl.ANY)]
        + [pl.BlockSpec(memory_space=pltpu.HBM)] * len(passing + kept),
        out_specs=tuple(whole(len(kept) + 7)),
        scratch_shapes=[pltpu.VMEM(value.shape, value.dtype) for value in passing]
        + [pltpu.SemaphoreType.DMA((len(passing + kept),))],
        compiler_params=params,
        name="start",
    )(wind_here, physics, mixing, packed, *(in_hbm(value) for value in passing + kept))

    def edge(upper, after):
        return pl.pallas_call(
            make_edge_kernel(rows, upper),
            out_shape=(shape_of((3 * levels + 16, width), bf16), shape_of((2, levels, width))),
            in_specs=whole(4) + [pl.BlockSpec(memory_space=pl.ANY)],
            out_specs=tuple(whole(2)),
            compiler_params=params,
            name="edge",
        )(air_here, wind_here, even_side, odd_side, after)

    to_high, partial_high = edge(1, start)
    below = shift(to_high, "atm", 1)
    to_low, partial_low = edge(0, partial_high)
    above = shift(to_low, "atm", -1)

    air_inner, near, bottom = pl.pallas_call(
        inner_kernel,
        out_shape=(
            pltpu.VMEM((rows, levels, width), f32),
            shape_of((4, levels, width)),
            shape_of((rows, width)),
        ),
        in_specs=whole(6),
        out_specs=tuple(whole(3)),
        scratch_shapes=[pltpu.VMEM((rows, levels, width), f32)],
        compiler_params=params,
        name="inner",
    )(air_here, wind_here, stack, packed, even_side, odd_side)

    air_edges, bottom_next, message = pl.pallas_call(
        make_outer_kernel(rows),
        out_shape=(
            shape_of((4, levels, width)),
            shape_of((rows, width)),
            shape_of((slots, width)),
        ),
        in_specs=whole(18),
        out_specs=tuple(whole(3)),
        compiler_params=params,
        name="outer",
    )(
        above,
        below,
        partial_low,
        partial_high,
        air_here,
        wind_here,
        packed,
        even_side,
        odd_side,
        near,
        stack,
        bottom,
        exchange_rate,
        sun,
        sea_surface,
        bank_near,
        forward,
        start,
    )

    if groups <= 4:
        turns = sorted(range(1, groups), key=lambda turn: abs(2 * turn - groups))
        gathered = [message] + [shift(message, "cpl", turn) for turn in turns]
    else:
        gathered = [message, lax.all_gather(message, "cpl")]

    air_next, base, response, total_weight, backward = pl.pallas_call(
        settle_kernel,
        out_shape=(
            shape_of((rows, levels, width)),
            shape_of(ocean_shape),
            shape_of((ocean_shape[0], width)),
            shape_of((rows, width)),
            shape_of((3 * remap_tiles.shape[0] * ocean_width, width), bf16),
        ),
        in_specs=whole(6),
        out_specs=tuple([pl.BlockSpec(memory_space=pltpu.HBM)] + whole(4)),
        scratch_shapes=[pltpu.SemaphoreType.DMA((3,))],
        compiler_params=params,
        name="settle",
    )(air_edges, air_inner, bank_near, remap_tiles, ocean_temp, mixing)

    ocean_next, surface_temp = pl.pallas_call(
        make_last_kernel(len(gathered)),
        out_shape=(shape_of(ocean_shape), shape_of((rows, width))),
        in_specs=whole(len(gathered) + 8),
        out_specs=(pl.BlockSpec(memory_space=pltpu.HBM),) * 2,
        scratch_shapes=[
            pltpu.VMEM(ocean_shape, f32),
            pltpu.VMEM((rows, width), f32),
            pltpu.SemaphoreType.DMA((2,)),
        ],
        compiler_params=params,
        name="last",
    )(
        *gathered,
        wanted,
        base,
        response,
        total_weight,
        bottom_next,
        ocean_mask,
        bank_near,
        backward,
    )
    return (air_next, ocean_next, surface_temp)


def solution(mesh):
    placed = (
        P("atm", None, "cpl"),
        P(None, "atm", None, "cpl"),
        P(),
        P("atm", "cpl"),
        P("atm", "cpl"),
        P("atm", "cpl"),
        P("cpl", "atm", None),
        P("cpl", "atm"),
        P("cpl", "atm"),
        P(),
        P(None, ("atm", "cpl")),
        P(),
    )
    return jax.shard_map(
        local,
        mesh=mesh,
        in_specs=placed,
        out_specs=(P("atm", None, "cpl"), P(None, ("atm", "cpl")), P("atm", "cpl")),
        check_vma=False,
    )
```

```python
import jax
import jax.numpy as jnp
from jax import lax
from jax.experimental import pallas as pl
from jax.experimental.pallas import tpu as pltpu
from jax.sharding import PartitionSpec as P

diffusion_rate = 0.05
physics_rate = 0.5
highest = lax.Precision.HIGHEST
f32 = jnp.float32
bf16 = jnp.bfloat16


def pair_even(count):
    return [(i, i ^ 1) for i in range(count)]


def pair_odd(count):
    up = [(i, (i + 1) % count) for i in range(1, count, 2)]
    return up + [(target, source) for source, target in up]


def exchange(to_even, to_odd, axis):
    count = lax.axis_size(axis)
    odd_side = lax.ppermute(to_odd, axis, pair_odd(count))
    even_side = lax.ppermute(to_even, axis, pair_even(count))
    return even_side, odd_side


def shift(block, axis, turn):
    count = lax.axis_size(axis)
    return lax.ppermute(block, axis, [(i, (i + turn) % count) for i in range(count)])


def iota(shape, dim):
    return lax.broadcasted_iota(jnp.int32, shape, dim)


def roll(value, shift):
    return pltpu.roll(value, shift % value.shape[-1], value.ndim - 1)


def pick(flag, yes, no):
    return jnp.where(flag, yes, no)


def rates(first, second):
    return (
        jnp.maximum(first, 0.0) + diffusion_rate,
        diffusion_rate - jnp.minimum(first, 0.0),
        jnp.maximum(second, 0.0) + diffusion_rate,
        diffusion_rate - jnp.minimum(second, 0.0),
    )


def split(value):
    high = value.astype(bf16)
    return high, (value - high.astype(f32)).astype(bf16)


def physics_stack(physics):
    high, low = split(physics)
    return jnp.concatenate([high, high, low], axis=1)


def column(stack, field):
    high, low = split(field)
    tendency = jnp.dot(
        stack, jnp.concatenate([high, low, high], axis=0), preferred_element_type=f32
    )
    return field + physics_rate * jnp.tanh(tendency)


def pack_kernel(
    air, wind, physics, mixing,
    packed, to_even, to_odd, air_here, wind_here, physics_here, mixing_here, sems, square_sems,
):
    rows, levels, width = air.shape
    lane = iota((levels, width), 1)
    place = lane // 4
    kind = lane % 4
    squares = [
        pltpu.make_async_copy(physics, physics_here, square_sems.at[0]),
        pltpu.make_async_copy(mixing, mixing_here, square_sems.at[1]),
    ]
    for copy in squares:
        copy.start()
    parts = sems.shape[1]
    size = rows // parts
    copies = []
    for part in range(parts):
        span = pl.ds(part * size, size)
        copies.append(
            (
                pltpu.make_async_copy(air.at[span], air_here.at[span], sems.at[0, part]),
                pltpu.make_async_copy(wind.at[:, span], wind_here.at[:, span], sems.at[1, part]),
            )
        )
        for copy in copies[-1]:
            copy.start()
    cells = jnp.zeros((levels, width), bf16)
    first = jnp.zeros((levels, width), bf16)
    second = jnp.zeros((levels, width), bf16)
    for x in range(rows):
        if x % size == 0:
            for copy in copies[x // size]:
                copy.wait()
        here = place == x
        cells = pick(here, roll(air_here[x].astype(bf16), 4 * x + 2), cells)
        first = pick(here, roll(wind_here[0, x], 4 * x + 2), first)
        second = pick(here, roll(wind_here[1, x], 4 * x + 2), second)
    to_high = pick(kind < 2, cells, pick(kind == 2, roll(first, 1), roll(second, 2)))
    to_low = pick(kind >= 2, cells, pick(kind == 0, roll(first, -2), roll(second, -1)))
    upper = lax.axis_index("cpl") % 2 == 0
    packed[...] = cells.astype(f32)
    to_even[...] = pick(upper, to_high, to_low)
    to_odd[...] = pick(upper, to_low, to_high)
    for copy in squares:
        copy.wait()


def cpl_sides(even_side, odd_side):
    upper = lax.axis_index("cpl") % 2 == 0
    high = pick(upper, even_side[...].astype(f32), odd_side[...].astype(f32))
    low = pick(upper, odd_side[...].astype(f32), even_side[...].astype(f32))
    return low, high


def outer_cells(low, high):
    kind = iota(low.shape, 1) % 4
    return pick(kind < 2, low, high)


def swap_cells(cells):
    kind = iota(cells.shape, 1) % 4
    return pick(kind == 2, roll(cells, 1), roll(cells, -1))


def sideways(field, swapped, x):
    width = field.shape[1]
    lane = iota(field.shape, 1)
    halo = roll(swapped, -(4 * x + 2))
    south = pick(lane == 0, halo, roll(field, 1))
    north = pick(lane == width - 1, halo, roll(field, -1))
    return south, north


def sideways_of(field, cells, x):
    width = field.shape[1]
    lane = iota(field.shape, 1)
    south = pick(lane == 0, roll(cells, -(4 * x + 1)), roll(field, 1))
    north = pick(lane == width - 1, roll(cells, -(4 * x + 3)), roll(field, -1))
    return south, north


def advance_row(center, west, east, south, north, first, second):
    around = (west + east) + (south + north)
    upwind_first = jnp.where(first > 0.0, west, east) - center
    upwind_second = jnp.where(second > 0.0, south, north) - center
    return ((1.0 - 4.0 * diffusion_rate) * center + diffusion_rate * around) + (
        jnp.abs(first) * upwind_first + jnp.abs(second) * upwind_second
    )


def advance_outer(own, low, high, outer, west, east):
    kind = iota(outer.shape, 1) % 4
    south = roll(pick(kind == 0, outer, own), 1)
    north = roll(pick(kind == 3, outer, own), -1)
    first = pick(kind == 1, roll(low, -1), roll(high, 2))
    second = pick(kind == 1, roll(low, -2), roll(high, 1))
    return advance_row(outer, west, east, south, north, first, second)


def pack_corners(outer, x):
    levels, width = outer.shape
    place = iota((8, width), 1) // 4
    held = jnp.zeros((8, width), f32)
    for at in range(levels // 8):
        held = pick(place == at, roll(outer[8 * at : 8 * at + 8], 4 * (at - x)), held)
    return jnp.concatenate([held, jnp.zeros_like(held)], axis=0)


def unpack_corners(held, levels, x):
    return jnp.concatenate([roll(held[0:8], 4 * (x - at)) for at in range(levels // 8)], axis=0)


def make_edge_kernel(rows, upper):
    def edge_kernel(air, wind, even_side, odd_side, _, message, partial):
        low, high = cpl_sides(even_side, odd_side)
        outer = outer_cells(low, high)
        at, beside = (rows - 1, rows - 2) if upper else (0, 1)
        center, inner = air[at], air[beside]
        levels = center.shape[0]
        cw, ce, cs, cn = rates(wind[0, at].astype(f32), wind[1, at].astype(f32))
        inside, outside = (cw, ce) if upper else (ce, cw)
        south, north = sideways_of(center, outer, rows - 1 if upper else 0)
        known = (
            center
            + (inside * (inner - center) - outside * center)
            + (cs * (south - center) + cn * (north - center))
        )
        partial[0] = known
        partial[1] = outside
        for part, value in enumerate((center, known, outside)):
            message[part * levels : (part + 1) * levels] = value.astype(bf16)
        message[3 * levels :] = pack_corners(outer, rows - 1 if upper else 0).astype(bf16)

    return edge_kernel


def inner_kernel(
    air, wind, stack_ref, own, even_side, odd_side, ready, near, bottom, field
):
    rows, levels, width = air.shape
    low, high = cpl_sides(even_side, odd_side)
    outer = outer_cells(low, high)
    stack = stack_ref[...]
    swapped = swap_cells(outer)
    after = advance_outer(
        own[...], low, high, outer, roll(outer, 4), roll(outer, -4)
    )
    swapped_after = swap_cells(column(stack, after))

    def step(source, halo, x):
        center = source[x]
        south, north = sideways(center, halo, x)
        first, second = wind[0, x].astype(f32), wind[1, x].astype(f32)
        return advance_row(center, source[x - 1], source[x + 1], south, north, first, second)

    def pair(source, halo, x):
        return column(stack, jnp.concatenate([step(source, halo, x), step(source, halo, x + 1)], axis=1))

    for x in range(1, rows - 1, 2):
        both = pair(air, swapped, x)
        field[x] = both[:, :width]
        field[x + 1] = both[:, width:]
    near[0] = field[1]
    near[1] = field[2]
    near[2] = field[rows - 3]
    near[3] = field[rows - 2]
    bottom[...] = jnp.zeros_like(bottom)
    for x in range(2, rows - 2, 2):
        both = pair(field, swapped_after, x)
        ready[x] = both[:, :width]
        ready[x + 1] = both[:, width:]
        bottom[x : x + 1] = both[0:1, :width]
        bottom[x + 1 : x + 2] = both[0:1, width:]


def as_column(row):
    size = row.shape[1]
    square = jnp.broadcast_to(row, (size, size))
    return jnp.sum(
        jnp.where(iota((size, size), 0) == iota((size, size), 1), square, 0.0),
        axis=1,
        keepdims=True,
    )


def fold(value, size):
    parts = [value] + [roll(value, at) for at in range(size, value.shape[1], size)]
    while len(parts) > 1:
        parts = [left + right for left, right in zip(parts[0::2], parts[1::2])]
    return parts[0]


def chosen_shares(fluxes, halves, bank, ocean_width):
    rows, width = fluxes[0].shape
    high, low = split(jnp.concatenate(fluxes, axis=0))
    every = jnp.dot(
        jnp.concatenate([high, low, high], axis=1), halves, preferred_element_type=f32
    )
    shares = []
    for part in range(len(fluxes)):
        total = jnp.zeros((rows, width), f32)
        for at in range(0, halves.shape[1], width):
            block = (iota((rows, width), 1) + at) // ocean_width
            mine = every[part * rows : (part + 1) * rows, at : at + width]
            total = total + jnp.where(block == bank, mine, 0.0)
        shares.append(fold(total, ocean_width))
    return shares


def start_kernel(winds, physics, mixing, _, *refs):
    count = 8
    far = refs[:count]
    mask, sea, weights, ocean, exchange_rate, sun, bank_near, message, wanted, forward, stack = refs[
        count : count + 11
    ]
    route, tile, shortwave, bank, sems = refs[count + 11 :]
    here = (route, tile, shortwave, bank, mask, sea, weights, ocean)
    copies = [
        pltpu.make_async_copy(source, target, sems.at[at])
        for at, (source, target) in enumerate(zip(far, here))
    ]
    for copy in copies:
        copy.start()
    rows, width = shortwave.shape
    banks, ocean_width, _ = weights.shape
    depth = ocean.shape[0]
    lane = iota((rows, width), 1)
    group = lax.axis_index("cpl")
    for x in range(rows):
        first = winds[0, x, 0:16].astype(f32)[0:1]
        second = winds[1, x, 0:16].astype(f32)[0:1]
        exchange_rate[x : x + 1] = first * first + second * second
    level = iota((depth, width), 0)
    profile = jnp.exp(level.astype(f32) / -8.0)
    profile = profile / jnp.sum(profile, axis=0, keepdims=True)
    unit = jnp.where(iota((depth, width), 1) == 0, (level == 0).astype(f32), profile)
    message[...] = jnp.full(message.shape, -1.0, f32)
    for copy in copies:
        copy.wait()
    stack[...] = physics_stack(physics[...])
    frac = mask[...].astype(f32)
    exchange_rate[...] = frac * (0.5 + 2.0 * jnp.sqrt(exchange_rate[...] + 0.01))
    target = route[...] * rows + tile[...]
    target_at = as_column(target.astype(f32))
    own_at = (group * rows + iota((rows, 1), 0)).astype(f32)
    wanted[0:rows] = jnp.broadcast_to(target_at, (rows, width))
    wanted[rows : 2 * rows] = jnp.broadcast_to(own_at, (rows, width))
    for at in (0, 2 * ocean_width):
        message[rows : rows + 1, at : at + rows] = target.astype(f32)
        message[rows : rows + 1, at + ocean_width : at + ocean_width + rows] = (
            group * rows + iota((1, rows), 1)
        ).astype(f32)
    bank_at = as_column(bank[...].astype(f32)).astype(jnp.int32)
    high, low = split(weights[...].reshape(banks * ocean_width, width).T)
    forward[...] = jnp.concatenate([high, high, low], axis=0)
    sun[...] = frac * shortwave[...]
    bank_near[...] = jnp.broadcast_to(bank_at, (rows, width))
    top = mixing[0:8]
    settled = 0.5 * ocean[0:8] + jnp.dot(
        top, ocean[...], precision=highest, preferred_element_type=f32
    )
    answer = 0.5 * unit[0:8] + jnp.dot(top, unit, precision=highest, preferred_element_type=f32)
    surface = jnp.zeros((rows, width), f32)
    for at in range(0, rows * ocean_width, width):
        spread = jnp.broadcast_to(settled[0:1, at : at + width], (rows, width))
        surface = surface + jnp.where((lane + at) // ocean_width == iota((rows, width), 0), spread, 0.0)
    surface = fold(surface, ocean_width)
    message[0:rows, :] = surface
    message[rows + 1 : rows + 2, :] = jnp.broadcast_to(answer[0:1, 0:1], (1, width))
    message[rows + 2 : rows + 3, :] = jnp.broadcast_to(answer[0:1, 1:2], (1, width))


def make_outer_kernel(rows):
    def outer_kernel(
        above_ref, below_ref, partial_low, partial_high, air, wind, own, even_side, odd_side,
        near, stack_ref, bottom, rate, sun, sea, bank, forward, start,
        air_edges, bottom_next, message,
    ):
        width = sea.shape[1]
        ocean_width = start.shape[0]
        levels = air.shape[1]
        above = [above_ref[at * levels : (at + 1) * levels].astype(f32) for at in range(3)]
        below = [below_ref[at * levels : (at + 1) * levels].astype(f32) for at in range(3)]
        above.append(unpack_corners(above_ref[3 * levels :].astype(f32), levels, rows - 1))
        below.append(unpack_corners(below_ref[3 * levels :].astype(f32), levels, 0))
        low, high = cpl_sides(even_side, odd_side)
        outer = outer_cells(low, high)
        stack = stack_ref[...]
        place = iota(outer.shape, 1) // 4
        after = advance_outer(
            own[...],
            low,
            high,
            outer,
            pick(place == 0, below[3], roll(outer, 4)),
            pick(place == rows - 1, above[3], roll(outer, -4)),
        )
        moved = jnp.concatenate(
            [
                below[1] + below[2] * air[0],
                partial_low[0] + partial_low[1] * below[0],
                partial_high[0] + partial_high[1] * above[0],
                above[1] + above[2] * air[rows - 1],
                after,
            ],
            axis=1,
        )
        stepped = column(stack, moved)
        parts = [stepped[:, at * width : (at + 1) * width] for at in range(5)]
        inner = [near[at] for at in range(4)]
        bottom_next[...] = bottom[...]
        cells = []
        for center, west, east, x in (
            (parts[1], parts[0], inner[0], 0),
            (inner[0], parts[1], inner[1], 1),
            (inner[3], inner[2], parts[2], rows - 2),
            (parts[2], inner[3], parts[3], rows - 1),
        ):
            south, north = sideways_of(center, parts[4], x)
            first, second = wind[0, x].astype(f32), wind[1, x].astype(f32)
            cells.append(advance_row(center, west, east, south, north, first, second))
        final = column(stack, jnp.concatenate(cells, axis=1))
        for at, x in enumerate((0, 1, rows - 2, rows - 1)):
            row = final[:, at * width : (at + 1) * width]
            air_edges[at] = row
            bottom_next[x : x + 1] = row[0:1]
        heat = rate[...] * (bottom_next[...] - sea[...])
        shares, solar = chosen_shares(
            [heat, sun[...]], forward[...], bank[...], ocean_width
        )
        message[...] = start[...]
        block = iota((rows, width), 1) // ocean_width
        raised = start[rows + 1 : rows + 2, :] * shares + start[rows + 2 : rows + 3, :] * solar
        message[0:rows, :] = jnp.where(
            block == 0,
            shares,
            jnp.where(block == 1, solar, jnp.where(block == 2, raised, start[0:rows, :])),
        )

    return outer_kernel


def settle_kernel(
    edges, inner, bank, weights, ocean, mixing, out, base, response, total_weight, backward, sems
):
    rows = out.shape[0]
    middle = pl.ds(2, rows - 4)
    copies = [
        pltpu.make_async_copy(inner.at[middle], out.at[middle], sems.at[2]),
        pltpu.make_async_copy(edges.at[pl.ds(0, 2)], out.at[pl.ds(0, 2)], sems.at[0]),
        pltpu.make_async_copy(edges.at[pl.ds(2, 2)], out.at[pl.ds(rows - 2, 2)], sems.at[1]),
    ]
    for copy in copies:
        copy.start()
    width = total_weight.shape[1]
    depth = ocean.shape[0]
    banks, ocean_width, _ = weights.shape
    high, low = split(weights[...].reshape(banks * ocean_width, width))
    backward[...] = jnp.concatenate([high, high, low], axis=0)
    sums = jnp.concatenate(
        [jnp.sum(weights[at], axis=0, keepdims=True) for at in range(banks)], axis=0
    )
    hot = (iota((rows, banks), 1) == bank[:, 0:banks]).astype(f32)
    total_weight[...] = jnp.dot(hot, sums, precision=highest, preferred_element_type=f32)
    mixed = mixing[...]
    held = ocean[...]
    base[...] = 0.5 * held + jnp.dot(mixed, held, precision=highest, preferred_element_type=f32)
    level = iota((depth, width), 0)
    profile = jnp.exp(level.astype(f32) / -8.0)
    profile = profile / jnp.sum(profile, axis=0, keepdims=True)
    part = iota((depth, width), 1)
    unit = jnp.where(part == 0, (level == 0).astype(f32), jnp.where(part == 1, profile, 0.0))
    response[...] = 0.5 * unit + jnp.dot(mixed, unit, precision=highest, preferred_element_type=f32)
    for copy in copies:
        copy.wait()


def make_last_kernel(count):
    def last_kernel(*refs):
        messages, (wanted, base, response, total_weight, bottom, mask, bank, backward, ocean_next, surface, ocean_here, surface_here, sems) = (
            refs[:count],
            refs[count:],
        )
        own = messages[0][...]
        if len(messages) == 2 and len(messages[1].shape) == 3:
            blocks = [messages[1][at] for at in range(messages[1].shape[0])]
        else:
            blocks = [ref[...] for ref in messages]
        rows, width = bottom.shape
        slots = own.shape[0]
        ocean_width = slots
        cells = backward.shape[0] // 3
        lane = iota((slots, width), 1)
        labels = []
        values = []
        for block in blocks:
            labels.append(block[rows : rows + 1, :])
            values.append(jnp.where(lane < 3 * ocean_width, block, 0.0))
            values.append(jnp.where(lane < 3 * ocean_width, 0.0, block))
        left = iota((1, width), 1) < 2 * ocean_width
        hot = [
            (wanted[...] == jnp.where(left, labels[at], labels[at + 1])).astype(f32).astype(bf16)
            for at in range(0, len(labels), 2)
        ]
        high, low = split(jnp.concatenate(values, axis=0))
        got = jnp.dot(
            jnp.concatenate(hot + hot, axis=1),
            jnp.concatenate([high, low], axis=0),
            preferred_element_type=f32,
        )
        near = iota((rows, width), 1)
        seen = fold(jnp.where(near >= 2 * ocean_width, got[0:rows], 0.0), ocean_width)
        bank_at = bank[...]
        high, low = split(
            jnp.concatenate(
                [
                    jnp.where((near + at) // ocean_width == bank_at, seen, 0.0)
                    for at in range(0, cells, width)
                ],
                axis=1,
            )
        )
        weighted = jnp.dot(
            jnp.concatenate([high, low, high], axis=1), backward[...], preferred_element_type=f32
        )
        forcing = got[rows : 2 * rows]
        heat = fold(jnp.where(near < ocean_width, forcing, 0.0), ocean_width)
        solar = fold(
            jnp.where((near >= ocean_width) & (near < 2 * ocean_width), forcing, 0.0), ocean_width
        )
        first = response[:, 0:1]
        second = response[:, 1:2]
        for at in range(0, base.shape[1], width):
            mine = (near + at) // ocean_width == iota((rows, width), 0)
            heat_row = jnp.sum(jnp.where(mine, heat, 0.0), axis=0, keepdims=True)
            solar_row = jnp.sum(jnp.where(mine, solar, 0.0), axis=0, keepdims=True)
            ocean_here[:, at : at + width] = base[:, at : at + width] + (
                first * heat_row + second * solar_row
            )
        ocean_out = pltpu.make_async_copy(ocean_here, ocean_next, sems.at[0])
        ocean_out.start()
        frac = mask[...].astype(f32)
        surface_here[...] = frac * (weighted / total_weight[...]) + (1.0 - frac) * bottom[...]
        surface_out = pltpu.make_async_copy(surface_here, surface, sems.at[1])
        surface_out.start()
        ocean_out.wait()
        surface_out.wait()

    return last_kernel


def shape_of(shape, dtype=f32):
    return jax.ShapeDtypeStruct(shape, dtype)


def whole(count):
    return [pl.BlockSpec(memory_space=pltpu.VMEM) for _ in range(count)]


def in_hbm(value):
    return pltpu.with_memory_space_constraint(value, pltpu.HBM)


params = pltpu.CompilerParams(vmem_limit_bytes=48 * 1024 * 1024)


def local(
    air_temp,
    wind_field,
    physics,
    sea_surface,
    shortwave,
    ocean_mask,
    owner_route,
    ocean_tile,
    weight_tile,
    remap_tiles,
    ocean_temp,
    mixing,
):
    rows, levels, width = air_temp.shape
    groups = lax.axis_size("cpl")
    ocean_width = remap_tiles.shape[1]
    slots = ocean_width
    ocean_shape = ocean_temp.shape

    packed, to_even, to_odd, air_here, wind_here, physics, mixing = pl.pallas_call(
        pack_kernel,
        out_shape=(
            pltpu.VMEM((levels, width), f32),
            pltpu.VMEM((levels, width), bf16),
            pltpu.VMEM((levels, width), bf16),
            pltpu.VMEM(air_temp.shape, f32),
            pltpu.VMEM(wind_field.shape, bf16),
            pltpu.VMEM(physics.shape, f32),
            pltpu.VMEM(mixing.shape, f32),
        ),
        in_specs=[pl.BlockSpec(memory_space=pltpu.HBM)] * 4,
        out_specs=tuple(whole(7)),
        scratch_shapes=[pltpu.SemaphoreType.DMA((2, 3)), pltpu.SemaphoreType.DMA((2,))],
        compiler_params=params,
        name="pack",
    )(*(in_hbm(value) for value in (air_temp, wind_field, physics, mixing)))
    even_side, odd_side = exchange(to_even, to_odd, "cpl")

    kept = (ocean_mask, sea_surface, remap_tiles, ocean_temp)
    passing = (owner_route.reshape(1, rows), ocean_tile, shortwave, weight_tile)
    (
        ocean_mask,
        sea_surface,
        remap_tiles,
        ocean_temp,
        exchange_rate,
        sun,
        bank_near,
        start,
        wanted,
        forward,
        stack,
    ) = pl.pallas_call(
        start_kernel,
        out_shape=tuple(pltpu.VMEM(value.shape, value.dtype) for value in kept)
        + (
            shape_of((rows, width)),
            shape_of((rows, width)),
            shape_of((rows, width), jnp.int32),
            shape_of((slots, width)),
            shape_of((2 * rows, width)),
            shape_of((3 * width, remap_tiles.shape[0] * ocean_width), bf16),
            shape_of((levels, 3 * levels), bf16),
        ),
        in_specs=whole(3)
        + [pl.BlockSpec(memory_space=pl.ANY)]
        + [pl.BlockSpec(memory_space=pltpu.HBM)] * len(passing + kept),
        out_specs=tuple(whole(len(kept) + 7)),
        scratch_shapes=[pltpu.VMEM(value.shape, value.dtype) for value in passing]
        + [pltpu.SemaphoreType.DMA((len(passing + kept),))],
        compiler_params=params,
        name="start",
    )(wind_here, physics, mixing, packed, *(in_hbm(value) for value in passing + kept))

    def edge(upper, after):
        return pl.pallas_call(
            make_edge_kernel(rows, upper),
            out_shape=(shape_of((3 * levels + 16, width), bf16), shape_of((2, levels, width))),
            in_specs=whole(4) + [pl.BlockSpec(memory_space=pl.ANY)],
            out_specs=tuple(whole(2)),
            compiler_params=params,
            name="edge",
        )(air_here, wind_here, even_side, odd_side, after)

    to_high, partial_high = edge(1, start)
    below = shift(to_high, "atm", 1)
    to_low, partial_low = edge(0, partial_high)
    above = shift(to_low, "atm", -1)

    air_inner, near, bottom = pl.pallas_call(
        inner_kernel,
        out_shape=(
            pltpu.VMEM((rows, levels, width), f32),
            shape_of((4, levels, width)),
            shape_of((rows, width)),
        ),
        in_specs=whole(6),
        out_specs=tuple(whole(3)),
        scratch_shapes=[pltpu.VMEM((rows, levels, width), f32)],
        compiler_params=params,
        name="inner",
    )(air_here, wind_here, stack, packed, even_side, odd_side)

    air_edges, bottom_next, message = pl.pallas_call(
        make_outer_kernel(rows),
        out_shape=(
            shape_of((4, levels, width)),
            shape_of((rows, width)),
            shape_of((slots, width)),
        ),
        in_specs=whole(18),
        out_specs=tuple(whole(3)),
        compiler_params=params,
        name="outer",
    )(
        above,
        below,
        partial_low,
        partial_high,
        air_here,
        wind_here,
        packed,
        even_side,
        odd_side,
        near,
        stack,
        bottom,
        exchange_rate,
        sun,
        sea_surface,
        bank_near,
        forward,
        start,
    )

    if groups <= 4:
        turns = sorted(range(1, groups), key=lambda turn: abs(2 * turn - groups))
        gathered = [message] + [shift(message, "cpl", turn) for turn in turns]
    else:
        gathered = [message, lax.all_gather(message, "cpl")]

    air_next, base, response, total_weight, backward = pl.pallas_call(
        settle_kernel,
        out_shape=(
            shape_of((rows, levels, width)),
            shape_of(ocean_shape),
            shape_of((ocean_shape[0], width)),
            shape_of((rows, width)),
            shape_of((3 * remap_tiles.shape[0] * ocean_width, width), bf16),
        ),
        in_specs=whole(6),
        out_specs=tuple([pl.BlockSpec(memory_space=pltpu.HBM)] + whole(4)),
        scratch_shapes=[pltpu.SemaphoreType.DMA((3,))],
        compiler_params=params,
        name="settle",
    )(air_edges, air_inner, bank_near, remap_tiles, ocean_temp, mixing)

    ocean_next, surface_temp = pl.pallas_call(
        make_last_kernel(len(gathered)),
        out_shape=(shape_of(ocean_shape), shape_of((rows, width))),
        in_specs=whole(len(gathered) + 8),
        out_specs=(pl.BlockSpec(memory_space=pltpu.HBM),) * 2,
        scratch_shapes=[
            pltpu.VMEM(ocean_shape, f32),
            pltpu.VMEM((rows, width), f32),
            pltpu.SemaphoreType.DMA((2,)),
        ],
        compiler_params=params,
        name="last",
    )(
        *gathered,
        wanted,
        base,
        response,
        total_weight,
        bottom_next,
        ocean_mask,
        bank_near,
        backward,
    )
    return (air_next, ocean_next, surface_temp)


def solution(mesh):
    placed = (
        P("atm", None, "cpl"),
        P(None, "atm", None, "cpl"),
        P(),
        P("atm", "cpl"),
        P("atm", "cpl"),
        P("atm", "cpl"),
        P("cpl", "atm", None),
        P("cpl", "atm"),
        P("cpl", "atm"),
        P(),
        P(None, ("atm", "cpl")),
        P(),
    )
    return jax.shard_map(
        local,
        mesh=mesh,
        in_specs=placed,
        out_specs=(P("atm", None, "cpl"), P(None, ("atm", "cpl")), P("atm", "cpl")),
        check_vma=False,
    )
```

```python
import jax
import jax.numpy as jnp
from jax import lax
from jax.experimental import pallas as pl
from jax.experimental.pallas import tpu as pltpu
from jax.sharding import PartitionSpec as P

diffusion_rate = 0.05
physics_rate = 0.5
highest = lax.Precision.HIGHEST
f32 = jnp.float32
bf16 = jnp.bfloat16


def pair_even(count):
    return [(i, i ^ 1) for i in range(count)]


def pair_odd(count):
    up = [(i, (i + 1) % count) for i in range(1, count, 2)]
    return up + [(target, source) for source, target in up]


def exchange(to_even, to_odd, axis):
    count = lax.axis_size(axis)
    odd_side = lax.ppermute(to_odd, axis, pair_odd(count))
    even_side = lax.ppermute(to_even, axis, pair_even(count))
    return even_side, odd_side


def shift(block, axis, turn):
    count = lax.axis_size(axis)
    return lax.ppermute(block, axis, [(i, (i + turn) % count) for i in range(count)])


def iota(shape, dim):
    return lax.broadcasted_iota(jnp.int32, shape, dim)


def roll(value, shift):
    return pltpu.roll(value, shift % value.shape[-1], value.ndim - 1)


def pick(flag, yes, no):
    return jnp.where(flag, yes, no)


def rates(first, second):
    return (
        jnp.maximum(first, 0.0) + diffusion_rate,
        diffusion_rate - jnp.minimum(first, 0.0),
        jnp.maximum(second, 0.0) + diffusion_rate,
        diffusion_rate - jnp.minimum(second, 0.0),
    )


def split(value):
    high = value.astype(bf16)
    return high, (value - high.astype(f32)).astype(bf16)


def physics_stack(physics):
    high, low = split(physics)
    return jnp.concatenate([high, high, low], axis=1)


def column(stack, field):
    high, low = split(field)
    tendency = jnp.dot(
        stack, jnp.concatenate([high, low, high], axis=0), preferred_element_type=f32
    )
    return field + physics_rate * jnp.tanh(tendency)


def pack_kernel(
    air, wind, physics, mixing,
    packed, to_even, to_odd, air_here, wind_here, physics_here, mixing_here, sems, square_sems,
):
    rows, levels, width = air.shape
    lane = iota((levels, width), 1)
    place = lane // 4
    kind = lane % 4
    squares = [
        pltpu.make_async_copy(physics, physics_here, square_sems.at[0]),
        pltpu.make_async_copy(mixing, mixing_here, square_sems.at[1]),
    ]
    parts = sems.shape[1]
    size = rows // parts
    copies = []
    for part in range(parts):
        span = pl.ds(part * size, size)
        copies.append(
            (
                pltpu.make_async_copy(air.at[span], air_here.at[span], sems.at[0, part]),
                pltpu.make_async_copy(wind.at[:, span], wind_here.at[:, span], sems.at[1, part]),
            )
        )
        for copy in copies[-1]:
            copy.start()
    for copy in squares:
        copy.start()
    cells = jnp.zeros((levels, width), bf16)
    first = jnp.zeros((levels, width), bf16)
    second = jnp.zeros((levels, width), bf16)
    for x in range(rows):
        if x % size == 0:
            for copy in copies[x // size]:
                copy.wait()
        here = place == x
        cells = pick(here, roll(air_here[x].astype(bf16), 4 * x + 2), cells)
        first = pick(here, roll(wind_here[0, x], 4 * x + 2), first)
        second = pick(here, roll(wind_here[1, x], 4 * x + 2), second)
    to_high = pick(kind < 2, cells, pick(kind == 2, roll(first, 1), roll(second, 2)))
    to_low = pick(kind >= 2, cells, pick(kind == 0, roll(first, -2), roll(second, -1)))
    upper = lax.axis_index("cpl") % 2 == 0
    packed[...] = cells.astype(f32)
    to_even[...] = pick(upper, to_high, to_low)
    to_odd[...] = pick(upper, to_low, to_high)
    for copy in squares:
        copy.wait()


def cpl_sides(even_side, odd_side):
    upper = lax.axis_index("cpl") % 2 == 0
    high = pick(upper, even_side[...].astype(f32), odd_side[...].astype(f32))
    low = pick(upper, odd_side[...].astype(f32), even_side[...].astype(f32))
    return low, high


def outer_cells(low, high):
    kind = iota(low.shape, 1) % 4
    return pick(kind < 2, low, high)


def swap_cells(cells):
    kind = iota(cells.shape, 1) % 4
    return pick(kind == 2, roll(cells, 1), roll(cells, -1))


def sideways(field, swapped, x):
    width = field.shape[1]
    lane = iota(field.shape, 1)
    halo = roll(swapped, -(4 * x + 2))
    south = pick(lane == 0, halo, roll(field, 1))
    north = pick(lane == width - 1, halo, roll(field, -1))
    return south, north


def sideways_of(field, cells, x):
    width = field.shape[1]
    lane = iota(field.shape, 1)
    south = pick(lane == 0, roll(cells, -(4 * x + 1)), roll(field, 1))
    north = pick(lane == width - 1, roll(cells, -(4 * x + 3)), roll(field, -1))
    return south, north


def advance_row(center, west, east, south, north, first, second):
    around = (west + east) + (south + north)
    upwind_first = jnp.where(first > 0.0, west, east) - center
    upwind_second = jnp.where(second > 0.0, south, north) - center
    return ((1.0 - 4.0 * diffusion_rate) * center + diffusion_rate * around) + (
        jnp.abs(first) * upwind_first + jnp.abs(second) * upwind_second
    )


def advance_outer(own, low, high, outer, west, east):
    kind = iota(outer.shape, 1) % 4
    south = roll(pick(kind == 0, outer, own), 1)
    north = roll(pick(kind == 3, outer, own), -1)
    first = pick(kind == 1, roll(low, -1), roll(high, 2))
    second = pick(kind == 1, roll(low, -2), roll(high, 1))
    return advance_row(outer, west, east, south, north, first, second)


def pack_corners(outer, x):
    levels, width = outer.shape
    place = iota((8, width), 1) // 4
    held = jnp.zeros((8, width), f32)
    for at in range(levels // 8):
        held = pick(place == at, roll(outer[8 * at : 8 * at + 8], 4 * (at - x)), held)
    return jnp.concatenate([held, jnp.zeros_like(held)], axis=0)


def unpack_corners(held, levels, x):
    return jnp.concatenate([roll(held[0:8], 4 * (x - at)) for at in range(levels // 8)], axis=0)


def make_edge_kernel(rows, upper):
    def edge_kernel(air, wind, even_side, odd_side, _, message, partial):
        low, high = cpl_sides(even_side, odd_side)
        outer = outer_cells(low, high)
        at, beside = (rows - 1, rows - 2) if upper else (0, 1)
        center, inner = air[at], air[beside]
        levels = center.shape[0]
        cw, ce, cs, cn = rates(wind[0, at].astype(f32), wind[1, at].astype(f32))
        inside, outside = (cw, ce) if upper else (ce, cw)
        south, north = sideways_of(center, outer, rows - 1 if upper else 0)
        known = (
            center
            + (inside * (inner - center) - outside * center)
            + (cs * (south - center) + cn * (north - center))
        )
        partial[0] = known
        partial[1] = outside
        for part, value in enumerate((center, known, outside)):
            message[part * levels : (part + 1) * levels] = value.astype(bf16)
        message[3 * levels :] = pack_corners(outer, rows - 1 if upper else 0).astype(bf16)

    return edge_kernel


def inner_kernel(
    air, wind, stack_ref, own, even_side, odd_side, ready, near, bottom, field
):
    rows, levels, width = air.shape
    low, high = cpl_sides(even_side, odd_side)
    outer = outer_cells(low, high)
    stack = stack_ref[...]
    swapped = swap_cells(outer)
    after = advance_outer(
        own[...], low, high, outer, roll(outer, 4), roll(outer, -4)
    )
    swapped_after = swap_cells(column(stack, after))

    def step(source, halo, x):
        center = source[x]
        south, north = sideways(center, halo, x)
        first, second = wind[0, x].astype(f32), wind[1, x].astype(f32)
        return advance_row(center, source[x - 1], source[x + 1], south, north, first, second)

    def pair(source, halo, x):
        return column(stack, jnp.concatenate([step(source, halo, x), step(source, halo, x + 1)], axis=1))

    for x in range(1, rows - 1, 2):
        both = pair(air, swapped, x)
        field[x] = both[:, :width]
        field[x + 1] = both[:, width:]
    near[0] = field[1]
    near[1] = field[2]
    near[2] = field[rows - 3]
    near[3] = field[rows - 2]
    bottom[...] = jnp.zeros_like(bottom)
    for x in range(2, rows - 2, 2):
        both = pair(field, swapped_after, x)
        ready[x] = both[:, :width]
        ready[x + 1] = both[:, width:]
        bottom[x : x + 1] = both[0:1, :width]
        bottom[x + 1 : x + 2] = both[0:1, width:]


def as_column(row):
    size = row.shape[1]
    square = jnp.broadcast_to(row, (size, size))
    return jnp.sum(
        jnp.where(iota((size, size), 0) == iota((size, size), 1), square, 0.0),
        axis=1,
        keepdims=True,
    )


def fold(value, size):
    parts = [value] + [roll(value, at) for at in range(size, value.shape[1], size)]
    while len(parts) > 1:
        parts = [left + right for left, right in zip(parts[0::2], parts[1::2])]
    return parts[0]


def chosen_shares(fluxes, halves, bank, ocean_width):
    rows, width = fluxes[0].shape
    high, low = split(jnp.concatenate(fluxes, axis=0))
    every = jnp.dot(
        jnp.concatenate([high, low, high], axis=1), halves, preferred_element_type=f32
    )
    shares = []
    for part in range(len(fluxes)):
        total = jnp.zeros((rows, width), f32)
        for at in range(0, halves.shape[1], width):
            block = (iota((rows, width), 1) + at) // ocean_width
            mine = every[part * rows : (part + 1) * rows, at : at + width]
            total = total + jnp.where(block == bank, mine, 0.0)
        shares.append(fold(total, ocean_width))
    return shares


def start_kernel(winds, physics, mixing, _, *refs):
    count = 8
    far = refs[:count]
    mask, sea, weights, ocean, exchange_rate, sun, bank_near, message, wanted, forward, stack = refs[
        count : count + 11
    ]
    route, tile, shortwave, bank, sems = refs[count + 11 :]
    here = (route, tile, shortwave, bank, mask, sea, weights, ocean)
    copies = [
        pltpu.make_async_copy(source, target, sems.at[at])
        for at, (source, target) in enumerate(zip(far, here))
    ]
    for copy in copies:
        copy.start()
    rows, width = shortwave.shape
    banks, ocean_width, _ = weights.shape
    depth = ocean.shape[0]
    lane = iota((rows, width), 1)
    group = lax.axis_index("cpl")
    for x in range(rows):
        first = winds[0, x, 0:16].astype(f32)[0:1]
        second = winds[1, x, 0:16].astype(f32)[0:1]
        exchange_rate[x : x + 1] = first * first + second * second
    level = iota((depth, width), 0)
    profile = jnp.exp(level.astype(f32) / -8.0)
    profile = profile / jnp.sum(profile, axis=0, keepdims=True)
    unit = jnp.where(iota((depth, width), 1) == 0, (level == 0).astype(f32), profile)
    message[...] = jnp.full(message.shape, -1.0, f32)
    for copy in copies:
        copy.wait()
    stack[...] = physics_stack(physics[...])
    frac = mask[...].astype(f32)
    exchange_rate[...] = frac * (0.5 + 2.0 * jnp.sqrt(exchange_rate[...] + 0.01))
    target = route[...] * rows + tile[...]
    target_at = as_column(target.astype(f32))
    own_at = (group * rows + iota((rows, 1), 0)).astype(f32)
    wanted[0:rows] = jnp.broadcast_to(target_at, (rows, width))
    wanted[rows : 2 * rows] = jnp.broadcast_to(own_at, (rows, width))
    for at in (0, 2 * ocean_width):
        message[rows : rows + 1, at : at + rows] = target.astype(f32)
        message[rows : rows + 1, at + ocean_width : at + ocean_width + rows] = (
            group * rows + iota((1, rows), 1)
        ).astype(f32)
    bank_at = as_column(bank[...].astype(f32)).astype(jnp.int32)
    high, low = split(weights[...].reshape(banks * ocean_width, width).T)
    forward[...] = jnp.concatenate([high, high, low], axis=0)
    sun[...] = frac * shortwave[...]
    bank_near[...] = jnp.broadcast_to(bank_at, (rows, width))
    top = mixing[0:8]
    settled = 0.5 * ocean[0:8] + jnp.dot(
        top, ocean[...], precision=highest, preferred_element_type=f32
    )
    answer = 0.5 * unit[0:8] + jnp.dot(top, unit, precision=highest, preferred_element_type=f32)
    surface = jnp.zeros((rows, width), f32)
    for at in range(0, rows * ocean_width, width):
        spread = jnp.broadcast_to(settled[0:1, at : at + width], (rows, width))
        surface = surface + jnp.where((lane + at) // ocean_width == iota((rows, width), 0), spread, 0.0)
    surface = fold(surface, ocean_width)
    message[0:rows, :] = surface
    message[rows + 1 : rows + 2, :] = jnp.broadcast_to(answer[0:1, 0:1], (1, width))
    message[rows + 2 : rows + 3, :] = jnp.broadcast_to(answer[0:1, 1:2], (1, width))


def make_outer_kernel(rows):
    def outer_kernel(
        above_ref, below_ref, partial_low, partial_high, air, wind, own, even_side, odd_side,
        near, stack_ref, bottom, rate, sun, sea, bank, forward, start,
        air_edges, bottom_next, message,
    ):
        width = sea.shape[1]
        ocean_width = start.shape[0]
        levels = air.shape[1]
        above = [above_ref[at * levels : (at + 1) * levels].astype(f32) for at in range(3)]
        below = [below_ref[at * levels : (at + 1) * levels].astype(f32) for at in range(3)]
        above.append(unpack_corners(above_ref[3 * levels :].astype(f32), levels, rows - 1))
        below.append(unpack_corners(below_ref[3 * levels :].astype(f32), levels, 0))
        low, high = cpl_sides(even_side, odd_side)
        outer = outer_cells(low, high)
        stack = stack_ref[...]
        place = iota(outer.shape, 1) // 4
        after = advance_outer(
            own[...],
            low,
            high,
            outer,
            pick(place == 0, below[3], roll(outer, 4)),
            pick(place == rows - 1, above[3], roll(outer, -4)),
        )
        moved = jnp.concatenate(
            [
                below[1] + below[2] * air[0],
                partial_low[0] + partial_low[1] * below[0],
                partial_high[0] + partial_high[1] * above[0],
                above[1] + above[2] * air[rows - 1],
                after,
            ],
            axis=1,
        )
        stepped = column(stack, moved)
        parts = [stepped[:, at * width : (at + 1) * width] for at in range(5)]
        inner = [near[at] for at in range(4)]
        bottom_next[...] = bottom[...]
        cells = []
        for center, west, east, x in (
            (parts[1], parts[0], inner[0], 0),
            (inner[0], parts[1], inner[1], 1),
            (inner[3], inner[2], parts[2], rows - 2),
            (parts[2], inner[3], parts[3], rows - 1),
        ):
            south, north = sideways_of(center, parts[4], x)
            first, second = wind[0, x].astype(f32), wind[1, x].astype(f32)
            cells.append(advance_row(center, west, east, south, north, first, second))
        final = column(stack, jnp.concatenate(cells, axis=1))
        for at, x in enumerate((0, 1, rows - 2, rows - 1)):
            row = final[:, at * width : (at + 1) * width]
            air_edges[at] = row
            bottom_next[x : x + 1] = row[0:1]
        heat = rate[...] * (bottom_next[...] - sea[...])
        shares, solar = chosen_shares(
            [heat, sun[...]], forward[...], bank[...], ocean_width
        )
        message[...] = start[...]
        block = iota((rows, width), 1) // ocean_width
        raised = start[rows + 1 : rows + 2, :] * shares + start[rows + 2 : rows + 3, :] * solar
        message[0:rows, :] = jnp.where(
            block == 0,
            shares,
            jnp.where(block == 1, solar, jnp.where(block == 2, raised, start[0:rows, :])),
        )

    return outer_kernel


def settle_kernel(
    edges, inner, bank, weights, ocean, mixing, out, base, response, total_weight, backward, sems
):
    rows = out.shape[0]
    middle = pl.ds(2, rows - 4)
    copies = [
        pltpu.make_async_copy(inner.at[middle], out.at[middle], sems.at[2]),
        pltpu.make_async_copy(edges.at[pl.ds(0, 2)], out.at[pl.ds(0, 2)], sems.at[0]),
        pltpu.make_async_copy(edges.at[pl.ds(2, 2)], out.at[pl.ds(rows - 2, 2)], sems.at[1]),
    ]
    for copy in copies:
        copy.start()
    width = total_weight.shape[1]
    depth = ocean.shape[0]
    banks, ocean_width, _ = weights.shape
    high, low = split(weights[...].reshape(banks * ocean_width, width))
    backward[...] = jnp.concatenate([high, high, low], axis=0)
    sums = jnp.concatenate(
        [jnp.sum(weights[at], axis=0, keepdims=True) for at in range(banks)], axis=0
    )
    hot = (iota((rows, banks), 1) == bank[:, 0:banks]).astype(f32)
    total_weight[...] = jnp.dot(hot, sums, precision=highest, preferred_element_type=f32)
    mixed = mixing[...]
    held = ocean[...]
    base[...] = 0.5 * held + jnp.dot(mixed, held, precision=highest, preferred_element_type=f32)
    level = iota((depth, width), 0)
    profile = jnp.exp(level.astype(f32) / -8.0)
    profile = profile / jnp.sum(profile, axis=0, keepdims=True)
    part = iota((depth, width), 1)
    unit = jnp.where(part == 0, (level == 0).astype(f32), jnp.where(part == 1, profile, 0.0))
    response[...] = 0.5 * unit + jnp.dot(mixed, unit, precision=highest, preferred_element_type=f32)
    for copy in copies:
        copy.wait()


def make_last_kernel(count):
    def last_kernel(*refs):
        messages, (wanted, base, response, total_weight, bottom, mask, bank, backward, ocean_next, surface, ocean_here, surface_here, sems) = (
            refs[:count],
            refs[count:],
        )
        own = messages[0][...]
        if len(messages) == 2 and len(messages[1].shape) == 3:
            blocks = [messages[1][at] for at in range(messages[1].shape[0])]
        else:
            blocks = [ref[...] for ref in messages]
        rows, width = bottom.shape
        slots = own.shape[0]
        ocean_width = slots
        cells = backward.shape[0] // 3
        lane = iota((slots, width), 1)
        labels = []
        values = []
        for block in blocks:
            labels.append(block[rows : rows + 1, :])
            values.append(jnp.where(lane < 3 * ocean_width, block, 0.0))
            values.append(jnp.where(lane < 3 * ocean_width, 0.0, block))
        left = iota((1, width), 1) < 2 * ocean_width
        hot = [
            (wanted[...] == jnp.where(left, labels[at], labels[at + 1])).astype(f32).astype(bf16)
            for at in range(0, len(labels), 2)
        ]
        high, low = split(jnp.concatenate(values, axis=0))
        marks = jnp.concatenate(hot, axis=1)
        got = jnp.dot(marks, high, preferred_element_type=f32) + jnp.dot(
            marks, low, preferred_element_type=f32
        )
        near = iota((rows, width), 1)
        seen = fold(jnp.where(near >= 2 * ocean_width, got[0:rows], 0.0), ocean_width)
        bank_at = bank[...]
        high, low = split(
            jnp.concatenate(
                [
                    jnp.where((near + at) // ocean_width == bank_at, seen, 0.0)
                    for at in range(0, cells, width)
                ],
                axis=1,
            )
        )
        weighted = jnp.dot(
            jnp.concatenate([high, low, high], axis=1), backward[...], preferred_element_type=f32
        )
        forcing = got[rows : 2 * rows]
        heat = fold(jnp.where(near < ocean_width, forcing, 0.0), ocean_width)
        solar = fold(
            jnp.where((near >= ocean_width) & (near < 2 * ocean_width), forcing, 0.0), ocean_width
        )
        first = response[:, 0:1]
        second = response[:, 1:2]
        for at in range(0, base.shape[1], width):
            mine = (near + at) // ocean_width == iota((rows, width), 0)
            heat_row = jnp.sum(jnp.where(mine, heat, 0.0), axis=0, keepdims=True)
            solar_row = jnp.sum(jnp.where(mine, solar, 0.0), axis=0, keepdims=True)
            ocean_here[:, at : at + width] = base[:, at : at + width] + (
                first * heat_row + second * solar_row
            )
        ocean_out = pltpu.make_async_copy(ocean_here, ocean_next, sems.at[0])
        ocean_out.start()
        frac = mask[...].astype(f32)
        surface_here[...] = frac * (weighted / total_weight[...]) + (1.0 - frac) * bottom[...]
        surface_out = pltpu.make_async_copy(surface_here, surface, sems.at[1])
        surface_out.start()
        ocean_out.wait()
        surface_out.wait()

    return last_kernel


def shape_of(shape, dtype=f32):
    return jax.ShapeDtypeStruct(shape, dtype)


def whole(count):
    return [pl.BlockSpec(memory_space=pltpu.VMEM) for _ in range(count)]


def in_hbm(value):
    return pltpu.with_memory_space_constraint(value, pltpu.HBM)


params = pltpu.CompilerParams(vmem_limit_bytes=48 * 1024 * 1024)


def local(
    air_temp,
    wind_field,
    physics,
    sea_surface,
    shortwave,
    ocean_mask,
    owner_route,
    ocean_tile,
    weight_tile,
    remap_tiles,
    ocean_temp,
    mixing,
):
    rows, levels, width = air_temp.shape
    groups = lax.axis_size("cpl")
    ocean_width = remap_tiles.shape[1]
    slots = ocean_width
    ocean_shape = ocean_temp.shape

    packed, to_even, to_odd, air_here, wind_here, physics, mixing = pl.pallas_call(
        pack_kernel,
        out_shape=(
            pltpu.VMEM((levels, width), f32),
            pltpu.VMEM((levels, width), bf16),
            pltpu.VMEM((levels, width), bf16),
            pltpu.VMEM(air_temp.shape, f32),
            pltpu.VMEM(wind_field.shape, bf16),
            pltpu.VMEM(physics.shape, f32),
            pltpu.VMEM(mixing.shape, f32),
        ),
        in_specs=[pl.BlockSpec(memory_space=pltpu.HBM)] * 4,
        out_specs=tuple(whole(7)),
        scratch_shapes=[pltpu.SemaphoreType.DMA((2, 3)), pltpu.SemaphoreType.DMA((2,))],
        compiler_params=params,
        name="pack",
    )(*(in_hbm(value) for value in (air_temp, wind_field, physics, mixing)))
    even_side, odd_side = exchange(to_even, to_odd, "cpl")

    kept = (ocean_mask, sea_surface, remap_tiles, ocean_temp)
    passing = (owner_route.reshape(1, rows), ocean_tile, shortwave, weight_tile)
    (
        ocean_mask,
        sea_surface,
        remap_tiles,
        ocean_temp,
        exchange_rate,
        sun,
        bank_near,
        start,
        wanted,
        forward,
        stack,
    ) = pl.pallas_call(
        start_kernel,
        out_shape=tuple(pltpu.VMEM(value.shape, value.dtype) for value in kept)
        + (
            shape_of((rows, width)),
            shape_of((rows, width)),
            shape_of((rows, width), jnp.int32),
            shape_of((slots, width)),
            shape_of((2 * rows, width)),
            shape_of((3 * width, remap_tiles.shape[0] * ocean_width), bf16),
            shape_of((levels, 3 * levels), bf16),
        ),
        in_specs=whole(3)
        + [pl.BlockSpec(memory_space=pl.ANY)]
        + [pl.BlockSpec(memory_space=pltpu.HBM)] * len(passing + kept),
        out_specs=tuple(whole(len(kept) + 7)),
        scratch_shapes=[pltpu.VMEM(value.shape, value.dtype) for value in passing]
        + [pltpu.SemaphoreType.DMA((len(passing + kept),))],
        compiler_params=params,
        name="start",
    )(wind_here, physics, mixing, packed, *(in_hbm(value) for value in passing + kept))

    def edge(upper, after):
        return pl.pallas_call(
            make_edge_kernel(rows, upper),
            out_shape=(shape_of((3 * levels + 16, width), bf16), shape_of((2, levels, width))),
            in_specs=whole(4) + [pl.BlockSpec(memory_space=pl.ANY)],
            out_specs=tuple(whole(2)),
            compiler_params=params,
            name="edge",
        )(air_here, wind_here, even_side, odd_side, after)

    to_high, partial_high = edge(1, start)
    below = shift(to_high, "atm", 1)
    to_low, partial_low = edge(0, partial_high)
    above = shift(to_low, "atm", -1)

    air_inner, near, bottom = pl.pallas_call(
        inner_kernel,
        out_shape=(
            pltpu.VMEM((rows, levels, width), f32),
            shape_of((4, levels, width)),
            shape_of((rows, width)),
        ),
        in_specs=whole(6),
        out_specs=tuple(whole(3)),
        scratch_shapes=[pltpu.VMEM((rows, levels, width), f32)],
        compiler_params=params,
        name="inner",
    )(air_here, wind_here, stack, packed, even_side, odd_side)

    air_edges, bottom_next, message = pl.pallas_call(
        make_outer_kernel(rows),
        out_shape=(
            shape_of((4, levels, width)),
            shape_of((rows, width)),
            shape_of((slots, width)),
        ),
        in_specs=whole(18),
        out_specs=tuple(whole(3)),
        compiler_params=params,
        name="outer",
    )(
        above,
        below,
        partial_low,
        partial_high,
        air_here,
        wind_here,
        packed,
        even_side,
        odd_side,
        near,
        stack,
        bottom,
        exchange_rate,
        sun,
        sea_surface,
        bank_near,
        forward,
        start,
    )

    if groups <= 4:
        turns = sorted(range(1, groups), key=lambda turn: abs(2 * turn - groups))
        gathered = [message] + [shift(message, "cpl", turn) for turn in turns]
    else:
        gathered = [message, lax.all_gather(message, "cpl")]

    air_next, base, response, total_weight, backward = pl.pallas_call(
        settle_kernel,
        out_shape=(
            shape_of((rows, levels, width)),
            shape_of(ocean_shape),
            shape_of((ocean_shape[0], width)),
            shape_of((rows, width)),
            shape_of((3 * remap_tiles.shape[0] * ocean_width, width), bf16),
        ),
        in_specs=whole(6),
        out_specs=tuple([pl.BlockSpec(memory_space=pltpu.HBM)] + whole(4)),
        scratch_shapes=[pltpu.SemaphoreType.DMA((3,))],
        compiler_params=params,
        name="settle",
    )(air_edges, air_inner, bank_near, remap_tiles, ocean_temp, mixing)

    ocean_next, surface_temp = pl.pallas_call(
        make_last_kernel(len(gathered)),
        out_shape=(shape_of(ocean_shape), shape_of((rows, width))),
        in_specs=whole(len(gathered) + 8),
        out_specs=(pl.BlockSpec(memory_space=pltpu.HBM),) * 2,
        scratch_shapes=[
            pltpu.VMEM(ocean_shape, f32),
            pltpu.VMEM((rows, width), f32),
            pltpu.SemaphoreType.DMA((2,)),
        ],
        compiler_params=params,
        name="last",
    )(
        *gathered,
        wanted,
        base,
        response,
        total_weight,
        bottom_next,
        ocean_mask,
        bank_near,
        backward,
    )
    return (air_next, ocean_next, surface_temp)


def solution(mesh):
    placed = (
        P("atm", None, "cpl"),
        P(None, "atm", None, "cpl"),
        P(),
        P("atm", "cpl"),
        P("atm", "cpl"),
        P("atm", "cpl"),
        P("cpl", "atm", None),
        P("cpl", "atm"),
        P("cpl", "atm"),
        P(),
        P(None, ("atm", "cpl")),
        P(),
    )
    return jax.shard_map(
        local,
        mesh=mesh,
        in_specs=placed,
        out_specs=(P("atm", None, "cpl"), P(None, ("atm", "cpl")), P("atm", "cpl")),
        check_vma=False,
    )
```

```python
import jax
import jax.numpy as jnp
from jax import lax
from jax.experimental import pallas as pl
from jax.experimental.pallas import tpu as pltpu
from jax.sharding import PartitionSpec as P

diffusion_rate = 0.05
physics_rate = 0.5
highest = lax.Precision.HIGHEST
f32 = jnp.float32
bf16 = jnp.bfloat16


def pair_even(count):
    return [(i, i ^ 1) for i in range(count)]


def pair_odd(count):
    up = [(i, (i + 1) % count) for i in range(1, count, 2)]
    return up + [(target, source) for source, target in up]


def exchange(to_even, to_odd, axis):
    count = lax.axis_size(axis)
    even_side = lax.ppermute(to_even, axis, pair_even(count))
    odd_side = lax.ppermute(to_odd, axis, pair_odd(count))
    return even_side, odd_side


def shift(block, axis, turn):
    count = lax.axis_size(axis)
    return lax.ppermute(block, axis, [(i, (i + turn) % count) for i in range(count)])


def iota(shape, dim):
    return lax.broadcasted_iota(jnp.int32, shape, dim)


def roll(value, shift):
    return pltpu.roll(value, shift % value.shape[-1], value.ndim - 1)


def pick(flag, yes, no):
    return jnp.where(flag, yes, no)


def rates(first, second):
    return (
        jnp.maximum(first, 0.0) + diffusion_rate,
        diffusion_rate - jnp.minimum(first, 0.0),
        jnp.maximum(second, 0.0) + diffusion_rate,
        diffusion_rate - jnp.minimum(second, 0.0),
    )


def split(value):
    high = value.astype(bf16)
    return high, (value - high.astype(f32)).astype(bf16)


def physics_stack(physics):
    high, low = split(physics)
    return jnp.concatenate([high, high, low], axis=1)


def column(stack, field):
    high, low = split(field)
    tendency = jnp.dot(
        stack, jnp.concatenate([high, low, high], axis=0), preferred_element_type=f32
    )
    return field + physics_rate * jnp.tanh(tendency)


def pack_kernel(
    air, wind, physics, mixing,
    packed, to_even, to_odd, air_here, wind_here, physics_here, mixing_here, sems, square_sems,
):
    rows, levels, width = air.shape
    lane = iota((levels, width), 1)
    place = lane // 4
    kind = lane % 4
    squares = [
        pltpu.make_async_copy(physics, physics_here, square_sems.at[0]),
        pltpu.make_async_copy(mixing, mixing_here, square_sems.at[1]),
    ]
    for copy in squares:
        copy.start()
    parts = sems.shape[1]
    size = rows // parts
    copies = []
    for part in range(parts):
        span = pl.ds(part * size, size)
        copies.append(
            (
                pltpu.make_async_copy(air.at[span], air_here.at[span], sems.at[0, part]),
                pltpu.make_async_copy(wind.at[:, span], wind_here.at[:, span], sems.at[1, part]),
            )
        )
        for copy in copies[-1]:
            copy.start()
    cells = jnp.zeros((levels, width), bf16)
    first = jnp.zeros((levels, width), bf16)
    second = jnp.zeros((levels, width), bf16)
    for x in range(rows):
        if x % size == 0:
            for copy in copies[x // size]:
                copy.wait()
        here = place == x
        cells = pick(here, roll(air_here[x].astype(bf16), 4 * x + 2), cells)
        first = pick(here, roll(wind_here[0, x], 4 * x + 2), first)
        second = pick(here, roll(wind_here[1, x], 4 * x + 2), second)
    to_high = pick(kind < 2, cells, pick(kind == 2, roll(first, 1), roll(second, 2)))
    to_low = pick(kind >= 2, cells, pick(kind == 0, roll(first, -2), roll(second, -1)))
    upper = lax.axis_index("cpl") % 2 == 0
    packed[...] = cells.astype(f32)
    to_even[...] = pick(upper, to_high, to_low)
    to_odd[...] = pick(upper, to_low, to_high)
    for copy in squares:
        copy.wait()


def cpl_sides(even_side, odd_side):
    upper = lax.axis_index("cpl") % 2 == 0
    high = pick(upper, even_side[...].astype(f32), odd_side[...].astype(f32))
    low = pick(upper, odd_side[...].astype(f32), even_side[...].astype(f32))
    return low, high


def outer_cells(low, high):
    kind = iota(low.shape, 1) % 4
    return pick(kind < 2, low, high)


def swap_cells(cells):
    kind = iota(cells.shape, 1) % 4
    return pick(kind == 2, roll(cells, 1), roll(cells, -1))


def sideways(field, swapped, x):
    width = field.shape[1]
    lane = iota(field.shape, 1)
    halo = roll(swapped, -(4 * x + 2))
    south = pick(lane == 0, halo, roll(field, 1))
    north = pick(lane == width - 1, halo, roll(field, -1))
    return south, north


def sideways_of(field, cells, x):
    width = field.shape[1]
    lane = iota(field.shape, 1)
    south = pick(lane == 0, roll(cells, -(4 * x + 1)), roll(field, 1))
    north = pick(lane == width - 1, roll(cells, -(4 * x + 3)), roll(field, -1))
    return south, north


def advance_row(center, west, east, south, north, first, second):
    around = (west + east) + (south + north)
    upwind_first = jnp.where(first > 0.0, west, east) - center
    upwind_second = jnp.where(second > 0.0, south, north) - center
    return ((1.0 - 4.0 * diffusion_rate) * center + diffusion_rate * around) + (
        jnp.abs(first) * upwind_first + jnp.abs(second) * upwind_second
    )


def advance_outer(own, low, high, outer, west, east):
    kind = iota(outer.shape, 1) % 4
    south = roll(pick(kind == 0, outer, own), 1)
    north = roll(pick(kind == 3, outer, own), -1)
    first = pick(kind == 1, roll(low, -1), roll(high, 2))
    second = pick(kind == 1, roll(low, -2), roll(high, 1))
    return advance_row(outer, west, east, south, north, first, second)


def pack_corners(outer, x):
    levels, width = outer.shape
    place = iota((8, width), 1) // 4
    held = jnp.zeros((8, width), f32)
    for at in range(levels // 8):
        held = pick(place == at, roll(outer[8 * at : 8 * at + 8], 4 * (at - x)), held)
    return jnp.concatenate([held, jnp.zeros_like(held)], axis=0)


def unpack_corners(held, levels, x):
    return jnp.concatenate([roll(held[0:8], 4 * (x - at)) for at in range(levels // 8)], axis=0)


def make_edge_kernel(rows, upper):
    def edge_kernel(air, wind, even_side, odd_side, _, message, partial):
        low, high = cpl_sides(even_side, odd_side)
        outer = outer_cells(low, high)
        at, beside = (rows - 1, rows - 2) if upper else (0, 1)
        center, inner = air[at], air[beside]
        levels = center.shape[0]
        cw, ce, cs, cn = rates(wind[0, at].astype(f32), wind[1, at].astype(f32))
        inside, outside = (cw, ce) if upper else (ce, cw)
        south, north = sideways_of(center, outer, rows - 1 if upper else 0)
        known = (
            center
            + (inside * (inner - center) - outside * center)
            + (cs * (south - center) + cn * (north - center))
        )
        partial[0] = known
        partial[1] = outside
        for part, value in enumerate((center, known, outside)):
            message[part * levels : (part + 1) * levels] = value.astype(bf16)
        message[3 * levels :] = pack_corners(outer, rows - 1 if upper else 0).astype(bf16)

    return edge_kernel


def inner_kernel(
    air, wind, stack_ref, own, even_side, odd_side, ready, near, bottom, field
):
    rows, levels, width = air.shape
    low, high = cpl_sides(even_side, odd_side)
    outer = outer_cells(low, high)
    stack = stack_ref[...]
    swapped = swap_cells(outer)
    after = advance_outer(
        own[...], low, high, outer, roll(outer, 4), roll(outer, -4)
    )
    swapped_after = swap_cells(column(stack, after))

    def step(source, halo, x):
        center = source[x]
        south, north = sideways(center, halo, x)
        first, second = wind[0, x].astype(f32), wind[1, x].astype(f32)
        return advance_row(center, source[x - 1], source[x + 1], south, north, first, second)

    def pair(source, halo, x):
        return column(stack, jnp.concatenate([step(source, halo, x), step(source, halo, x + 1)], axis=1))

    for x in range(1, rows - 1, 2):
        both = pair(air, swapped, x)
        field[x] = both[:, :width]
        field[x + 1] = both[:, width:]
    near[0] = field[1]
    near[1] = field[2]
    near[2] = field[rows - 3]
    near[3] = field[rows - 2]
    bottom[...] = jnp.zeros_like(bottom)
    for x in range(2, rows - 2, 2):
        both = pair(field, swapped_after, x)
        ready[x] = both[:, :width]
        ready[x + 1] = both[:, width:]
        bottom[x : x + 1] = both[0:1, :width]
        bottom[x + 1 : x + 2] = both[0:1, width:]


def as_column(row):
    size = row.shape[1]
    square = jnp.broadcast_to(row, (size, size))
    return jnp.sum(
        jnp.where(iota((size, size), 0) == iota((size, size), 1), square, 0.0),
        axis=1,
        keepdims=True,
    )


def fold(value, size):
    parts = [value] + [roll(value, at) for at in range(size, value.shape[1], size)]
    while len(parts) > 1:
        parts = [left + right for left, right in zip(parts[0::2], parts[1::2])]
    return parts[0]


def chosen_shares(fluxes, halves, bank, ocean_width):
    rows, width = fluxes[0].shape
    high, low = split(jnp.concatenate(fluxes, axis=0))
    every = jnp.dot(
        jnp.concatenate([high, low, high], axis=1), halves, preferred_element_type=f32
    )
    shares = []
    for part in range(len(fluxes)):
        total = jnp.zeros((rows, width), f32)
        for at in range(0, halves.shape[1], width):
            block = (iota((rows, width), 1) + at) // ocean_width
            mine = every[part * rows : (part + 1) * rows, at : at + width]
            total = total + jnp.where(block == bank, mine, 0.0)
        shares.append(fold(total, ocean_width))
    return shares


def start_kernel(winds, physics, mixing, _, *refs):
    count = 8
    far = refs[:count]
    mask, sea, weights, ocean, exchange_rate, sun, bank_near, message, wanted, forward, stack = refs[
        count : count + 11
    ]
    route, tile, shortwave, bank, sems = refs[count + 11 :]
    here = (route, tile, shortwave, bank, mask, sea, weights, ocean)
    copies = [
        pltpu.make_async_copy(source, target, sems.at[at])
        for at, (source, target) in enumerate(zip(far, here))
    ]
    for copy in copies:
        copy.start()
    rows, width = shortwave.shape
    banks, ocean_width, _ = weights.shape
    depth = ocean.shape[0]
    lane = iota((rows, width), 1)
    group = lax.axis_index("cpl")
    for x in range(rows):
        first = winds[0, x, 0:16].astype(f32)[0:1]
        second = winds[1, x, 0:16].astype(f32)[0:1]
        exchange_rate[x : x + 1] = first * first + second * second
    level = iota((depth, width), 0)
    profile = jnp.exp(level.astype(f32) / -8.0)
    profile = profile / jnp.sum(profile, axis=0, keepdims=True)
    unit = jnp.where(iota((depth, width), 1) == 0, (level == 0).astype(f32), profile)
    message[...] = jnp.full(message.shape, -1.0, f32)
    for copy in copies:
        copy.wait()
    stack[...] = physics_stack(physics[...])
    frac = mask[...].astype(f32)
    exchange_rate[...] = frac * (0.5 + 2.0 * jnp.sqrt(exchange_rate[...] + 0.01))
    target = route[...] * rows + tile[...]
    target_at = as_column(target.astype(f32))
    own_at = (group * rows + iota((rows, 1), 0)).astype(f32)
    wanted[0:rows] = jnp.broadcast_to(target_at, (rows, width))
    wanted[rows : 2 * rows] = jnp.broadcast_to(own_at, (rows, width))
    for at in (0, 2 * ocean_width):
        message[rows : rows + 1, at : at + rows] = target.astype(f32)
        message[rows : rows + 1, at + ocean_width : at + ocean_width + rows] = (
            group * rows + iota((1, rows), 1)
        ).astype(f32)
    bank_at = as_column(bank[...].astype(f32)).astype(jnp.int32)
    high, low = split(weights[...].reshape(banks * ocean_width, width).T)
    forward[...] = jnp.concatenate([high, high, low], axis=0)
    sun[...] = frac * shortwave[...]
    bank_near[...] = jnp.broadcast_to(bank_at, (rows, width))
    top = mixing[0:8]
    settled = 0.5 * ocean[0:8] + jnp.dot(
        top, ocean[...], precision=highest, preferred_element_type=f32
    )
    answer = 0.5 * unit[0:8] + jnp.dot(top, unit, precision=highest, preferred_element_type=f32)
    surface = jnp.zeros((rows, width), f32)
    for at in range(0, rows * ocean_width, width):
        spread = jnp.broadcast_to(settled[0:1, at : at + width], (rows, width))
        surface = surface + jnp.where((lane + at) // ocean_width == iota((rows, width), 0), spread, 0.0)
    surface = fold(surface, ocean_width)
    message[0:rows, :] = surface
    message[rows + 1 : rows + 2, :] = jnp.broadcast_to(answer[0:1, 0:1], (1, width))
    message[rows + 2 : rows + 3, :] = jnp.broadcast_to(answer[0:1, 1:2], (1, width))


def make_outer_kernel(rows):
    def outer_kernel(
        above_ref, below_ref, partial_low, partial_high, air, wind, own, even_side, odd_side,
        near, stack_ref, bottom, rate, sun, sea, bank, forward, start,
        air_edges, bottom_next, message,
    ):
        width = sea.shape[1]
        ocean_width = start.shape[0]
        levels = air.shape[1]
        above = [above_ref[at * levels : (at + 1) * levels].astype(f32) for at in range(3)]
        below = [below_ref[at * levels : (at + 1) * levels].astype(f32) for at in range(3)]
        above.append(unpack_corners(above_ref[3 * levels :].astype(f32), levels, rows - 1))
        below.append(unpack_corners(below_ref[3 * levels :].astype(f32), levels, 0))
        low, high = cpl_sides(even_side, odd_side)
        outer = outer_cells(low, high)
        stack = stack_ref[...]
        place = iota(outer.shape, 1) // 4
        after = advance_outer(
            own[...],
            low,
            high,
            outer,
            pick(place == 0, below[3], roll(outer, 4)),
            pick(place == rows - 1, above[3], roll(outer, -4)),
        )
        moved = jnp.concatenate(
            [
                below[1] + below[2] * air[0],
                partial_low[0] + partial_low[1] * below[0],
                partial_high[0] + partial_high[1] * above[0],
                above[1] + above[2] * air[rows - 1],
                after,
            ],
            axis=1,
        )
        stepped = column(stack, moved)
        parts = [stepped[:, at * width : (at + 1) * width] for at in range(5)]
        inner = [near[at] for at in range(4)]
        bottom_next[...] = bottom[...]
        cells = []
        for center, west, east, x in (
            (parts[1], parts[0], inner[0], 0),
            (inner[0], parts[1], inner[1], 1),
            (inner[3], inner[2], parts[2], rows - 2),
            (parts[2], inner[3], parts[3], rows - 1),
        ):
            south, north = sideways_of(center, parts[4], x)
            first, second = wind[0, x].astype(f32), wind[1, x].astype(f32)
            cells.append(advance_row(center, west, east, south, north, first, second))
        final = column(stack, jnp.concatenate(cells, axis=1))
        for at, x in enumerate((0, 1, rows - 2, rows - 1)):
            row = final[:, at * width : (at + 1) * width]
            air_edges[at] = row
            bottom_next[x : x + 1] = row[0:1]
        heat = rate[...] * (bottom_next[...] - sea[...])
        shares, solar = chosen_shares(
            [heat, sun[...]], forward[...], bank[...], ocean_width
        )
        message[...] = start[...]
        block = iota((rows, width), 1) // ocean_width
        raised = start[rows + 1 : rows + 2, :] * shares + start[rows + 2 : rows + 3, :] * solar
        message[0:rows, :] = jnp.where(
            block == 0,
            shares,
            jnp.where(block == 1, solar, jnp.where(block == 2, raised, start[0:rows, :])),
        )

    return outer_kernel


def settle_kernel(
    edges, inner, bank, weights, ocean, mixing, out, base, response, total_weight, backward, sems
):
    rows = out.shape[0]
    middle = pl.ds(2, rows - 4)
    copies = [
        pltpu.make_async_copy(inner.at[middle], out.at[middle], sems.at[2]),
        pltpu.make_async_copy(edges.at[pl.ds(0, 2)], out.at[pl.ds(0, 2)], sems.at[0]),
        pltpu.make_async_copy(edges.at[pl.ds(2, 2)], out.at[pl.ds(rows - 2, 2)], sems.at[1]),
    ]
    for copy in copies:
        copy.start()
    width = total_weight.shape[1]
    depth = ocean.shape[0]
    banks, ocean_width, _ = weights.shape
    high, low = split(weights[...].reshape(banks * ocean_width, width))
    backward[...] = jnp.concatenate([high, high, low], axis=0)
    sums = jnp.concatenate(
        [jnp.sum(weights[at], axis=0, keepdims=True) for at in range(banks)], axis=0
    )
    hot = (iota((rows, banks), 1) == bank[:, 0:banks]).astype(f32)
    total_weight[...] = jnp.dot(hot, sums, precision=highest, preferred_element_type=f32)
    mixed = mixing[...]
    held = ocean[...]
    base[...] = 0.5 * held + jnp.dot(mixed, held, precision=highest, preferred_element_type=f32)
    level = iota((depth, width), 0)
    profile = jnp.exp(level.astype(f32) / -8.0)
    profile = profile / jnp.sum(profile, axis=0, keepdims=True)
    part = iota((depth, width), 1)
    unit = jnp.where(part == 0, (level == 0).astype(f32), jnp.where(part == 1, profile, 0.0))
    response[...] = 0.5 * unit + jnp.dot(mixed, unit, precision=highest, preferred_element_type=f32)
    for copy in copies:
        copy.wait()


def make_last_kernel(count):
    def last_kernel(*refs):
        messages, (wanted, base, response, total_weight, bottom, mask, bank, backward, ocean_next, surface, ocean_here, surface_here, sems) = (
            refs[:count],
            refs[count:],
        )
        own = messages[0][...]
        if len(messages) == 2 and len(messages[1].shape) == 3:
            blocks = [messages[1][at] for at in range(messages[1].shape[0])]
        else:
            blocks = [ref[...] for ref in messages]
        rows, width = bottom.shape
        slots = own.shape[0]
        ocean_width = slots
        cells = backward.shape[0] // 3
        lane = iota((slots, width), 1)
        labels = []
        values = []
        for block in blocks:
            labels.append(block[rows : rows + 1, :])
            values.append(jnp.where(lane < 3 * ocean_width, block, 0.0))
            values.append(jnp.where(lane < 3 * ocean_width, 0.0, block))
        left = iota((1, width), 1) < 2 * ocean_width
        hot = [
            (wanted[...] == jnp.where(left, labels[at], labels[at + 1])).astype(f32).astype(bf16)
            for at in range(0, len(labels), 2)
        ]
        high, low = split(jnp.concatenate(values, axis=0))
        got = jnp.dot(
            jnp.concatenate(hot + hot, axis=1),
            jnp.concatenate([high, low], axis=0),
            preferred_element_type=f32,
        )
        near = iota((rows, width), 1)
        seen = fold(jnp.where(near >= 2 * ocean_width, got[0:rows], 0.0), ocean_width)
        bank_at = bank[...]
        high, low = split(
            jnp.concatenate(
                [
                    jnp.where((near + at) // ocean_width == bank_at, seen, 0.0)
                    for at in range(0, cells, width)
                ],
                axis=1,
            )
        )
        weighted = jnp.dot(
            jnp.concatenate([high, low, high], axis=1), backward[...], preferred_element_type=f32
        )
        forcing = got[rows : 2 * rows]
        heat = fold(jnp.where(near < ocean_width, forcing, 0.0), ocean_width)
        solar = fold(
            jnp.where((near >= ocean_width) & (near < 2 * ocean_width), forcing, 0.0), ocean_width
        )
        first = response[:, 0:1]
        second = response[:, 1:2]
        for at in range(0, base.shape[1], width):
            mine = (near + at) // ocean_width == iota((rows, width), 0)
            heat_row = jnp.sum(jnp.where(mine, heat, 0.0), axis=0, keepdims=True)
            solar_row = jnp.sum(jnp.where(mine, solar, 0.0), axis=0, keepdims=True)
            ocean_here[:, at : at + width] = base[:, at : at + width] + (
                first * heat_row + second * solar_row
            )
        ocean_out = pltpu.make_async_copy(ocean_here, ocean_next, sems.at[0])
        ocean_out.start()
        frac = mask[...].astype(f32)
        surface_here[...] = frac * (weighted / total_weight[...]) + (1.0 - frac) * bottom[...]
        surface_out = pltpu.make_async_copy(surface_here, surface, sems.at[1])
        surface_out.start()
        ocean_out.wait()
        surface_out.wait()

    return last_kernel


def shape_of(shape, dtype=f32):
    return jax.ShapeDtypeStruct(shape, dtype)


def whole(count):
    return [pl.BlockSpec(memory_space=pltpu.VMEM) for _ in range(count)]


def in_hbm(value):
    return pltpu.with_memory_space_constraint(value, pltpu.HBM)


params = pltpu.CompilerParams(vmem_limit_bytes=48 * 1024 * 1024)


def local(
    air_temp,
    wind_field,
    physics,
    sea_surface,
    shortwave,
    ocean_mask,
    owner_route,
    ocean_tile,
    weight_tile,
    remap_tiles,
    ocean_temp,
    mixing,
):
    rows, levels, width = air_temp.shape
    groups = lax.axis_size("cpl")
    ocean_width = remap_tiles.shape[1]
    slots = ocean_width
    ocean_shape = ocean_temp.shape

    packed, to_even, to_odd, air_here, wind_here, physics, mixing = pl.pallas_call(
        pack_kernel,
        out_shape=(
            pltpu.VMEM((levels, width), f32),
            pltpu.VMEM((levels, width), bf16),
            pltpu.VMEM((levels, width), bf16),
            pltpu.VMEM(air_temp.shape, f32),
            pltpu.VMEM(wind_field.shape, bf16),
            pltpu.VMEM(physics.shape, f32),
            pltpu.VMEM(mixing.shape, f32),
        ),
        in_specs=[pl.BlockSpec(memory_space=pltpu.HBM)] * 4,
        out_specs=tuple(whole(7)),
        scratch_shapes=[pltpu.SemaphoreType.DMA((2, 3)), pltpu.SemaphoreType.DMA((2,))],
        compiler_params=params,
        name="pack",
    )(*(in_hbm(value) for value in (air_temp, wind_field, physics, mixing)))
    even_side, odd_side = exchange(to_even, to_odd, "cpl")

    kept = (ocean_mask, sea_surface, remap_tiles, ocean_temp)
    passing = (owner_route.reshape(1, rows), ocean_tile, shortwave, weight_tile)
    (
        ocean_mask,
        sea_surface,
        remap_tiles,
        ocean_temp,
        exchange_rate,
        sun,
        bank_near,
        start,
        wanted,
        forward,
        stack,
    ) = pl.pallas_call(
        start_kernel,
        out_shape=tuple(pltpu.VMEM(value.shape, value.dtype) for value in kept)
        + (
            shape_of((rows, width)),
            shape_of((rows, width)),
            shape_of((rows, width), jnp.int32),
            shape_of((slots, width)),
            shape_of((2 * rows, width)),
            shape_of((3 * width, remap_tiles.shape[0] * ocean_width), bf16),
            shape_of((levels, 3 * levels), bf16),
        ),
        in_specs=whole(3)
        + [pl.BlockSpec(memory_space=pl.ANY)]
        + [pl.BlockSpec(memory_space=pltpu.HBM)] * len(passing + kept),
        out_specs=tuple(whole(len(kept) + 7)),
        scratch_shapes=[pltpu.VMEM(value.shape, value.dtype) for value in passing]
        + [pltpu.SemaphoreType.DMA((len(passing + kept),))],
        compiler_params=params,
        name="start",
    )(wind_here, physics, mixing, packed, *(in_hbm(value) for value in passing + kept))

    def edge(upper, after):
        return pl.pallas_call(
            make_edge_kernel(rows, upper),
            out_shape=(shape_of((3 * levels + 16, width), bf16), shape_of((2, levels, width))),
            in_specs=whole(4) + [pl.BlockSpec(memory_space=pl.ANY)],
            out_specs=tuple(whole(2)),
            compiler_params=params,
            name="edge",
        )(air_here, wind_here, even_side, odd_side, after)

    to_high, partial_high = edge(1, start)
    below = shift(to_high, "atm", 1)
    to_low, partial_low = edge(0, partial_high)
    above = shift(to_low, "atm", -1)

    air_inner, near, bottom = pl.pallas_call(
        inner_kernel,
        out_shape=(
            pltpu.VMEM((rows, levels, width), f32),
            shape_of((4, levels, width)),
            shape_of((rows, width)),
        ),
        in_specs=whole(6),
        out_specs=tuple(whole(3)),
        scratch_shapes=[pltpu.VMEM((rows, levels, width), f32)],
        compiler_params=params,
        name="inner",
    )(air_here, wind_here, stack, packed, even_side, odd_side)

    air_edges, bottom_next, message = pl.pallas_call(
        make_outer_kernel(rows),
        out_shape=(
            shape_of((4, levels, width)),
            shape_of((rows, width)),
            shape_of((slots, width)),
        ),
        in_specs=whole(18),
        out_specs=tuple(whole(3)),
        compiler_params=params,
        name="outer",
    )(
        above,
        below,
        partial_low,
        partial_high,
        air_here,
        wind_here,
        packed,
        even_side,
        odd_side,
        near,
        stack,
        bottom,
        exchange_rate,
        sun,
        sea_surface,
        bank_near,
        forward,
        start,
    )

    if groups <= 4:
        turns = sorted(range(1, groups), key=lambda turn: abs(2 * turn - groups))
        gathered = [message] + [shift(message, "cpl", turn) for turn in turns]
    else:
        gathered = [message, lax.all_gather(message, "cpl")]

    air_next, base, response, total_weight, backward = pl.pallas_call(
        settle_kernel,
        out_shape=(
            shape_of((rows, levels, width)),
            shape_of(ocean_shape),
            shape_of((ocean_shape[0], width)),
            shape_of((rows, width)),
            shape_of((3 * remap_tiles.shape[0] * ocean_width, width), bf16),
        ),
        in_specs=whole(6),
        out_specs=tuple([pl.BlockSpec(memory_space=pltpu.HBM)] + whole(4)),
        scratch_shapes=[pltpu.SemaphoreType.DMA((3,))],
        compiler_params=params,
        name="settle",
    )(air_edges, air_inner, bank_near, remap_tiles, ocean_temp, mixing)

    ocean_next, surface_temp = pl.pallas_call(
        make_last_kernel(len(gathered)),
        out_shape=(shape_of(ocean_shape), shape_of((rows, width))),
        in_specs=whole(len(gathered) + 8),
        out_specs=(pl.BlockSpec(memory_space=pltpu.HBM),) * 2,
        scratch_shapes=[
            pltpu.VMEM(ocean_shape, f32),
            pltpu.VMEM((rows, width), f32),
            pltpu.SemaphoreType.DMA((2,)),
        ],
        compiler_params=params,
        name="last",
    )(
        *gathered,
        wanted,
        base,
        response,
        total_weight,
        bottom_next,
        ocean_mask,
        bank_near,
        backward,
    )
    return (air_next, ocean_next, surface_temp)


def solution(mesh):
    placed = (
        P("atm", None, "cpl"),
        P(None, "atm", None, "cpl"),
        P(),
        P("atm", "cpl"),
        P("atm", "cpl"),
        P("atm", "cpl"),
        P("cpl", "atm", None),
        P("cpl", "atm"),
        P("cpl", "atm"),
        P(),
        P(None, ("atm", "cpl")),
        P(),
    )
    return jax.shard_map(
        local,
        mesh=mesh,
        in_specs=placed,
        out_specs=(P("atm", None, "cpl"), P(None, ("atm", "cpl")), P("atm", "cpl")),
        check_vma=False,
    )
```
